32 devices in a mesh: seq: 8 (over z, y), fsdp: 4 (over x, core).
Axes of the slice: x: 2, y: 2, z: 4, core: 2. Of those that a mesh axis runs over, the one named last changes fastest.
Arguments:
- block_input: bfloat16 [8, 512, 2048], P('fsdp', 'seq'), may hold values from -6 to 6
- seq_lengths: int32 [8, 2], replicated, may hold values from 0 to 512, as said below
- mixer_gain: bfloat16 [2048], P(('seq', 'fsdp')), may hold values from 0.5 to 1.5
- branch_weight: bfloat16 [2560, 2048], P(('seq', 'fsdp')), may hold values from -0.125 to 0.125
- recur_weight: bfloat16 [2560, 2048], P(('seq', 'fsdp')), may hold values from -0.125 to 0.125
- conv_kernel: bfloat16 [2560, 4], P(('seq', 'fsdp')), may hold values from -3 to 3
- conv_bias: bfloat16 [2560], P(('seq', 'fsdp')), may hold values from -3 to 3
- recur_gate_weight: bfloat16 [2560, 160], P(('seq', 'fsdp')), may hold values from -0.5 to 0.5
- recur_gate_bias: bfloat16 [2560], P(('seq', 'fsdp')), may hold values from -3 to 3
- input_gate_weight: bfloat16 [2560, 160], P(('seq', 'fsdp')), may hold values from -0.5 to 0.5
- input_gate_bias: bfloat16 [2560], P(('seq', 'fsdp')), may hold values from -3 to 3
- decay_param: bfloat16 [2560], P(('seq', 'fsdp')), may hold values from 3 to 16
- mixer_weight: bfloat16 [2048, 2560], P(('seq', 'fsdp')), may hold values from -0.25 to 0.25
- mlp_gain: bfloat16 [2048], P(('seq', 'fsdp')), may hold values from 0.5 to 1.5
- gate_weight: bfloat16 [6144, 2048], P(('seq', 'fsdp')), may hold values from -0.125 to 0.125
- up_weight: bfloat16 [6144, 2048], P(('seq', 'fsdp')), may hold values from -0.125 to 0.125
- down_weight: bfloat16 [2048, 6144], P(('seq', 'fsdp')), may hold values from -0.109375 to 0.109375
- cotangent: bfloat16 [8, 512, 2048], P('fsdp', 'seq'), may hold values from -6 to 6
Outputs:
- block_output: bfloat16 [8, 512, 2048], P('fsdp', 'seq')
- input_grad: bfloat16 [8, 512, 2048], P('fsdp', 'seq')
- mixer_gain_grad: float32 [2048], P(('seq', 'fsdp'))
- branch_weight_grad: float32 [2560, 2048], P(('seq', 'fsdp'))
- recur_weight_grad: float32 [2560, 2048], P(('seq', 'fsdp'))
- conv_kernel_grad: float32 [2560, 4], P(('seq', 'fsdp'))
- conv_bias_grad: float32 [2560], P(('seq', 'fsdp'))
- recur_gate_weight_grad: float32 [2560, 160], P(('seq', 'fsdp'))
- recur_gate_bias_grad: float32 [2560], P(('seq', 'fsdp'))
- input_gate_weight_grad: float32 [2560, 160], P(('seq', 'fsdp'))
- input_gate_bias_grad: float32 [2560], P(('seq', 'fsdp'))
- decay_param_grad: float32 [2560], P(('seq', 'fsdp'))
- mixer_weight_grad: float32 [2048, 2560], P(('seq', 'fsdp'))
- mlp_gain_grad: float32 [2048], P(('seq', 'fsdp'))
- gate_weight_grad: float32 [6144, 2048], P(('seq', 'fsdp'))
- up_weight_grad: float32 [6144, 2048], P(('seq', 'fsdp'))
- down_weight_grad: float32 [2048, 6144], P(('seq', 'fsdp'))
The draws below stay inside these ranges and needn't reach their ends.
Inputs may be any that keep to these rules, and one draw needn't show every extreme that they name: `seq_lengths`: each row lists the lengths of the sequences packed one after another into its 512 positions, in order, followed by zeros; the positive ones sum to 512 and are 128 or more. In each aligned block of 2 rows one row holds a single sequence of 512 positions.
All inputs are finite; a program needn't handle non-finite values.
Results may differ from the reference program's by a relative error of at most 0.025.
Values may be sent and summed in bfloat16 or wider, within the bound.
No kernel may reach another device: no remote copies, remote signals or barrier semaphores. Data moves between devices by JAX's collectives and lax.ppermute only.
A program may use at most 256 MiB of HBM per device.

```python
import math
import jax
import jax.numpy as jnp
from jax import lax

D = 2048
R = 2560
FF = 6144
NBLK = 16
CONV = 4
LMIN = 128
ROWS_DEV = 2
BS = 160
ROWS = 8
LEN = 512


decay_scale = 8.0


def draw_seq_lengths(key, part):
    key = jax.random.fold_in(key, 5)
    subkeys = jax.random.split(key, 4)
    slot_count = LEN // (2 * LMIN)
    cut_place = (jnp.arange(1, slot_count, dtype=jnp.int32) * (2 * LMIN))[None, :] + jax.random.randint(subkeys[0], (ROWS, slot_count - 1), 0, LMIN + 1, dtype=jnp.int32)
    cut_level = jax.random.randint(subkeys[1], (ROWS, 1), 1, 4, dtype=jnp.int32)
    cut_kept = jax.random.randint(subkeys[2], (ROWS, slot_count - 1), 0, 4, dtype=jnp.int32) < cut_level
    chosen = jax.random.randint(subkeys[3], (ROWS // ROWS_DEV,), 0, ROWS_DEV, dtype=jnp.int32)
    whole_row = jnp.arange(ROWS, dtype=jnp.int32) % ROWS_DEV == jnp.repeat(chosen, ROWS_DEV)
    cut_kept = cut_kept & jnp.logical_not(whole_row)[:, None]
    cut_sorted = jnp.sort(jnp.where(cut_kept, cut_place, LEN), axis=1)
    bounds = jnp.concatenate([jnp.zeros((ROWS, 1), jnp.int32), cut_sorted, jnp.full((ROWS, 1), LEN, jnp.int32)], axis=1)
    return bounds[:, 1:] - bounds[:, :-1]


def draw_decay_param(key, part):
    key = jax.random.fold_in(key, 9)
    subkeys = jax.random.split(key, 3)
    slow_share = 0.5
    slow_pick = jax.random.uniform(subkeys[0], (R,)) < slow_share
    slow_rate = jnp.exp(jax.random.uniform(subkeys[1], (R,), minval=math.log(0.05), maxval=math.log(0.5))) / (decay_scale * LEN)
    fast_rate = jnp.exp(jax.random.uniform(subkeys[2], (R,), minval=math.log(0.004), maxval=math.log(0.03)))
    base_rate = jnp.where(slow_pick, slow_rate, fast_rate)
    return (-jnp.log(jnp.expm1(base_rate))).astype(jnp.bfloat16)


def strengthened(array, key, source, target, parts, factor):
    owner, partner = [(jnp.arange(array.shape[dim]) // (array.shape[dim] // parts)).reshape([-1 if axis == dim else 1 for axis in range(array.ndim)]) for dim in (source, target)]
    chosen = jax.random.permutation(key, parts)[partner]
    strong = (owner == chosen) | (owner == (partner + parts // 2) % parts)
    return jnp.where(strong, factor * array, array)


def steps_of(own_key, shape, cuts, smallest, high):
    def one(position, blocks):
        heights = jax.random.uniform(jax.random.fold_in(jax.random.fold_in(own_key, 6), position), (blocks,), jnp.float32, smallest / len(cuts), high / len(cuts))
        return jnp.repeat(jnp.exp(heights), shape[position] // blocks).reshape((-1,) + (1,) * (len(shape) - position - 1))

    level = one(*cuts[0])
    for cut in cuts[1:]:
        level = level * one(*cut)
    return level


def noise(rng, extent, deviation, reach, shards=(), kind=jnp.bfloat16):
    gain = steps_of(rng, extent, shards, -0.22, 0.18) if shards else 1.0
    entries = jax.random.normal(rng, extent, jnp.float32) * deviation * gain
    return jnp.minimum(jnp.maximum(entries, -reach), reach).astype(kind)


def bell_draw_with(key, dims, spread, limit, cuts, heavy, kind=jnp.bfloat16):
    values = spread * jax.random.normal(key, dims, jnp.float32)
    if cuts:
        values = values * steps_of(key, dims, cuts, -0.22, 0.18)
    return jnp.clip(strengthened(values, jax.random.fold_in(key, 3), *heavy), -limit, limit).astype(kind)


def setup_inputs(seed: int = 0) -> dict:
    splits = jax.random.split(jax.random.key(seed), 19)
    return {
        "block_input": noise(splits[0], (ROWS, LEN, D), 1.0, 6.0, ((0, 4), (1, 8))),
        "seq_lengths": draw_seq_lengths(jax.random.fold_in(splits[18], 71), 0),
        "mixer_gain": jnp.clip(1.0 + 0.1 * jax.random.normal(splits[2], (D,), jnp.float32), 0.5, 1.5).astype(jnp.bfloat16),
        "branch_weight": noise(splits[3], (R, D), D ** -0.5, 0.125, ((0, 32),)),
        "recur_weight": noise(splits[4], (R, D), D ** -0.5, 0.125, ((0, 32),)),
        "conv_kernel": noise(splits[5], (R, CONV), CONV ** -0.5, 3.0, ((0, 32),)),
        "conv_bias": noise(splits[6], (R,), 0.5, 3.0, ((0, 32),)),
        "recur_gate_weight": noise(splits[7], (R, BS), BS ** -0.5, 0.5, ((0, 32),)),
        "recur_gate_bias": noise(splits[8], (R,), 0.5, 3.0, ((0, 32),)),
        "input_gate_weight": noise(splits[9], (R, BS), BS ** -0.5, 0.5, ((0, 32),)),
        "input_gate_bias": noise(splits[10], (R,), 0.5, 3.0, ((0, 32),)),
        "decay_param": draw_decay_param(jax.random.fold_in(splits[18], 71), 0),
        "mixer_weight": noise(splits[12], (D, R), (R // 4) ** -0.5, 0.25, ((0, 32),)),
        "mlp_gain": jnp.clip(1.0 + 0.1 * jax.random.normal(splits[13], (D,), jnp.float32), 0.5, 1.5).astype(jnp.bfloat16),
        "gate_weight": noise(splits[14], (FF, D), D ** -0.5, 0.125, ((0, 32),)),
        "up_weight": noise(splits[15], (FF, D), D ** -0.5, 0.125, ((0, 32),)),
        "down_weight": noise(splits[16], (D, FF), (FF // 2) ** -0.5, 0.109375, ((0, 32),)),
        "cotangent": bell_draw_with(splits[17], (ROWS, LEN, D), 1.0, 6.0, ((0, 4), (1, 8)), (1, 2, 8, 2.0)),
    }


epsilon = 1e-06
decay_scale = 8.0

@jax.custom_vjp
def low(v):
    return lax.optimization_barrier(v.astype(jnp.bfloat16)).astype(jnp.float32)

@jax.custom_vjp
def low_back(v):
    return v

def low_keep(v):
    return (low(v), None)

def low_pass(kept, grad):
    return (grad,)

def back_keep(v):
    return (v, None)

def back_low(kept, grad):
    return (low(grad),)
low.defvjp(low_keep, low_pass)
low_back.defvjp(back_keep, back_low)

def rms_scale(values, gain_vec):
    return values * lax.rsqrt(lax.optimization_barrier(jnp.mean(values * values, axis=-1, keepdims=True)) + epsilon) * gain_vec

def linear(left_rows, weight):
    return jnp.einsum('ni,oi->no', left_rows, weight, precision=lax.Precision.HIGHEST)

def combine(earlier, later_pair):
    return (earlier[0] * later_pair[0], later_pair[0] * earlier[1] + later_pair[1])

def recur_terms(rate_pre, gate_pre, conv_vals, decay_param, first_mask):
    rate_open = jax.nn.sigmoid(rate_pre)
    log_decay = -decay_scale * rate_open * jax.nn.softplus(-decay_param)
    decay_gate = jnp.exp(log_decay) * (1.0 - first_mask)[..., None]
    inject = jnp.sqrt(-jnp.expm1(2.0 * log_decay)) * jax.nn.sigmoid(gate_pre) * conv_vals
    return (decay_gate, inject)

def segment_info(lengths):
    offsets = jnp.cumsum(lengths, dtype=jnp.int32) - lengths
    is_live = lengths > 0
    places = jnp.arange(LEN, dtype=jnp.int32)
    covered = is_live[:, None] & (offsets[:, None] <= places[None, :])
    segment = lax.optimization_barrier(jnp.sum(covered.astype(jnp.int32), axis=0, dtype=jnp.int32)) - 1
    starting = jnp.any(is_live[:, None] & (offsets[:, None] == places[None, :]), axis=0)
    return (segment, starting.astype(jnp.float32))

def row_forward(params, row_input, segment, first_mask):
    mixer_gain, branch_weight, recur_weight, conv_kernel, conv_bias, rate_weight, rate_bias, input_weight, input_bias, decay_param, mixer_weight, mlp_gain, gate_weight, up_weight, down_weight = params
    normed = low(rms_scale(row_input, mixer_gain))
    branch_act = jax.nn.gelu(low_back(linear(normed, branch_weight)))
    recur_in = low(low_back(linear(normed, recur_weight)))
    padded = jnp.pad(recur_in, ((CONV - 1, 0), (0, 0)))
    padded_seg = jnp.concatenate([jnp.full((CONV - 1,), -1, jnp.int32), segment])
    conv_acc = conv_bias + jnp.zeros_like(recur_in)
    for lag_index in range(CONV):
        start_at = CONV - 1 - lag_index
        same_seg = (padded_seg[start_at:start_at + LEN] == segment).astype(recur_in.dtype)[:, None]
        conv_acc = conv_acc + conv_kernel[:, lag_index] * padded[start_at:start_at + LEN] * same_seg
    conv_out = low(conv_acc)
    blocks = conv_out.reshape(LEN, NBLK, BS)
    rate_pre = jnp.einsum('tbi,bji->tbj', blocks, rate_weight.reshape(NBLK, BS, BS), precision=lax.Precision.HIGHEST).reshape(LEN, R) + rate_bias
    gate_pre = jnp.einsum('tbi,bji->tbj', blocks, input_weight.reshape(NBLK, BS, BS), precision=lax.Precision.HIGHEST).reshape(LEN, R) + input_bias
    decay_gate, inject = recur_terms(rate_pre, gate_pre, conv_out, decay_param, first_mask)
    hidden_state = lax.associative_scan(combine, (decay_gate, inject), axis=0)[1]
    mixed_out = low(hidden_state * branch_act)
    residual = row_input + low_back(linear(mixed_out, mixer_weight))
    normed_two = low(rms_scale(residual, mlp_gain))
    gate_val = low_back(linear(normed_two, gate_weight))
    up_val = low_back(linear(normed_two, up_weight))
    hidden = low(jax.nn.gelu(gate_val) * up_val)
    return residual + linear(hidden, down_weight)

def reference(block_input, seq_lengths, mixer_gain, branch_weight, recur_weight, conv_kernel, conv_bias, recur_gate_weight, recur_gate_bias, input_gate_weight, input_gate_bias, decay_param, mixer_weight, mlp_gain, gate_weight, up_weight, down_weight, cotangent):
    params = tuple((arr.astype(jnp.float32) for arr in (mixer_gain, branch_weight, recur_weight, conv_kernel, conv_bias, recur_gate_weight, recur_gate_bias, input_gate_weight, input_gate_bias, decay_param, mixer_weight, mlp_gain, gate_weight, up_weight, down_weight)))
    segment, first_mask = jax.vmap(segment_info)(seq_lengths)
    row_step = jax.checkpoint(row_forward)

    def whole(inputs, weights):

        def one_row(carried, row_item):
            return (carried, row_step(weights, row_item[0], row_item[1], row_item[2]))
        return lax.scan(one_row, None, (inputs, segment, first_mask))[1]
    output, pullback = jax.vjp(whole, block_input.astype(jnp.float32), params)
    input_grad, weight_grads = pullback(cotangent.astype(jnp.float32))
    grad_gain_one, grad_branch, grad_recur, grad_kernel, grad_conv_bias, grad_rate_weight, grad_rate_bias, grad_input_weight, grad_input_bias, grad_decay, grad_mixer, grad_gain_two, grad_gate, grad_up, grad_down = weight_grads
    return (output.astype(jnp.bfloat16), input_grad.astype(jnp.bfloat16), grad_gain_one, grad_branch, grad_recur, grad_kernel, grad_conv_bias, grad_rate_weight, grad_rate_bias, grad_input_weight, grad_input_bias, grad_decay, grad_mixer, grad_gain_two, grad_gate, grad_up, grad_down)
```

```python
import functools

import jax
import jax.numpy as jnp
from jax import lax
from jax.experimental import pallas as pl
from jax.experimental.pallas import tpu as pltpu
from jax.sharding import PartitionSpec as P

AXES = ("seq", "fsdp")
TAPS = 4
EPSILON = 1e-06
DECAY_SCALE = 8.0
VMEM_BYTES = 56 * 1024 * 1024
BF16 = jnp.bfloat16
F32 = jnp.float32


def device_bits(seq_count, fsdp_count, rows, block):
    low = fsdp_count
    while low * rows < block:
        low *= 2
    total = seq_count * fsdp_count
    every = [1 << k for k in range(total.bit_length() - 1)]
    dp = tuple(b for b in every if b not in (low, 2 * low))
    return low, dp


def linear_index():
    return lax.axis_index("seq") * lax.axis_size("fsdp") + lax.axis_index("fsdp")


def bit_of(index, bit):
    return lax.rem(lax.div(index, jnp.int32(bit)), jnp.int32(2))


def number_of(index, bits):
    value = jnp.int32(0)
    for b in bits:
        value = value * 2 + bit_of(index, b)
    return value


def trade(value, mask):
    count = lax.axis_size("seq") * lax.axis_size("fsdp")
    return lax.ppermute(value, AXES, [(i, i ^ mask) for i in range(count)])


def pick(value, index, axis):
    return lax.dynamic_index_in_dim(value, index, axis, keepdims=False)


def put(buffer, part, index, axis):
    return lax.dynamic_update_index_in_dim(buffer, part, index, axis)


def gather_units(own, dp):
    units = [(0, own)]
    for b in reversed(dp):
        units += [(mask | b, trade(unit, b)) for mask, unit in units]
    return units


def gather_rows(own, dp, me):
    units = gather_units(own, dp)
    whole = jnp.zeros((len(units),) + own.shape, own.dtype)
    for mask, unit in units:
        whole = put(whole, unit, number_of(jnp.bitwise_xor(me, mask), dp), 0)
    return whole


def scatter_bit(value, axis, bit, me):
    mine = bit_of(me, bit)
    sent = trade(pick(value, 1 - mine, axis).astype(BF16), bit)
    return pick(value, mine, axis).astype(F32) + sent.astype(F32)


def scatter_rows(value, dp, me):
    value = value.reshape((2,) * len(dp) + value.shape[1:])
    for b in dp:
        value = scatter_bit(value, 0, b, me)
        if b != dp[-1]:
            value = value.astype(BF16)
    return value


def share_tokens(own, low):
    half = own.shape[0] // 2
    one, two = trade(own, low), trade(own, 2 * low)
    three = [trade(two[:half], low), trade(one[half:], 2 * low)]
    return jnp.concatenate([own, one, two] + three, axis=0)


def sum_tokens(partial, low):
    rows = partial.shape[0] // 4
    total = partial[:rows].astype(F32)
    for j in (1, 2, 3):
        total = total + trade(partial[j * rows : (j + 1) * rows], j * low).astype(F32)
    return total


def project(left, weight):
    return lax.dot_general(left, weight, (((1,), (1,)), ((), ())), preferred_element_type=F32)


def back_project(left, weight):
    return lax.dot_general(left, weight, (((1,), (0,)), ((), ())), preferred_element_type=F32)


def outer(grads, values):
    return lax.dot_general(grads, values, (((0,), (0,)), ((), ())), preferred_element_type=F32)


def inverse_rms(values):
    return lax.rsqrt(jnp.mean(values * values, axis=-1, keepdims=True) + EPSILON)


def gelu_parts(v):
    c = 0.7978845608028654
    t = jnp.tanh(c * (v + 0.044715 * v * v * v))
    act = 0.5 * v * (1.0 + t)
    slope = 0.5 * (1.0 + t) + 0.5 * v * (1.0 - t * t) * c * (1.0 + 3 * 0.044715 * v * v)
    return act, slope


def call(body, outs, scalars, arrays, scratch=()):
    return pl.pallas_call(
        body,
        out_shape=[jax.ShapeDtypeStruct(shape, kind) for shape, kind in outs],
        in_specs=[pl.BlockSpec(memory_space=pltpu.SMEM)]
        + [pl.BlockSpec(memory_space=pltpu.VMEM)] * len(arrays),
        out_specs=[pl.BlockSpec(memory_space=pltpu.VMEM)] * len(outs),
        scratch_shapes=list(scratch),
        compiler_params=pltpu.CompilerParams(vmem_limit_bytes=VMEM_BYTES),
    )(scalars, *arrays)


def block_number(scalars, n, rows, step):
    return jnp.bitwise_xor(scalars[0], (n // rows) * step)


def injection(s, speed):
    y = speed * s
    e = jnp.exp(-y)
    z = 2.0 * y
    series = 1.0 - z * (1 / 7)
    for k in (6, 5, 4, 3, 2):
        series = 1.0 - z * (1 / k) * series
    return e, jnp.sqrt(jnp.where(z < 0.35, z * series, 1.0 - e * e))


def span_scan(a, b, reverse):
    span, channels = a.shape
    within = lax.broadcasted_iota(jnp.int32, (span, channels), 0) % 8
    for k in (1, 2, 4):
        turn = span - k if reverse else k
        reached = within < 8 - k if reverse else within >= k
        a_far = jnp.where(reached, pltpu.roll(a, turn, 0), 1.0)
        b_far = jnp.where(reached, pltpu.roll(b, turn, 0), 0.0)
        b = b + a * b_far
        a = a * a_far
    count = span // 8
    order = range(count - 1, -1, -1) if reverse else range(count)
    edge = 0 if reverse else 7
    a_all, b_all = [None] * count, [None] * count
    p = jnp.ones((1, channels), F32)
    h = jnp.zeros((1, channels), F32)
    for i in order:
        a_i, b_i = a[8 * i : 8 * i + 8], b[8 * i : 8 * i + 8]
        b_all[i] = b_i + a_i * h
        a_all[i] = a_i * p
        p = a_all[i][edge : edge + 1]
        h = b_all[i][edge : edge + 1]
    return jnp.concatenate(a_all, axis=0), jnp.concatenate(b_all, axis=0), p, h


def forward_kernel(
    rows, step, scalars, recur, halo, marks, coef, rate_w, gate_w,
    conv, s_out, q_out, prod, part, ends, pad,
):
    count, span, channels = recur.shape

    def convolve(n, carry):
        block = block_number(scalars, n, rows, step)
        before = jnp.bitwise_xor(jnp.maximum(block - 1, 0), scalars[0])
        pad[4:8, :] = halo[before * rows + n % rows]
        pad[8:, :] = recur[n].astype(F32)
        total = coef[4:5, :] + coef[0:1, :] * pad[8:, :]
        for k in range(1, TAPS):
            total = total + coef[k : k + 1, :] * pad[8 - k : 8 - k + span, :] * marks[n][:, k : k + 1]
        conv[n] = total.astype(BF16)
        return carry

    lax.fori_loop(0, count, convolve, 0)
    flat = conv[...].reshape(count * span, channels)
    s_out[...] = project(flat, rate_w[...]).reshape(count, span, channels)
    q_out[...] = project(flat, gate_w[...]).reshape(count, span, channels)

    def scan(n, carry):
        s = jax.nn.sigmoid(s_out[n] + coef[5:6, :])
        q = jax.nn.sigmoid(q_out[n] + coef[6:7, :])
        s_out[n] = s
        q_out[n] = q
        e, m = injection(s, coef[7:8, :])
        decay = e * (1.0 - marks[n][:, 0:1])
        p_all, h_all, p, h = span_scan(decay, m * q * conv[n].astype(F32), False)
        prod[n] = p_all
        part[n] = h_all
        ends[n, 0:1, :] = p
        ends[n, 1:2, :] = h
        return carry

    lax.fori_loop(0, count, scan, 0)


def join(ends, into, scalars, rows, blocks, reverse):
    def lap(k, carry):
        block = blocks - 1 - k if reverse else k
        place = jnp.bitwise_xor(block, scalars[0]) * rows
        new = []
        for r in range(rows):
            into[block * rows + r] = carry[r]
            pair = ends[place + r]
            new.append(pair[0:1] * carry[r] + pair[1:2])
        return tuple(new)

    channels = into.shape[-1]
    lax.fori_loop(0, blocks, lap, (jnp.zeros((1, channels), F32),) * rows)


def state_kernel(rows, step, scalars, prod, part, ends, branch, state, mixed, came, into):
    count = prod.shape[0]
    join(ends, into, scalars, rows, into.shape[0] // rows, False)

    def finish(n, carry):
        incoming = into[block_number(scalars, n, rows, step) * rows + n % rows]
        h = part[n] + prod[n] * incoming
        came[n] = incoming
        state[n] = h
        mixed[n] = (h * gelu_parts(branch[n])[0]).astype(BF16)
        return carry

    lax.fori_loop(0, count, finish, 0)


def adjoint_kernel(
    scalars, grad_mixed, state, branch, s_in, marks, coef, grad_branch, prod, part, ends, pad
):
    count, span, channels = state.shape
    pad[span:, :] = jnp.ones((8, channels), F32)

    def scan(n, carry):
        act, slope = gelu_parts(branch[n])
        grad = grad_mixed[n]
        grad_branch[n] = (grad * state[n] * slope).astype(BF16)
        decay = jnp.exp(-coef[7:8, :] * s_in[n]) * (1.0 - marks[n][:, 0:1])
        pad[:span, :] = decay
        p_all, h_all, p, h = span_scan(pad[1 : span + 1, :], grad * act, True)
        prod[n] = p_all
        part[n] = h_all
        ends[n, 0:1, :] = decay[0:1] * p
        ends[n, 1:2, :] = decay[0:1] * h
        return carry

    lax.fori_loop(0, count, scan, 0)


def gates_kernel(
    rows, step, scalars, prod, part, ends, s_in, q_in, conv, state, came, recur, halo, marks, coef,
    rate_w, gate_w, grad_conv, rate_grad, gate_grad, sums, grad_rate, grad_gate, into, pad, pad_two,
):
    count, span, channels = prod.shape
    join(ends, into, scalars, rows, into.shape[0] // rows, True)
    sums[...] = jnp.zeros((8, channels), F32)

    def terms(n, carry):
        block = block_number(scalars, n, rows, step)
        total = part[n] + prod[n] * into[block * rows + n % rows]
        pad[7:8, :] = came[n]
        pad[8:, :] = state[n]
        s, q = s_in[n], q_in[n]
        e, m = injection(s, coef[7:8, :])
        c = conv[n].astype(F32)
        first = marks[n][:, 0:1]
        grad_log = total * (pad[7 : 7 + span, :] * e * (1.0 - first) - e * e * q * c / m)
        rate = -coef[7:8, :] * s * (1.0 - s) * grad_log
        gate = total * m * c * q * (1.0 - q)
        grad_conv[n] = total * m * q
        grad_rate[pl.ds(pl.multiple_of(n * span, span), span), :] = rate.astype(BF16)
        grad_gate[pl.ds(pl.multiple_of(n * span, span), span), :] = gate.astype(BF16)
        sums[0:1, :] += jnp.sum(rate, axis=0, keepdims=True)
        sums[1:2, :] += jnp.sum(gate, axis=0, keepdims=True)
        sums[2:3, :] += jnp.sum(s * grad_log, axis=0, keepdims=True)
        return carry

    lax.fori_loop(0, count, terms, 0)
    through = back_project(grad_rate[...], rate_w[...]) + back_project(grad_gate[...], gate_w[...])
    grad_conv[...] += through.reshape(count, span, channels)
    flat = conv[...].reshape(count * span, channels)
    rate_grad[...] = outer(grad_rate[...], flat)
    gate_grad[...] = outer(grad_gate[...], flat)

    def kernel_terms(n, carry):
        block = block_number(scalars, n, rows, step)
        before = jnp.bitwise_xor(jnp.maximum(block - 1, 0), scalars[0])
        pad_two[4:8, :] = halo[before * rows + n % rows]
        pad_two[8:, :] = recur[n].astype(F32)
        grad = grad_conv[n]
        sums[3:4, :] += jnp.sum(grad, axis=0, keepdims=True)
        sums[4:5, :] += jnp.sum(grad * pad_two[8:, :], axis=0, keepdims=True)
        for k in range(1, TAPS):
            term = grad * pad_two[8 - k : 8 - k + span, :] * marks[n][:, k : k + 1]
            sums[4 + k : 5 + k, :] += jnp.sum(term, axis=0, keepdims=True)
        return carry

    lax.fori_loop(0, count, kernel_terms, 0)


def unconvolve_kernel(rows, step, blocks, scalars, grad_conv, halo, marks, coef, grad_recur, pad):
    count, span, channels = grad_conv.shape

    def body(n, carry):
        block = block_number(scalars, n, rows, step)
        behind = jnp.bitwise_xor(jnp.minimum(block + 1, blocks - 1), scalars[0])
        pad[:span, :] = grad_conv[n]
        pad[span : span + 4, :] = halo[behind * rows + n % rows]
        total = coef[0:1, :] * pad[:span, :]
        for k in range(1, TAPS):
            seen = marks[n][:, 3 + k : 4 + k]
            total = total + coef[k : k + 1, :] * pad[k : k + span, :] * seen
        grad_recur[n] = total.astype(BF16)
        return carry

    lax.fori_loop(0, count, body, 0)


def sequence_marks(lengths, block_ids, span, total_len):
    reach = TAPS - 1
    offsets = jnp.cumsum(lengths, axis=1, dtype=jnp.int32) - lengths
    live = (lengths > 0)[None, :, :, None]
    places = block_ids[:, None] * span + jnp.arange(-reach, span + reach, dtype=jnp.int32)
    starts = offsets[None, :, :, None]
    at = places[:, None, None, :]
    segment = jnp.sum((live & (starts <= at)).astype(jnp.int32), axis=2) - 1
    segment = jnp.where(places[:, None, :] < total_len, segment, -2)
    first = jnp.any(live & (starts == at), axis=2)[:, :, reach : reach + span]
    here = segment[:, :, reach : reach + span]
    columns = [first]
    for k in range(1, TAPS):
        columns.append(segment[:, :, reach - k : reach - k + span] == here)
    for k in range(1, TAPS):
        columns.append(segment[:, :, reach + k : reach + k + span] == here)
    columns.append(jnp.zeros_like(first))
    return jnp.stack(columns, axis=-1).astype(F32)


def shards(
    block_input,
    seq_lengths,
    mixer_gain,
    branch_weight,
    recur_weight,
    conv_kernel,
    conv_bias,
    recur_gate_weight,
    recur_gate_bias,
    input_gate_weight,
    input_gate_bias,
    decay_param,
    mixer_weight,
    mlp_gain,
    gate_weight,
    up_weight,
    down_weight,
    cotangent,
):
    rows, span, width = block_input.shape
    tokens = rows * span
    seq_count, fsdp_count = lax.axis_size("seq"), lax.axis_size("fsdp")
    device_count = seq_count * fsdp_count
    channel_rows = branch_weight.shape[0]
    block_size = recur_gate_weight.shape[1]
    low, dp = device_bits(seq_count, fsdp_count, channel_rows, block_size)
    step = low // fsdp_count
    me = linear_index()
    seq_index = lax.axis_index("seq")
    tp_index = number_of(me, (2 * low, low))
    share = 1 << len(dp)
    channels = share * channel_rows
    blocks = 4 * rows
    scalars = seq_index.astype(jnp.int32).reshape(1)
    place_bits = len(dp) + 2
    high_bits = tuple(b for b in reversed(dp) if b > low)
    low_bits = tuple(b for b in reversed(dp) if b < low)
    high, deep = 1 << len(high_bits), 1 << len(low_bits)
    seq_dp = tuple(b for b in dp if b >= fsdp_count)

    def across_blocks(own):
        found = {}
        for mask, unit in gather_units(own, seq_dp):
            for j in range(4):
                found[mask // fsdp_count | j * step] = unit[j]
        return jnp.stack([found[x] for x in range(seq_count)])

    def by_owner(weight, unit):
        names = list(range(place_bits - 1, -1, -1))
        where = {1 << k: 1 + i for i, k in enumerate(names)}
        split = weight.reshape((weight.shape[0],) + (2,) * place_bits + (unit,))
        axes = (where[2 * low], where[low], 0) + tuple(where[b] for b in dp) + (place_bits + 1,)
        return jnp.transpose(split, axes).reshape(4, weight.shape[0], share * unit)

    def from_owner(parts, unit):
        count = parts.shape[1]
        split = parts.reshape((2, 2, count) + (2,) * len(dp) + (unit,))
        where = {2 * low: 0, low: 1}
        where.update({b: 3 + i for i, b in enumerate(dp)})
        names = [1 << k for k in range(place_bits - 1, -1, -1)]
        axes = (2,) + tuple(where[b] for b in names) + (3 + len(dp),)
        return jnp.transpose(split, axes).reshape(count, device_count * unit)

    def swap_owners(parts):
        got = jnp.zeros_like(parts)
        for j in range(4):
            peer = jnp.bitwise_xor(tp_index, j)
            part = pick(parts, peer, 0)
            got = put(got, trade(part, j * low) if j else part, peer, 0)
        return got

    def gather_columns(weight, unit):
        piece = swap_owners(by_owner(weight, unit))
        whole = jnp.zeros((high, 4, deep) + piece.shape[1:], weight.dtype)
        for mask, got in gather_units(piece, dp):
            owner = jnp.bitwise_xor(me, mask)
            whole = lax.dynamic_update_slice(
                whole,
                got[None, :, None],
                (number_of(owner, high_bits), 0, number_of(owner, low_bits), 0, 0),
            )
        return whole.reshape(-1, piece.shape[-1])

    def scatter_columns(grads, unit):
        rows_each = grads.shape[0] // device_count
        value = grads.reshape(
            (2,) * len(high_bits) + (4,) + (2,) * len(low_bits) + (rows_each, grads.shape[1])
        )
        for b in dp:
            axis = len(high_bits) - 1 if b > low else len(high_bits) + 1 + len(low_bits) - 1
            left = [c for c in dp if c >= b]
            axis = sum(c > low for c in left) - 1 if b > low else (
                sum(c > low for c in left) + sum(c < low for c in left)
            )
            value = scatter_bit(value, axis, b, me).astype(BF16)
        return from_owner(swap_owners(value).astype(F32), unit)

    gains = jnp.stack([mixer_gain, mlp_gain])[None]
    for b in dp:
        got = trade(gains, b)
        mine = bit_of(me, b) == 0
        gains = jnp.concatenate([jnp.where(mine, gains, got), jnp.where(mine, got, gains)])
    gains = jnp.stack([gains] + [trade(gains, j * low) for j in (1, 2, 3)])
    gains = jnp.take(gains, jnp.bitwise_xor(tp_index, jnp.arange(4)), axis=0)
    gains = gains.reshape(4, high, deep, 2, -1).transpose(3, 1, 0, 2, 4).reshape(2, width)
    gain_one, gain_two = gains[0].astype(F32), gains[1].astype(F32)

    small = jnp.concatenate(
        [
            conv_kernel,
            conv_bias[:, None],
            recur_gate_bias[:, None],
            input_gate_bias[:, None],
            decay_param[:, None],
            recur_gate_weight,
            input_gate_weight,
        ],
        axis=1,
    )
    small = gather_rows(small, dp, me).reshape(channels, -1)
    coef = small[:, :8].astype(F32).T
    decay_vec = coef[7]
    speed = DECAY_SCALE * jax.nn.softplus(-decay_vec)
    coef = jnp.concatenate([coef[:7], speed[None]])
    in_block = block_size // channel_rows
    place = jnp.arange(share, dtype=jnp.int32)
    spots = [(place >> (len(dp) - 1 - i)) & 1 for i in range(len(dp))]
    inner_bits = [b for b in dp if b < in_block]
    offset = sum((spots[dp.index(b)] * b for b in inner_bits), jnp.zeros_like(place))
    group = sum(
        (spots[dp.index(b)] * b for b in dp if b >= in_block), jnp.zeros_like(place)
    )
    same_block = group[:, None] == group[None, :]

    def widen(gate_rows):
        parts = gate_rows.reshape(share, channel_rows, in_block, channel_rows)
        spread = jnp.take(parts, offset, axis=2)
        spread = jnp.where(same_block[:, None, :, None], spread, jnp.zeros_like(spread))
        return spread.reshape(channels, channels)

    def narrow(wide):
        parts = wide.reshape(share, channel_rows, share, channel_rows)
        out = []
        for i in range(in_block):
            chosen = same_block & (offset == i)[None, :]
            out.append(jnp.sum(jnp.where(chosen[:, None, :, None], parts, 0.0), axis=2))
        return jnp.stack(out, axis=2).reshape(channels, block_size)

    rate_wide = widen(small[:, 8 : 8 + block_size])
    gate_wide = widen(small[:, 8 + block_size :])

    lengths = lax.dynamic_slice_in_dim(seq_lengths, lax.axis_index("fsdp") * rows, rows, 0)
    block_ids = jnp.bitwise_xor(seq_index, jnp.arange(4, dtype=jnp.int32) * step)
    marks = sequence_marks(lengths, block_ids, span, seq_count * span).reshape(blocks, span, 8)

    branch_q = gather_rows(branch_weight, dp, me).reshape(channels, width)
    recur_q = gather_rows(recur_weight, dp, me).reshape(channels, width)
    mixer_q = gather_columns(mixer_weight, channel_rows)
    hidden_rows = gate_weight.shape[0]
    gate_q = gather_rows(gate_weight, dp, me).reshape(-1, width)
    up_q = gather_rows(up_weight, dp, me).reshape(-1, width)
    down_q = gather_columns(down_weight, hidden_rows)

    input_own = block_input.reshape(tokens, width)
    cot_own = cotangent.reshape(tokens, width)
    input_all = share_tokens(input_own, low).astype(F32)
    scale_one = inverse_rms(input_all)
    normed = (input_all * scale_one * gain_one).astype(BF16)
    recur_in = project(normed, recur_q).astype(BF16).reshape(blocks, span, channels)
    edge = recur_in[:, span - 4 :].reshape(4, rows, 4, channels)
    halo = across_blocks(edge).astype(F32).reshape(seq_count * rows, 4, channels)
    branch = project(normed, branch_q).reshape(blocks, span, channels)
    shape = (blocks, span, channels)
    one = (blocks, 1, channels)
    everything = (seq_count * rows, 1, channels)
    conv, s_val, q_val, prod, part, ends = call(
        functools.partial(forward_kernel, rows, step),
        [(shape, BF16)] + [(shape, F32)] * 4 + [((blocks, 2, channels), F32)],
        scalars,
        [recur_in, halo, marks, coef, rate_wide, gate_wide],
        [pltpu.VMEM((span + 8, channels), F32)],
    )
    ends = across_blocks(ends.reshape(4, rows, 2, channels)).reshape(-1, 2, channels)
    state, mixed, came = call(
        functools.partial(state_kernel, rows, step),
        [(shape, F32), (shape, BF16), (one, F32)],
        scalars,
        [prod, part, ends, branch],
        [pltpu.VMEM(everything, F32)],
    )
    mixed_flat = mixed.reshape(4 * tokens, channels)
    residual = input_own.astype(F32) + sum_tokens(project(mixed_flat, mixer_q).astype(BF16), low)

    scale_two = inverse_rms(residual)
    unit_two = residual * scale_two
    normed_two = share_tokens((unit_two * gain_two).astype(BF16), low)
    cot_all = share_tokens(cot_own, low)
    gate_val = project(normed_two, gate_q)
    up_val = project(normed_two, up_q)
    act, slope = gelu_parts(gate_val)
    hidden = (act * up_val).astype(BF16)
    down_part = project(hidden, down_q).astype(BF16)
    grad_hidden = back_project(cot_all, down_q)
    grad_gate = (grad_hidden * up_val * slope).astype(BF16)
    grad_up = (grad_hidden * act).astype(BF16)
    grad_two_part = (back_project(grad_gate, gate_q) + back_project(grad_up, up_q)).astype(BF16)
    grad_two = sum_tokens(grad_two_part, low)
    block_output = (residual + sum_tokens(down_part, low)).astype(BF16)
    scaled = grad_two * gain_two
    grad_residual = cot_own.astype(F32) + scale_two * (
        scaled - unit_two * jnp.mean(scaled * unit_two, axis=-1, keepdims=True)
    )
    gain_two_part = jnp.sum(grad_two * unit_two, axis=0)

    grad_mix = share_tokens(grad_residual.astype(BF16), low)
    grad_mixed = back_project(grad_mix, mixer_q).reshape(shape)
    grad_branch, prod_back, part_back, ends_back = call(
        adjoint_kernel,
        [(shape, BF16), (shape, F32), (shape, F32), ((blocks, 2, channels), F32)],
        scalars,
        [grad_mixed, state, branch, s_val, marks, coef],
        [pltpu.VMEM((span + 8, channels), F32)],
    )
    ends_back = across_blocks(ends_back.reshape(4, rows, 2, channels)).reshape(-1, 2, channels)
    square = (channels, channels)
    grad_conv, rate_square, gate_square, sums = call(
        functools.partial(gates_kernel, rows, step),
        [(shape, F32), (square, F32), (square, F32), ((8, channels), F32)],
        scalars,
        [
            prod_back, part_back, ends_back, s_val, q_val, conv, state, came, recur_in, halo,
            marks, coef, rate_wide, gate_wide,
        ],
        [
            pltpu.VMEM((4 * tokens, channels), BF16),
            pltpu.VMEM((4 * tokens, channels), BF16),
            pltpu.VMEM(everything, F32),
            pltpu.VMEM((span + 8, channels), F32),
            pltpu.VMEM((span + 8, channels), F32),
        ],
    )
    edge_back = grad_conv[:, :4].astype(BF16).reshape(4, rows, 4, channels)
    halo_back = across_blocks(edge_back).astype(F32).reshape(seq_count * rows, 4, channels)
    (grad_recur,) = call(
        functools.partial(unconvolve_kernel, rows, step, seq_count),
        [(shape, BF16)],
        scalars,
        [grad_conv, halo_back, marks, coef],
        [pltpu.VMEM((span + 8, channels), F32)],
    )
    grad_branch = grad_branch.reshape(4 * tokens, channels)
    grad_recur = grad_recur.reshape(4 * tokens, channels)
    grad_normed_part = back_project(grad_branch, branch_q) + back_project(grad_recur, recur_q)
    gain_one_part = jnp.sum(grad_normed_part * input_all * scale_one, axis=0)
    grad_normed = sum_tokens(grad_normed_part.astype(BF16), low)
    own_scale = scale_one[:tokens]
    unit_one = input_own.astype(F32) * own_scale
    scaled_one = grad_normed * gain_one
    input_grad = (
        grad_residual
        + own_scale
        * (scaled_one - unit_one * jnp.mean(scaled_one * unit_one, axis=-1, keepdims=True))
    ).astype(BF16)

    def row_grad(grads, values):
        whole = outer(grads, values).astype(BF16)
        return scatter_rows(whole.reshape(share, -1, width), dp, me)

    gate_weight_grad = row_grad(grad_gate, normed_two)
    up_weight_grad = row_grad(grad_up, normed_two)
    down_weight_grad = scatter_columns(outer(cot_all, hidden).astype(BF16), hidden_rows)
    mixer_weight_grad = scatter_columns(outer(grad_mix, mixed_flat).astype(BF16), channel_rows)
    branch_weight_grad = row_grad(grad_branch, normed)
    recur_weight_grad = row_grad(grad_recur, normed)

    gain_parts = jnp.stack([gain_one_part, gain_two_part]).reshape(2, high, 4, deep, -1)
    gain_parts = gain_parts.transpose(2, 1, 3, 0, 4).reshape(4, share, -1).astype(BF16)
    gain_sum = pick(gain_parts, tp_index, 0).astype(F32)
    for j in (1, 2, 3):
        sent = pick(gain_parts, jnp.bitwise_xor(tp_index, j), 0)
        gain_sum = gain_sum + trade(sent, j * low).astype(F32)
    gain_sum = gain_sum.reshape((2,) * len(dp) + (-1,))
    gain_sum = jnp.transpose(gain_sum, tuple(reversed(range(len(dp)))) + (len(dp),))
    gain_sum = gain_sum.reshape(share, -1)
    decay_sum = DECAY_SCALE * jax.nn.sigmoid(-decay_vec) * sums[2]
    small_grads = jnp.concatenate(
        [
            sums[4:8].T,
            sums[3][:, None],
            sums[0][:, None],
            sums[1][:, None],
            decay_sum[:, None],
            narrow(rate_square),
            narrow(gate_square),
        ],
        axis=1,
    )
    per_row = small_grads.shape[1]
    packed = jnp.concatenate([small_grads.reshape(share, -1), gain_sum], axis=1).astype(BF16)
    packed = scatter_rows(packed, dp, me)
    gain_grads = packed[channel_rows * per_row :].reshape(2, -1)
    mine = packed[: channel_rows * per_row].reshape(channel_rows, per_row)
    return (
        block_output.reshape(rows, span, width),
        input_grad.reshape(rows, span, width),
        gain_grads[0],
        branch_weight_grad,
        recur_weight_grad,
        mine[:, :TAPS],
        mine[:, 4],
        mine[:, 8 : 8 + block_size],
        mine[:, 5],
        mine[:, 8 + block_size :],
        mine[:, 6],
        mine[:, 7],
        mixer_weight_grad,
        gain_grads[1],
        gate_weight_grad,
        up_weight_grad,
        down_weight_grad,
    )


def solution(mesh):
    tokens, spread, table = P("fsdp", "seq", None), P(AXES), P(AXES, None)
    in_specs = (
        tokens, P(), spread, table, table, table, spread, table, spread, table, spread, spread,
        table, spread, table, table, table, tokens,
    )
    out_specs = (
        tokens, tokens, spread, table, table, table, spread, table, spread, table, spread, spread,
        table, spread, table, table, table,
    )
    return jax.shard_map(shards, mesh=mesh, in_specs=in_specs, out_specs=out_specs, check_vma=False)
```

```python
import functools

import jax
import jax.numpy as jnp
import numpy as np
from jax import lax
from jax.experimental import pallas as pl
from jax.experimental.pallas import tpu as pltpu
from jax.sharding import PartitionSpec as P

AXES = ("seq", "fsdp")
TAPS = 4
EPSILON = 1e-06
DECAY_SCALE = 8.0
VMEM_BYTES = 56 * 1024 * 1024
BF16 = jnp.bfloat16
F32 = jnp.float32


def device_bits(seq_count, fsdp_count, rows, block):
    low = fsdp_count
    while low * rows < block:
        low *= 2
    total = seq_count * fsdp_count
    every = [1 << k for k in reversed(range(total.bit_length() - 1))]
    return low, tuple(every)


def linear_index():
    return lax.axis_index("seq") * lax.axis_size("fsdp") + lax.axis_index("fsdp")


def bit_of(index, bit):
    return lax.rem(lax.div(index, jnp.int32(bit)), jnp.int32(2))


def number_of(index, bits):
    value = jnp.int32(0)
    for b in bits:
        value = value * 2 + bit_of(index, b)
    return value


def fence(value, *others):
    return lax.optimization_barrier((value,) + others)[0]


def trade(value, mask):
    count = lax.axis_size("seq") * lax.axis_size("fsdp")
    return lax.ppermute(value, AXES, [(i, i ^ mask) for i in range(count)])


class Streams:
    def __init__(self):
        self.last = {}

    def trade(self, value, bit):
        if bit > 1:
            if bit in self.last:
                value = fence(value, self.last[bit])
            self.last[bit] = value = trade(value, bit)
            return value
        return trade(value, bit)


def pick(value, index, axis):
    return lax.dynamic_index_in_dim(value, index, axis, keepdims=False)


def put(buffer, part, index, axis):
    return lax.dynamic_update_index_in_dim(buffer, part, index, axis)


def gather_units(own, bits, send):
    units = [(0, own)]
    for b in bits:
        units += [(mask | b, send(unit, b)) for mask, unit in units]
    return units


def copy_kernel(count, shapes, places, scalars, *refs):
    pieces, wholes, sems = refs[:count], refs[count:-1], refs[-1]
    copies = []
    for i, piece in enumerate(pieces):
        for source, which, target in places(i, scalars[0]):
            here = piece if source is None else piece.at[source]
            copies.append(
                pltpu.make_async_copy(here, wholes[which].at[target], sems.at[len(copies)])
            )
    for c in copies:
        c.start()
    for c in copies:
        c.wait()


def assemble(pieces, shapes, places, me, copies):
    where = pl.BlockSpec(memory_space=pl.ANY)
    return pl.pallas_call(
        functools.partial(copy_kernel, len(pieces), shapes, places),
        out_shape=[jax.ShapeDtypeStruct(shape, pieces[0].dtype) for shape in shapes],
        in_specs=[pl.BlockSpec(memory_space=pltpu.SMEM)] + [where] * len(pieces),
        out_specs=[pl.BlockSpec(memory_space=pltpu.VMEM)] * len(shapes),
        scratch_shapes=[pltpu.SemaphoreType.DMA((copies,))],
        compiler_params=pltpu.CompilerParams(vmem_limit_bytes=VMEM_BYTES),
    )(me.astype(jnp.int32).reshape(1), *pieces)


def stack_pieces(pieces, me):
    (whole,) = assemble(
        pieces,
        [(len(pieces),) + pieces[0].shape],
        lambda i, at: [(None, 0, i)],
        me,
        len(pieces),
    )
    return whole


def halves(value, axis, bit, me):
    mine = bit_of(me, bit)
    return pick(value, 1 - mine, axis), pick(value, mine, axis)


def scatter_bits(value, axes, bits, me, send):
    for k, (b, axis) in enumerate(zip(bits, axes)):
        away, kept = halves(value, axis, b, me)
        value = kept.astype(F32) + send(away.astype(BF16), b).astype(F32)
        if k < len(bits) - 1:
            value = value.astype(BF16)
    return value


def share_list(own, low):
    half = own.shape[-2] // 2
    one, two = trade(own, low), trade(own, 2 * low)
    three = (trade(two[..., :half, :], low), trade(one[..., half:, :], 2 * low))
    return [own, one, two, three]


def place_tokens(lists, me):
    rows, width = lists[0][0].shape
    pieces, spots = [], []
    for k, units in enumerate(lists):
        for j, unit in enumerate(units[:3]):
            pieces.append(unit)
            spots.append(pl.ds((4 * k + j) * rows, rows))
        for i, unit in enumerate(units[3]):
            pieces.append(unit)
            spots.append(pl.ds((4 * k + 3) * rows + i * (rows // 2), rows // 2))
    (whole,) = assemble(
        pieces,
        [(4 * len(lists) * rows, width)],
        lambda i, at: [(None, 0, spots[i])],
        me,
        len(pieces),
    )
    return whole


def sum_tokens(partial, low):
    total = partial[0].astype(F32)
    for j in (1, 2, 3):
        total = total + trade(partial[j], j * low).astype(F32)
    return total


def project(left, weight):
    return lax.dot_general(left, weight, (((1,), (1,)), ((), ())), preferred_element_type=F32)


def back_project(left, weight):
    return lax.dot_general(left, weight, (((1,), (0,)), ((), ())), preferred_element_type=F32)


def outer(grads, values):
    return lax.dot_general(grads, values, (((0,), (0,)), ((), ())), preferred_element_type=F32)


def inverse_rms(values):
    return lax.rsqrt(jnp.mean(values * values, axis=-1, keepdims=True) + EPSILON)


def gelu_parts(v):
    c = 0.7978845608028654
    t = jnp.tanh(c * (v + 0.044715 * v * v * v))
    act = 0.5 * v * (1.0 + t)
    slope = 0.5 * (1.0 + t) + 0.5 * v * (1.0 - t * t) * c * (1.0 + 3 * 0.044715 * v * v)
    return act, slope


def call(body, outs, scalars, arrays, scratch=()):
    return pl.pallas_call(
        body,
        out_shape=[jax.ShapeDtypeStruct(shape, kind) for shape, kind in outs],
        in_specs=[pl.BlockSpec(memory_space=pltpu.SMEM)]
        + [pl.BlockSpec(memory_space=pltpu.VMEM)] * len(arrays),
        out_specs=[pl.BlockSpec(memory_space=pltpu.VMEM)] * len(outs),
        scratch_shapes=list(scratch),
        compiler_params=pltpu.CompilerParams(vmem_limit_bytes=VMEM_BYTES),
    )(scalars, *arrays)


def block_number(scalars, n, rows, step):
    return jnp.bitwise_xor(scalars[0], (n // rows) * step)


def injection(s, speed):
    y = speed * s
    e = jnp.exp(-y)
    z = 2.0 * y
    series = 1.0 - z * (1 / 7)
    for k in (6, 5, 4, 3, 2):
        series = 1.0 - z * (1 / k) * series
    return e, jnp.sqrt(jnp.where(z < 0.35, z * series, 1.0 - e * e))


def span_scan(a, b, reverse):
    span, channels = a.shape
    within = lax.broadcasted_iota(jnp.int32, (span, channels), 0) % 8
    for k in (1, 2, 4):
        turn = span - k if reverse else k
        reached = within < 8 - k if reverse else within >= k
        a_far = jnp.where(reached, pltpu.roll(a, turn, 0), 1.0)
        b_far = jnp.where(reached, pltpu.roll(b, turn, 0), 0.0)
        b = b + a * b_far
        a = a * a_far
    count = span // 8
    order = range(count - 1, -1, -1) if reverse else range(count)
    edge = 0 if reverse else 7
    a_all, b_all = [None] * count, [None] * count
    p = jnp.ones((1, channels), F32)
    h = jnp.zeros((1, channels), F32)
    for i in order:
        a_i, b_i = a[8 * i : 8 * i + 8], b[8 * i : 8 * i + 8]
        b_all[i] = b_i + a_i * h
        a_all[i] = a_i * p
        p = a_all[i][edge : edge + 1]
        h = b_all[i][edge : edge + 1]
    return jnp.concatenate(a_all, axis=0), jnp.concatenate(b_all, axis=0), p, h


def sequence_marks(scalars, block, row, span, total_len):
    rows = row[1]
    slots = (scalars.shape[0] - 1) // rows
    place = block * span + lax.broadcasted_iota(jnp.int32, (span, 8), 0)
    column = lax.broadcasted_iota(jnp.int32, (span, 8), 1)
    other = place + jnp.where(column <= 3, -column, column - 3)
    here = jnp.full((span, 8), -1, jnp.int32)
    there = jnp.full((span, 8), -1, jnp.int32)
    first = jnp.zeros((span, 8), jnp.int32)
    offset = jnp.int32(0)
    for j in range(slots):
        length = scalars[1 + row[0] * slots + j]
        live = jnp.where(length > 0, 1, 0)
        here = here + jnp.where(place >= offset, live, 0)
        there = there + jnp.where(other >= offset, live, 0)
        first = first + jnp.where(place == offset, live, 0)
        offset = offset + length
    inside = (other >= 0) & (other < total_len)
    same = jnp.where(inside & (here == there), 1, 0)
    return jnp.where(column == 0, first, same).astype(F32)


def forward_kernel(
    rows, step, total_len, scalars, recur, halo, coef, rate_rows, gate_rows, spread, diagonal,
    conv, s_out, q_out, prod, part, ends, marks, rate_w, gate_w, pad,
):
    count, span, channels = recur.shape
    for n in range(count):
        block = block_number(scalars, n, rows, step)
        marks[n] = sequence_marks(scalars, block, (n % rows, rows), span, total_len)
    for narrow, wide in ((rate_rows, rate_w), (gate_rows, gate_w)):
        wide[...] = (back_project(narrow[...], spread[...]) * diagonal[...].astype(F32)).astype(BF16)

    def convolve(n, carry):
        block = block_number(scalars, n, rows, step)
        before = jnp.bitwise_xor(jnp.maximum(block - 1, 0), scalars[0])
        pad[4:8, :] = halo[before * rows + n % rows]
        pad[8:, :] = recur[n].astype(F32)
        total = coef[4:5, :] + coef[0:1, :] * pad[8:, :]
        for k in range(1, TAPS):
            total = total + coef[k : k + 1, :] * pad[8 - k : 8 - k + span, :] * marks[n][:, k : k + 1]
        conv[n] = total.astype(BF16)
        return carry

    lax.fori_loop(0, count, convolve, 0)
    flat = conv[...].reshape(count * span, channels)
    s_out[...] = project(flat, rate_w[...]).reshape(count, span, channels)
    q_out[...] = project(flat, gate_w[...]).reshape(count, span, channels)

    def scan(n, carry):
        s = jax.nn.sigmoid(s_out[n] + coef[5:6, :])
        q = jax.nn.sigmoid(q_out[n] + coef[6:7, :])
        s_out[n] = s
        q_out[n] = q
        e, m = injection(s, coef[7:8, :])
        decay = e * (1.0 - marks[n][:, 0:1])
        p_all, h_all, p, h = span_scan(decay, m * q * conv[n].astype(F32), False)
        prod[n] = p_all
        part[n] = h_all
        ends[n, 0:1, :] = p
        ends[n, 1:2, :] = h
        return carry

    lax.fori_loop(0, count, scan, 0)


def join(ends, into, scalars, rows, blocks, reverse):
    def lap(k, carry):
        block = blocks - 1 - k if reverse else k
        place = jnp.bitwise_xor(block, scalars[0]) * rows
        new = []
        for r in range(rows):
            into[block * rows + r] = carry[r]
            pair = ends[place + r]
            new.append(pair[0:1] * carry[r] + pair[1:2])
        return tuple(new)

    channels = into.shape[-1]
    lax.fori_loop(0, blocks, lap, (jnp.zeros((1, channels), F32),) * rows)


def state_kernel(rows, step, scalars, prod, part, ends, branch, state, mixed, came, into):
    count = prod.shape[0]
    join(ends, into, scalars, rows, into.shape[0] // rows, False)

    def finish(n, carry):
        incoming = into[block_number(scalars, n, rows, step) * rows + n % rows]
        h = part[n] + prod[n] * incoming
        came[n] = incoming
        state[n] = h
        mixed[n] = (h * gelu_parts(branch[n])[0]).astype(BF16)
        return carry

    lax.fori_loop(0, count, finish, 0)


def adjoint_kernel(
    scalars, grad_mixed, state, branch, s_in, marks, coef, grad_branch, prod, part, ends, pad
):
    count, span, channels = state.shape
    pad[span:, :] = jnp.ones((8, channels), F32)

    def scan(n, carry):
        act, slope = gelu_parts(branch[n])
        grad = grad_mixed[n]
        grad_branch[n] = (grad * state[n] * slope).astype(BF16)
        decay = jnp.exp(-coef[7:8, :] * s_in[n]) * (1.0 - marks[n][:, 0:1])
        pad[:span, :] = decay
        p_all, h_all, p, h = span_scan(pad[1 : span + 1, :], grad * act, True)
        prod[n] = p_all
        part[n] = h_all
        ends[n, 0:1, :] = decay[0:1] * p
        ends[n, 1:2, :] = decay[0:1] * h
        return carry

    lax.fori_loop(0, count, scan, 0)


def gates_kernel(
    rows, step, scalars, prod, part, ends, s_in, q_in, conv, state, came, recur, halo, marks, coef,
    rate_w, gate_w, collect, diagonal, eye, grad_conv, edges, packed, grad_rate, grad_gate, sums,
    into, pad, pad_two,
):
    count, span, channels = prod.shape
    join(ends, into, scalars, rows, into.shape[0] // rows, True)
    sums[...] = jnp.zeros((8, channels), F32)

    def terms(n, carry):
        block = block_number(scalars, n, rows, step)
        total = part[n] + prod[n] * into[block * rows + n % rows]
        pad[7:8, :] = came[n]
        pad[8:, :] = state[n]
        s, q = s_in[n], q_in[n]
        e, m = injection(s, coef[7:8, :])
        c = conv[n].astype(F32)
        first = marks[n][:, 0:1]
        grad_log = total * (pad[7 : 7 + span, :] * e * (1.0 - first) - e * e * q * c / m)
        rate = -coef[7:8, :] * s * (1.0 - s) * grad_log
        gate = total * m * c * q * (1.0 - q)
        grad_conv[n] = total * m * q
        grad_rate[pl.ds(pl.multiple_of(n * span, span), span), :] = rate.astype(BF16)
        grad_gate[pl.ds(pl.multiple_of(n * span, span), span), :] = gate.astype(BF16)
        sums[5:6, :] += jnp.sum(rate, axis=0, keepdims=True)
        sums[6:7, :] += jnp.sum(gate, axis=0, keepdims=True)
        sums[7:8, :] += jnp.sum(coef[8:9, :] * s * grad_log, axis=0, keepdims=True)
        return carry

    lax.fori_loop(0, count, terms, 0)
    through = back_project(grad_rate[...], rate_w[...]) + back_project(grad_gate[...], gate_w[...])
    grad_conv[...] += through.reshape(count, span, channels)
    flat = conv[...].reshape(count * span, channels)

    def kernel_terms(n, carry):
        block = block_number(scalars, n, rows, step)
        before = jnp.bitwise_xor(jnp.maximum(block - 1, 0), scalars[0])
        pad_two[4:8, :] = halo[before * rows + n % rows]
        pad_two[8:, :] = recur[n].astype(F32)
        grad = grad_conv[n]
        edges[n] = grad[:4].astype(BF16)
        sums[4:5, :] += jnp.sum(grad, axis=0, keepdims=True)
        sums[0:1, :] += jnp.sum(grad * pad_two[8:, :], axis=0, keepdims=True)
        for k in range(1, TAPS):
            term = grad * pad_two[8 - k : 8 - k + span, :] * marks[n][:, k : k + 1]
            sums[k : k + 1, :] += jnp.sum(term, axis=0, keepdims=True)
        return carry

    lax.fori_loop(0, count, kernel_terms, 0)
    on = diagonal[...].astype(F32)
    size = collect.shape[1] // 3
    total = back_project((outer(grad_rate[...], flat) * on).astype(BF16), collect[:, :size])
    total += back_project((outer(grad_gate[...], flat) * on).astype(BF16), collect[:, size : 2 * size])
    turned = project(eye[...], sums[...].astype(BF16))
    total += back_project(turned.astype(BF16), collect[:8, 2 * size :])
    packed[...] = total.astype(BF16)


def unconvolve_kernel(rows, step, blocks, scalars, grad_conv, halo, marks, coef, grad_recur, pad):
    count, span, channels = grad_conv.shape

    def body(n, carry):
        block = block_number(scalars, n, rows, step)
        behind = jnp.bitwise_xor(jnp.minimum(block + 1, blocks - 1), scalars[0])
        pad[:span, :] = grad_conv[n]
        pad[span : span + 4, :] = halo[behind * rows + n % rows]
        total = coef[0:1, :] * pad[:span, :]
        for k in range(1, TAPS):
            seen = marks[n][:, 3 + k : 4 + k]
            total = total + coef[k : k + 1, :] * pad[k : k + span, :] * seen
        grad_recur[n] = total.astype(BF16)
        return carry

    lax.fori_loop(0, count, body, 0)


def shards(
    block_input,
    seq_lengths,
    mixer_gain,
    branch_weight,
    recur_weight,
    conv_kernel,
    conv_bias,
    recur_gate_weight,
    recur_gate_bias,
    input_gate_weight,
    input_gate_bias,
    decay_param,
    mixer_weight,
    mlp_gain,
    gate_weight,
    up_weight,
    down_weight,
    cotangent,
):
    rows, span, width = block_input.shape
    tokens = rows * span
    seq_count, fsdp_count = lax.axis_size("seq"), lax.axis_size("fsdp")
    channel_rows = branch_weight.shape[0]
    hidden_rows = gate_weight.shape[0]
    out_rows = mixer_weight.shape[0]
    block_size = recur_gate_weight.shape[1]
    low, every = device_bits(seq_count, fsdp_count, channel_rows, block_size)
    wide = 4 * low
    tp, tp_wide = (2 * low, low), (wide, 2 * low, low)
    dp = tuple(b for b in every if b not in tp)
    dp_wide = tuple(b for b in every if b not in tp_wide)
    above, below = tuple(b for b in dp if b > low), tuple(b for b in dp if b < low)
    above_wide = tuple(b for b in above if b != wide)
    step = low // fsdp_count
    me = linear_index().astype(jnp.int32)
    seq_index = lax.axis_index("seq")
    tp_index, wide_index = number_of(me, tp), number_of(me, tp_wide)
    share, share_wide = 1 << len(dp), 1 << len(dp_wide)
    high, deep, high_wide = 1 << len(above), 1 << len(below), 1 << len(above_wide)
    channels = share * channel_rows
    hidden = share_wide * hidden_rows
    blocks = 4 * rows
    seq_dp = tuple(b for b in dp if b >= fsdp_count)
    streams = Streams()

    def across_blocks(own):
        units = sorted(gather_units(own, seq_dp, trade), key=lambda unit: unit[0])
        every_slot = jnp.stack([unit for _, unit in units])
        every_slot = every_slot.reshape((-1, step) + own.shape)
        return jnp.moveaxis(every_slot, 2, 1).reshape((seq_count,) + own.shape[1:])

    def slot_places(units, bits, arrays):
        def places(i, at):
            slot = number_of(jnp.bitwise_xor(at, units[i][0]), bits)
            if arrays == 1:
                return [(None, 0, slot)]
            return [(a, a, slot) for a in range(arrays)]

        return places

    def column_places(units, up_bits, down_bits):
        def places(i, at):
            owner = jnp.bitwise_xor(at, units[i][0])
            return [(None, 0, (number_of(owner, up_bits), slice(None), number_of(owner, down_bits)))]

        return places

    def by_rank(weight, upper, ranks):
        split = weight.reshape(weight.shape[0], upper, ranks, -1)
        return jnp.transpose(split, (2, 0, 1, 3)).reshape(ranks, weight.shape[0], -1)

    def swap_ranks(parts, index, bits):
        masks = [sum(b for k, b in enumerate(reversed(bits)) if j >> k & 1) for j in range(len(parts))]
        sent = [pick(parts, jnp.bitwise_xor(index, j), 0) for j in range(len(parts))]
        return [trade(part, mask) if mask else part for part, mask in zip(sent, masks)]

    input_own = block_input.reshape(tokens, width)
    cot_own = cotangent.reshape(tokens, width)
    input_all = place_tokens([share_list(input_own, low)], me)

    gain_columns = jnp.stack([mixer_gain, mlp_gain], axis=1)
    gain_columns = jnp.pad(gain_columns, ((0, channel_rows - out_rows), (0, 0)))
    small = jnp.concatenate(
        [
            conv_kernel,
            jnp.stack([conv_bias, recur_gate_bias, input_gate_bias, decay_param], axis=1),
            gain_columns,
            recur_gate_weight,
            input_gate_weight,
        ],
        axis=1,
    )
    for i, b in enumerate(dp):
        got = trade(small, b)
        mine = bit_of(me, b) == 0
        small = jnp.stack([jnp.where(mine, small, got), jnp.where(mine, got, small)], axis=i)
    small = small.reshape((share,) + small.shape[len(dp) :])
    gains = jnp.moveaxis(small[:, :out_rows, 8:10], 2, 0)
    gains = jnp.stack([gains] + [trade(gains, j * low) for j in (1, 2, 3)])
    gains = jnp.take(gains, jnp.bitwise_xor(tp_index, jnp.arange(4)), axis=0)
    gains = gains.reshape(4, 2, high, deep, out_rows).transpose(1, 2, 0, 3, 4).reshape(2, width)
    gain_one, gain_two = gains[0].astype(F32), gains[1].astype(F32)
    small = small.reshape(channels, -1)
    coef = small[:, :8].astype(F32).T
    decay_vec = coef[7:]
    coef = jnp.concatenate(
        [
            coef[:7],
            DECAY_SCALE * jax.nn.softplus(-decay_vec),
            DECAY_SCALE * jax.nn.sigmoid(-decay_vec),
            jnp.zeros((7, channels), F32),
        ]
    )
    rate_rows, gate_rows = small[:, 10 : 10 + block_size], small[:, 10 + block_size :]
    number = np.arange(channels)
    spread = jnp.asarray(number[None] % block_size == np.arange(block_size)[:, None], BF16)
    diagonal = jnp.asarray(number[None] // block_size == number[:, None] // block_size, BF16)
    eye = jnp.asarray(np.eye(channels), BF16)
    packed_width = -(-(2 * block_size + 8) // 128) * 128
    collect = np.zeros((channels, 3, packed_width))
    collect[number, 0, number % block_size] = 1
    collect[number, 1, block_size + number % block_size] = 1
    collect[np.arange(8), 2, 2 * block_size + np.arange(8)] = 1
    collect = jnp.asarray(collect.reshape(channels, -1), BF16)
    lengths = lax.dynamic_slice_in_dim(seq_lengths, lax.axis_index("fsdp") * rows, rows, 0)
    scalars = jnp.concatenate([seq_index.astype(jnp.int32)[None], lengths.reshape(-1)])

    units = gather_units(jnp.stack([branch_weight, recur_weight]), dp, streams.trade)
    branch_q, recur_q = assemble(
        [unit for _, unit in units],
        [(share, channel_rows, width)] * 2,
        slot_places(units, dp, 2),
        me,
        2 * share,
    )
    branch_q, recur_q = branch_q.reshape(channels, width), recur_q.reshape(channels, width)
    mixer_weight = fence(mixer_weight, input_all)
    pieces = swap_ranks(by_rank(mixer_weight, high, 4), tp_index, tp)
    (piece,) = assemble(
        pieces,
        [(4,) + pieces[0].shape],
        lambda i, at: [(None, 0, jnp.bitwise_xor(number_of(at, tp), i))],
        me,
        4,
    )
    units = gather_units(piece, dp, streams.trade)
    (mixer_q,) = assemble(
        [unit for _, unit in units],
        [(high, 4, deep, out_rows, channels)],
        column_places(units, above, below),
        me,
        share,
    )
    mixer_q = mixer_q.reshape(width, channels)

    cot_far = streams.trade(cot_own, wide)
    cot_lists = [share_list(cot_own, low), share_list(cot_far, low)]

    units = gather_units(jnp.stack([gate_weight, up_weight]), dp_wide, streams.trade)
    gate_q, up_q = assemble(
        [unit for _, unit in units],
        [(share_wide, hidden_rows, width)] * 2,
        slot_places(units, dp_wide, 2),
        me,
        2 * share_wide,
    )
    gate_q, up_q = gate_q.reshape(hidden, width), up_q.reshape(hidden, width)

    scale_one = inverse_rms(input_all.astype(F32))
    normed = (input_all.astype(F32) * scale_one * gain_one).astype(BF16)
    recur_in = project(normed, recur_q).astype(BF16).reshape(blocks, span, channels)
    edge = recur_in[:, span - 4 :].reshape(4, rows, 4, channels)
    halo = across_blocks(edge).astype(F32).reshape(seq_count * rows, 4, channels)
    branch = project(normed, branch_q).reshape(blocks, span, channels)
    shape = (blocks, span, channels)
    one = (blocks, 1, channels)
    everything = (seq_count * rows, 1, channels)
    square = (channels, channels)
    padded = (span + 8, channels)
    conv, s_val, q_val, prod, part, ends, marks, rate_wide, gate_wide = call(
        functools.partial(forward_kernel, rows, step, seq_count * span),
        [(shape, BF16)] + [(shape, F32)] * 4
        + [((blocks, 2, channels), F32), ((blocks, span, 8), F32), (square, BF16), (square, BF16)],
        scalars,
        [recur_in, halo, coef, rate_rows, gate_rows, spread, diagonal],
        [pltpu.VMEM(padded, F32)],
    )
    ends = across_blocks(ends.reshape(4, rows, 2, channels)).reshape(-1, 2, channels)
    state, mixed, came = call(
        functools.partial(state_kernel, rows, step),
        [(shape, F32), (shape, BF16), (one, F32)],
        scalars,
        [prod, part, ends, branch],
        [pltpu.VMEM(everything, F32)],
    )
    mixed_flat = mixed.reshape(4 * tokens, channels)
    mixer_part = project(mixed_flat, mixer_q).astype(BF16).reshape(4, tokens, width)
    residual = input_own.astype(F32) + sum_tokens(mixer_part, low)

    down_weight = fence(down_weight, mixed)
    pieces = swap_ranks(by_rank(down_weight, high_wide, 8), wide_index, tp_wide)
    (piece,) = assemble(
        pieces,
        [(8,) + pieces[0].shape],
        lambda i, at: [(None, 0, jnp.bitwise_xor(number_of(at, tp_wide), i))],
        me,
        8,
    )
    units = gather_units(piece, dp_wide, streams.trade)
    (down_q,) = assemble(
        [unit for _, unit in units],
        [(high_wide, 8, deep, out_rows, hidden)],
        column_places(units, above_wide, below),
        me,
        share_wide,
    )
    down_q = down_q.reshape(width, hidden)

    scale_two = inverse_rms(residual)
    unit_two = residual * scale_two
    normed_own = (unit_two * gain_two).astype(BF16)
    normed_far = streams.trade(normed_own, wide)
    normed_two = place_tokens([share_list(normed_own, low), share_list(normed_far, low)], me)
    cot_all = place_tokens(cot_lists, me)
    gate_val = project(normed_two, gate_q)
    up_val = project(normed_two, up_q)
    act, slope = gelu_parts(gate_val)
    hidden_val = (act * up_val).astype(BF16)
    grad_hidden = back_project(cot_all, down_q)
    grad_gate = (grad_hidden * up_val * slope).astype(BF16)
    grad_up = (grad_hidden * act).astype(BF16)
    grad_two_part = (back_project(grad_gate, gate_q) + back_project(grad_up, up_q)).astype(BF16)
    grad_two_part = grad_two_part.reshape(2, 4, tokens, width)
    grad_two_far = sum_tokens(grad_two_part[1], low).astype(BF16)
    grad_two = sum_tokens(grad_two_part[0], low) + trade(grad_two_far, wide).astype(F32)
    down_part = project(hidden_val, down_q).astype(BF16).reshape(2, 4, tokens, width)
    down_far = sum_tokens(down_part[1], low).astype(BF16)
    down_own = sum_tokens(down_part[0], low) + trade(down_far, wide).astype(F32)
    block_output = (residual + down_own).astype(BF16)
    scaled = grad_two * gain_two
    grad_residual = cot_own.astype(F32) + scale_two * (
        scaled - unit_two * jnp.mean(scaled * unit_two, axis=-1, keepdims=True)
    )
    gain_two_part = jnp.sum(grad_two * unit_two, axis=0)

    def row_axes(bits):
        return list(range(len(bits)))

    def row_grad(grads, values, bits):
        whole = outer(grads, values).astype(BF16)
        whole = whole.reshape((2,) * len(bits) + (-1, width))
        order = tuple(reversed(bits))
        return scatter_bits(whole, tuple(reversed(row_axes(bits))), order, me, streams.trade)

    def column_grad(grads, values, bits, ranks):
        up_bits = [b for b in bits if b > low]
        whole = outer(grads, values).astype(BF16)
        whole = whole.reshape((2,) * len(up_bits) + (ranks,) + (2,) * (len(bits) - len(up_bits)) + (out_rows, -1))
        axes = [k if b > low else k + 1 for k, b in enumerate(bits)]
        order = tuple(reversed(bits))
        return scatter_bits(whole, tuple(reversed(axes)), order, me, streams.trade).astype(BF16)

    def join_ranks(parts, index, bits, upper):
        ranks = len(parts)
        got = swap_ranks(parts, index, bits)
        count = got[0].shape[0]
        whole = jnp.zeros((ranks, count, upper, got[0].shape[1] // upper), BF16)
        for j, part in enumerate(got):
            whole = put(whole, part.reshape(count, upper, -1), jnp.bitwise_xor(index, j), 0)
        return jnp.transpose(whole, (1, 2, 0, 3)).reshape(count, -1).astype(F32)

    down_grad = column_grad(cot_all, hidden_val, dp_wide, 8)
    gate_weight_grad = row_grad(grad_gate, normed_two, dp_wide)
    up_weight_grad = row_grad(grad_up, normed_two, dp_wide)

    grad_mix_own = fence(grad_residual.astype(BF16), gate_weight_grad, down_grad)
    grad_mix = place_tokens([share_list(grad_mix_own, low)], me)
    grad_mixed = back_project(grad_mix, mixer_q).reshape(shape)
    grad_branch, prod_back, part_back, ends_back = call(
        adjoint_kernel,
        [(shape, BF16), (shape, F32), (shape, F32), ((blocks, 2, channels), F32)],
        scalars,
        [grad_mixed, state, branch, s_val, marks, coef],
        [pltpu.VMEM(padded, F32)],
    )
    ends_back = across_blocks(ends_back.reshape(4, rows, 2, channels)).reshape(-1, 2, channels)
    ends_back = fence(ends_back, up_weight_grad, block_output)
    down_weight_grad = join_ranks(down_grad.reshape(8, out_rows, hidden), wide_index, tp_wide, high_wide)
    mixer_grad = column_grad(grad_mix, mixed_flat, dp, 4)
    grad_branch = grad_branch.reshape(4 * tokens, channels)
    branch_weight_grad = row_grad(grad_branch, normed, dp)
    packed_shape = (channels, packed_width)
    grad_conv, edge_back, packed = call(
        functools.partial(gates_kernel, rows, step),
        [(shape, F32), ((blocks, 4, channels), BF16), (packed_shape, BF16)],
        scalars,
        [
            prod_back, part_back, ends_back, s_val, q_val, conv, state, came, recur_in, halo,
            marks, coef, rate_wide, gate_wide, collect, diagonal, eye,
        ],
        [
            pltpu.VMEM((4 * tokens, channels), BF16),
            pltpu.VMEM((4 * tokens, channels), BF16),
            pltpu.VMEM((8, channels), F32),
            pltpu.VMEM(everything, F32),
            pltpu.VMEM(padded, F32),
            pltpu.VMEM(padded, F32),
        ],
    )
    edge_back = edge_back.reshape(4, rows, 4, channels)
    halo_back = across_blocks(edge_back).astype(F32).reshape(seq_count * rows, 4, channels)
    halo_back = fence(halo_back, down_weight_grad)
    (grad_recur,) = call(
        functools.partial(unconvolve_kernel, rows, step, seq_count),
        [(shape, BF16)],
        scalars,
        [grad_conv, halo_back, marks, coef],
        [pltpu.VMEM(padded, F32)],
    )
    grad_recur = grad_recur.reshape(4 * tokens, channels)
    grad_normed_part = back_project(grad_branch, branch_q) + back_project(grad_recur, recur_q)
    grad_normed_sent = grad_normed_part.astype(BF16)
    gain_one_part = jnp.sum(grad_normed_sent.astype(F32) * input_all.astype(F32) * scale_one, axis=0)
    grad_normed_sent = fence(grad_normed_sent.reshape(4, tokens, width), mixer_grad)
    grad_normed = sum_tokens(grad_normed_sent, low)
    own_scale = scale_one[:tokens]
    unit_one = input_own.astype(F32) * own_scale
    scaled_one = grad_normed * gain_one
    input_grad = (
        grad_residual
        + own_scale
        * (scaled_one - unit_one * jnp.mean(scaled_one * unit_one, axis=-1, keepdims=True))
    ).astype(BF16)
    mixer_weight_grad = join_ranks(mixer_grad.reshape(4, out_rows, channels), tp_index, tp, high)
    recur_weight_grad = row_grad(grad_recur, normed, dp)

    packed = packed.reshape((2,) * len(dp) + (channel_rows, packed_width))
    order = tuple(reversed(dp))
    axes = tuple(reversed(row_axes(dp)))
    packed = scatter_bits(packed, axes, order, me, trade)
    gain_parts = jnp.stack([gain_one_part, gain_two_part]).reshape(2, high, 4, deep, -1)
    gain_parts = gain_parts.transpose(2, 1, 3, 0, 4).reshape(4, share, -1).astype(BF16)
    gain_sum = pick(gain_parts, tp_index, 0).astype(F32)
    for j in (1, 2, 3):
        sent = pick(gain_parts, jnp.bitwise_xor(tp_index, j), 0)
        gain_sum = gain_sum + trade(sent, j * low).astype(F32)
    gain_sum = gain_sum.astype(BF16).reshape((2,) * len(dp) + (-1,))
    gain_grads = scatter_bits(gain_sum, axes, order, me, trade).reshape(2, -1)
    numbers = packed[:, 2 * block_size : 2 * block_size + 8]
    return (
        block_output.reshape(rows, span, width),
        input_grad.reshape(rows, span, width),
        gain_grads[0],
        branch_weight_grad,
        recur_weight_grad,
        numbers[:, :TAPS],
        numbers[:, 4],
        packed[:, :block_size],
        numbers[:, 5],
        packed[:, block_size : 2 * block_size],
        numbers[:, 6],
        numbers[:, 7],
        mixer_weight_grad,
        gain_grads[1],
        gate_weight_grad,
        up_weight_grad,
        down_weight_grad,
    )


def solution(mesh):
    tokens, spread, table = P("fsdp", "seq", None), P(AXES), P(AXES, None)
    in_specs = (
        tokens, P(), spread, table, table, table, spread, table, spread, table, spread, spread,
        table, spread, table, table, table, tokens,
    )
    out_specs = (
        tokens, tokens, spread, table, table, table, spread, table, spread, table, spread, spread,
        table, spread, table, table, table,
    )
    return jax.shard_map(shards, mesh=mesh, in_specs=in_specs, out_specs=out_specs, check_vma=False)
```

```python
import functools
import math

import jax
import jax.numpy as jnp
import numpy as np
from jax import lax
from jax.experimental import pallas as pl
from jax.experimental.pallas import tpu as pltpu
from jax.sharding import PartitionSpec as P

AXES = ("seq", "fsdp")
TAPS = 4
EPSILON = 1e-06
DECAY_SCALE = 8.0
VMEM_BYTES = 56 * 1024 * 1024
BF16 = jnp.bfloat16
F32 = jnp.float32


def device_bits(seq_count, fsdp_count, rows, block):
    low = fsdp_count
    while low * rows < block:
        low *= 2
    total = seq_count * fsdp_count
    every = [1 << k for k in reversed(range(total.bit_length() - 1))]
    return low, tuple(every)


def linear_index():
    return lax.axis_index("seq") * lax.axis_size("fsdp") + lax.axis_index("fsdp")


def bit_of(index, bit):
    return lax.rem(lax.div(index, jnp.int32(bit)), jnp.int32(2))


def number_of(index, bits):
    value = jnp.int32(0)
    for b in bits:
        value = value * 2 + bit_of(index, b)
    return value


def fence(value, *others):
    return lax.optimization_barrier((value,) + others)[0]


def fence_all(values, *others):
    return list(lax.optimization_barrier(tuple(values) + others)[: len(values)])


def trade(value, mask):
    count = lax.axis_size("seq") * lax.axis_size("fsdp")
    return lax.ppermute(value, AXES, [(i, i ^ mask) for i in range(count)])


class Streams:
    def __init__(self):
        self.last = {}

    def trade(self, value, bit):
        if bit > 1:
            if bit in self.last:
                value = fence(value, self.last[bit])
            self.last[bit] = value = trade(value, bit)
            return value
        return trade(value, bit)


def pick(value, index, axis):
    return lax.dynamic_index_in_dim(value, index, axis, keepdims=False)


def put(buffer, part, index, axis):
    return lax.dynamic_update_index_in_dim(buffer, part, index, axis)


def gather_units(owns, bits, send):
    lists = [[(0, own)] for own in owns]
    for b in bits:
        fresh = [[] for _ in owns]
        for k in range(len(lists[0])):
            for units, new in zip(lists, fresh):
                mask, unit = units[k]
                new.append((mask | b, send(unit, b)))
        lists = [units + new for units, new in zip(lists, fresh)]
    return lists


def copy_kernel(count, shapes, places, scalars, *refs):
    pieces, wholes, sems = refs[:count], refs[count:-1], refs[-1]
    copies = []
    for i, piece in enumerate(pieces):
        for source, which, target in places(i, scalars[0]):
            here = piece if source is None else piece.at[source]
            copies.append(
                pltpu.make_async_copy(here, wholes[which].at[target], sems.at[len(copies)])
            )
    for c in copies:
        c.start()
    for c in copies:
        c.wait()


def assemble(pieces, shapes, places, me, copies):
    where = pl.BlockSpec(memory_space=pl.ANY)
    return pl.pallas_call(
        functools.partial(copy_kernel, len(pieces), shapes, places),
        out_shape=[jax.ShapeDtypeStruct(shape, pieces[0].dtype) for shape in shapes],
        in_specs=[pl.BlockSpec(memory_space=pltpu.SMEM)] + [where] * len(pieces),
        out_specs=[pl.BlockSpec(memory_space=pltpu.VMEM)] * len(shapes),
        scratch_shapes=[pltpu.SemaphoreType.DMA((copies,))],
        compiler_params=pltpu.CompilerParams(vmem_limit_bytes=VMEM_BYTES),
        cost_estimate=pl.CostEstimate(
            flops=0, bytes_accessed=4 * sum(piece.size for piece in pieces), transcendentals=0
        ),
    )(me.astype(jnp.int32).reshape(1), *pieces)


def halves(value, axis, bit, me):
    mine = bit_of(me, bit)
    return pick(value, 1 - mine, axis), pick(value, mine, axis)


class Reduction:
    def __init__(self, value, axes, bits, me):
        self.kept, self.got, self.me = value, None, me
        self.left = list(zip(axes, bits))

    def send(self, *after):
        value = self.total(*after).astype(BF16)
        axis, bit = self.left.pop()
        away, self.kept = halves(value, axis, bit, self.me)
        self.got = trade(away, bit)
        return away

    def send_to(self, count, *after):
        while len(self.left) > count:
            away = self.send(*after)
        return away

    def total(self, *after):
        if self.got is None:
            return self.kept
        return self.kept.astype(F32) + fence(self.got, *after).astype(F32)


def reduce_rows(whole, bits, me):
    whole = whole.astype(BF16).reshape((2,) * len(bits) + (whole.shape[0] >> len(bits), -1))
    return Reduction(whole, range(len(bits)), bits, me)


def reduce_columns(whole, bits, ranks, low, me):
    above = sum(b > low for b in bits)
    split = (2,) * above + (ranks,) + (2,) * (len(bits) - above)
    rows = whole.shape[0] // (ranks << len(bits))
    whole = whole.astype(BF16).reshape(split + (rows, whole.shape[1]))
    return Reduction(whole, [k if b > low else k + 1 for k, b in enumerate(bits)], bits, me)


def share_list(own, low):
    half = own.shape[-2] // 2
    one, two = trade(own, low), trade(own, 2 * low)
    three = (trade(two[..., :half, :], low), trade(one[..., half:, :], 2 * low))
    return [own, one, two, *three]


def share_direct(own, low):
    return [own] + [trade(own, j * low) for j in (1, 2, 3)]


def place_tokens(units, low, me):
    rows, width = units[0].shape
    pieces = list(units)

    def places(i, at):
        slot = jnp.bitwise_xor(number_of(at, (2 * low, low)), min(i, 3))
        start = pl.multiple_of(slot * rows + (rows // 2 if i == 4 else 0), rows // 2)
        return [(None, 0, pl.ds(start, pieces[i].shape[0]))]

    (whole,) = assemble(pieces, [(4 * rows, width)], places, me, len(pieces))
    return whole


def groups_of(bits, count):
    inside = [0]
    for b in bits:
        inside = [i | k for i in inside for k in (0, b)]
    return [[first | i for i in inside] for first in range(count) if not first & sum(bits)]


def line_of(bits):
    fsdp_count, count = lax.axis_size("fsdp"), lax.axis_size("seq") * lax.axis_size("fsdp")
    if sum(bits) == fsdp_count - 1:
        return {"axis_name": "fsdp"}
    if sum(bits) == count - 1:
        return {"axis_name": AXES}
    return {"axis_name": AXES, "axis_index_groups": groups_of(bits, count)}


def gather_along(own, bits, axis):
    return lax.all_gather(own, axis=axis, tiled=True, **line_of(bits))


def scatter_along(partial, bits, axis):
    return lax.psum_scatter(partial, scatter_dimension=axis, tiled=True, **line_of(bits))


def pair_up(own, bits, me, *pins):
    value = own
    for i, b in enumerate(bits):
        got = fence(trade(value, b), *pins)
        mine = bit_of(me, b) == 0
        value = jnp.stack([jnp.where(mine, value, got), jnp.where(mine, got, value)], axis=i)
    return value.reshape((1 << len(bits),) + own.shape)


def exchange(parts, step):
    ranks, count = parts.shape[0], lax.axis_size("seq")
    inside = [r * step for r in range(ranks)]
    groups = [[b + i for i in inside] for b in range(count) if not b & ((ranks - 1) * step)]
    return lax.all_to_all(parts, "seq", 0, 0, axis_index_groups=groups, tiled=True)


def sum_tokens(partial, step):
    return jnp.sum(exchange(partial, step).astype(F32), axis=0)


def project(left, weight):
    return lax.dot_general(left, weight, (((1,), (1,)), ((), ())), preferred_element_type=F32)


def back_project(left, weight):
    return lax.dot_general(left, weight, (((1,), (0,)), ((), ())), preferred_element_type=F32)


def outer(grads, values):
    return lax.dot_general(grads, values, (((0,), (0,)), ((), ())), preferred_element_type=F32)


def inverse_rms(values):
    return lax.rsqrt(jnp.mean(values * values, axis=-1, keepdims=True) + EPSILON)


def gelu_parts(v):
    c = 0.7978845608028654
    t = jnp.tanh(c * (v + 0.044715 * v * v * v))
    act = 0.5 * v * (1.0 + t)
    slope = 0.5 * (1.0 + t) + 0.5 * v * (1.0 - t * t) * c * (1.0 + 3 * 0.044715 * v * v)
    return act, slope


def call(body, outs, scalars, arrays, scratch=(), passes=1):
    sizes = [array.size * array.dtype.itemsize for array in arrays]
    sizes += [math.prod(shape) * jnp.dtype(kind).itemsize for shape, kind in outs]
    return pl.pallas_call(
        body,
        out_shape=[jax.ShapeDtypeStruct(shape, kind) for shape, kind in outs],
        in_specs=[pl.BlockSpec(memory_space=pltpu.SMEM)]
        + [pl.BlockSpec(memory_space=pltpu.VMEM)] * len(arrays),
        out_specs=[pl.BlockSpec(memory_space=pltpu.VMEM)] * len(outs),
        scratch_shapes=list(scratch),
        compiler_params=pltpu.CompilerParams(vmem_limit_bytes=VMEM_BYTES),
        cost_estimate=pl.CostEstimate(
            flops=0, bytes_accessed=passes * sum(sizes), transcendentals=0
        ),
    )(scalars, *arrays)


def block_number(scalars, n, rows, step):
    return jnp.bitwise_xor(scalars[0], (n // rows) * step)


def injection(s, speed):
    y = speed * s
    e = jnp.exp(-y)
    z = 2.0 * y
    series = 1.0 - z * (1 / 7)
    for k in (6, 5, 4, 3, 2):
        series = 1.0 - z * (1 / k) * series
    return e, jnp.sqrt(jnp.where(z < 0.35, z * series, 1.0 - e * e))


def span_scan(a, b, reverse):
    span, channels = a.shape
    within = lax.broadcasted_iota(jnp.int32, (span, channels), 0) % 8
    for k in (1, 2, 4):
        turn = span - k if reverse else k
        reached = within < 8 - k if reverse else within >= k
        a_far = jnp.where(reached, pltpu.roll(a, turn, 0), 1.0)
        b_far = jnp.where(reached, pltpu.roll(b, turn, 0), 0.0)
        b = b + a * b_far
        a = a * a_far
    count = span // 8
    order = range(count - 1, -1, -1) if reverse else range(count)
    edge = 0 if reverse else 7
    a_all, b_all = [None] * count, [None] * count
    p = jnp.ones((1, channels), F32)
    h = jnp.zeros((1, channels), F32)
    for i in order:
        a_i, b_i = a[8 * i : 8 * i + 8], b[8 * i : 8 * i + 8]
        b_all[i] = b_i + a_i * h
        a_all[i] = a_i * p
        p = a_all[i][edge : edge + 1]
        h = b_all[i][edge : edge + 1]
    return jnp.concatenate(a_all, axis=0), jnp.concatenate(b_all, axis=0), p, h


def sequence_marks(scalars, block, row, span, total_len):
    rows = row[1]
    slots = (scalars.shape[0] - 1) // rows
    place = block * span + lax.broadcasted_iota(jnp.int32, (span, 8), 0)
    column = lax.broadcasted_iota(jnp.int32, (span, 8), 1)
    other = place + jnp.where(column <= 3, -column, column - 3)
    here = jnp.full((span, 8), -1, jnp.int32)
    there = jnp.full((span, 8), -1, jnp.int32)
    first = jnp.zeros((span, 8), jnp.int32)
    offset = jnp.int32(0)
    for j in range(slots):
        length = scalars[1 + row[0] * slots + j]
        live = jnp.where(length > 0, 1, 0)
        here = here + jnp.where(place >= offset, live, 0)
        there = there + jnp.where(other >= offset, live, 0)
        first = first + jnp.where(place == offset, live, 0)
        offset = offset + length
    inside = (other >= 0) & (other < total_len)
    same = jnp.where(inside & (here == there), 1, 0)
    return jnp.where(column == 0, first, same).astype(F32)


def forward_kernel(
    rows, step, total_len, scalars, recur, halo, coef, rate_rows, gate_rows, spread, diagonal,
    conv, s_out, q_out, prod, part, ends, marks, rate_w, gate_w, pad,
):
    count, span, channels = recur.shape

    def mark(n, carry):
        block = block_number(scalars, n, rows, step)
        marks[n] = sequence_marks(scalars, block, (n % rows, rows), span, total_len)
        return carry

    lax.fori_loop(0, count, mark, 0)
    for narrow, wide in ((rate_rows, rate_w), (gate_rows, gate_w)):
        wide[...] = (back_project(narrow[...], spread[...]) * diagonal[...].astype(F32)).astype(BF16)

    def convolve(n, carry):
        block = block_number(scalars, n, rows, step)
        before = jnp.bitwise_xor(jnp.maximum(block - 1, 0), scalars[0])
        pad[4:8, :] = halo[before * rows + n % rows]
        pad[8:, :] = recur[n].astype(F32)
        total = coef[4:5, :] + coef[0:1, :] * pad[8:, :]
        for k in range(1, TAPS):
            total = total + coef[k : k + 1, :] * pad[8 - k : 8 - k + span, :] * marks[n][:, k : k + 1]
        conv[n] = total.astype(BF16)
        return carry

    lax.fori_loop(0, count, convolve, 0)
    flat = conv[...].reshape(count * span, channels)
    s_out[...] = project(flat, rate_w[...]).reshape(count, span, channels)
    q_out[...] = project(flat, gate_w[...]).reshape(count, span, channels)

    def scan(n, carry):
        s = jax.nn.sigmoid(s_out[n] + coef[5:6, :])
        q = jax.nn.sigmoid(q_out[n] + coef[6:7, :])
        s_out[n] = s
        q_out[n] = q
        e, m = injection(s, coef[7:8, :])
        decay = e * (1.0 - marks[n][:, 0:1])
        p_all, h_all, p, h = span_scan(decay, m * q * conv[n].astype(F32), False)
        prod[n] = p_all
        part[n] = h_all
        ends[n, 0:1, :] = p
        ends[n, 1:2, :] = h
        return carry

    lax.fori_loop(0, count, scan, 0)


def join(ends, into, scalars, rows, blocks, reverse):
    def lap(k, carry):
        block = blocks - 1 - k if reverse else k
        place = jnp.bitwise_xor(block, scalars[0]) * rows
        new = []
        for r in range(rows):
            into[block * rows + r] = carry[r]
            pair = ends[place + r]
            new.append(pair[0:1] * carry[r] + pair[1:2])
        return tuple(new)

    channels = into.shape[-1]
    lax.fori_loop(0, blocks, lap, (jnp.zeros((1, channels), F32),) * rows)


def state_kernel(rows, step, scalars, prod, part, ends, branch, state, mixed, came, into):
    count = prod.shape[0]
    join(ends, into, scalars, rows, into.shape[0] // rows, False)

    def finish(n, carry):
        incoming = into[block_number(scalars, n, rows, step) * rows + n % rows]
        h = part[n] + prod[n] * incoming
        came[n] = incoming
        state[n] = h
        mixed[n] = (h * gelu_parts(branch[n])[0]).astype(BF16)
        return carry

    lax.fori_loop(0, count, finish, 0)


def adjoint_kernel(
    scalars, grad_mixed, state, branch, s_in, marks, coef, grad_branch, prod, part, ends, pad
):
    count, span, channels = state.shape
    pad[span:, :] = jnp.ones((8, channels), F32)

    def scan(n, carry):
        act, slope = gelu_parts(branch[n])
        grad = grad_mixed[n]
        grad_branch[n] = (grad * state[n] * slope).astype(BF16)
        decay = jnp.exp(-coef[7:8, :] * s_in[n]) * (1.0 - marks[n][:, 0:1])
        pad[:span, :] = decay
        p_all, h_all, p, h = span_scan(pad[1 : span + 1, :], grad * act, True)
        prod[n] = p_all
        part[n] = h_all
        ends[n, 0:1, :] = decay[0:1] * p
        ends[n, 1:2, :] = decay[0:1] * h
        return carry

    lax.fori_loop(0, count, scan, 0)


def gates_kernel(
    rows, step, scalars, prod, part, ends, s_in, q_in, conv, state, came, recur, halo, marks, coef,
    rate_w, gate_w, collect, diagonal, eye, grad_conv, edges, packed, grad_rate, grad_gate, sums,
    into, pad, pad_two,
):
    count, span, channels = prod.shape
    join(ends, into, scalars, rows, into.shape[0] // rows, True)
    sums[...] = jnp.zeros((8, channels), F32)

    def terms(n, carry):
        block = block_number(scalars, n, rows, step)
        total = part[n] + prod[n] * into[block * rows + n % rows]
        pad[7:8, :] = came[n]
        pad[8:, :] = state[n]
        s, q = s_in[n], q_in[n]
        e, m = injection(s, coef[7:8, :])
        c = conv[n].astype(F32)
        first = marks[n][:, 0:1]
        grad_log = total * (pad[7 : 7 + span, :] * e * (1.0 - first) - e * e * q * c / m)
        rate = -coef[7:8, :] * s * (1.0 - s) * grad_log
        gate = total * m * c * q * (1.0 - q)
        grad_conv[n] = total * m * q
        grad_rate[pl.ds(pl.multiple_of(n * span, span), span), :] = rate.astype(BF16)
        grad_gate[pl.ds(pl.multiple_of(n * span, span), span), :] = gate.astype(BF16)
        sums[5:6, :] += jnp.sum(rate, axis=0, keepdims=True)
        sums[6:7, :] += jnp.sum(gate, axis=0, keepdims=True)
        sums[7:8, :] += jnp.sum(coef[8:9, :] * s * grad_log, axis=0, keepdims=True)
        return carry

    lax.fori_loop(0, count, terms, 0)
    through = back_project(grad_rate[...], rate_w[...]) + back_project(grad_gate[...], gate_w[...])
    grad_conv[...] += through.reshape(count, span, channels)
    flat = conv[...].reshape(count * span, channels)

    def kernel_terms(n, carry):
        block = block_number(scalars, n, rows, step)
        before = jnp.bitwise_xor(jnp.maximum(block - 1, 0), scalars[0])
        pad_two[4:8, :] = halo[before * rows + n % rows]
        pad_two[8:, :] = recur[n].astype(F32)
        grad = grad_conv[n]
        edges[n] = grad[:4].astype(BF16)
        sums[4:5, :] += jnp.sum(grad, axis=0, keepdims=True)
        sums[0:1, :] += jnp.sum(grad * pad_two[8:, :], axis=0, keepdims=True)
        for k in range(1, TAPS):
            term = grad * pad_two[8 - k : 8 - k + span, :] * marks[n][:, k : k + 1]
            sums[k : k + 1, :] += jnp.sum(term, axis=0, keepdims=True)
        return carry

    lax.fori_loop(0, count, kernel_terms, 0)
    on = diagonal[...].astype(F32)
    size = collect.shape[1] // 3
    total = back_project((outer(grad_rate[...], flat) * on).astype(BF16), collect[:, :size])
    total += back_project((outer(grad_gate[...], flat) * on).astype(BF16), collect[:, size : 2 * size])
    turned = project(eye[...], sums[...].astype(BF16))
    total += back_project(turned.astype(BF16), collect[:8, 2 * size :])
    packed[...] = total.astype(BF16)


def unconvolve_kernel(rows, step, blocks, scalars, grad_conv, halo, marks, coef, grad_recur, pad):
    count, span, channels = grad_conv.shape

    def body(n, carry):
        block = block_number(scalars, n, rows, step)
        behind = jnp.bitwise_xor(jnp.minimum(block + 1, blocks - 1), scalars[0])
        pad[:span, :] = grad_conv[n]
        pad[span : span + 4, :] = halo[behind * rows + n % rows]
        total = coef[0:1, :] * pad[:span, :]
        for k in range(1, TAPS):
            seen = marks[n][:, 3 + k : 4 + k]
            total = total + coef[k : k + 1, :] * pad[k : k + span, :] * seen
        grad_recur[n] = total.astype(BF16)
        return carry

    lax.fori_loop(0, count, body, 0)


def forward_backward_kernel(
    tokens, cot, gate_w, up_w, down_w, down, grad, hidden, grad_gate, grad_up, down_sum, grad_sum
):
    step = pl.program_id(0)
    gate_val = project(tokens[...], gate_w[...])
    up_val = project(tokens[...], up_w[...])
    act, slope = gelu_parts(gate_val)
    hidden_val = (act * up_val).astype(BF16)
    hidden[...] = hidden_val
    grad_hidden = back_project(cot[...], down_w[...])
    gate_part = (grad_hidden * up_val * slope).astype(BF16)
    up_part = (grad_hidden * act).astype(BF16)
    grad_gate[...] = gate_part
    grad_up[...] = up_part

    @pl.when(step == 0)
    def _():
        grad_sum[...] = jnp.zeros(grad_sum.shape, F32)
        down_sum[...] = jnp.zeros(down_sum.shape, F32)

    grad_sum[...] += back_project(gate_part, gate_w[...]) + back_project(up_part, up_w[...])
    down_sum[...] += project(hidden_val, down_w[...])

    @pl.when(step == pl.num_programs(0) - 1)
    def _():
        grad[...] = grad_sum[...].astype(BF16)
        down[...] = down_sum[...].astype(BF16)


def pack_kernel(taps, bias, rate_bias, gate_bias, decay, gain_one, gain_two, rate_w, gate_w, packed):
    count, size = rate_w.shape
    packed[...] = jnp.zeros(packed.shape, F32)
    packed[:count, :size] = rate_w[...].astype(F32)
    packed[:count, size : 2 * size] = gate_w[...].astype(F32)
    first = packed.shape[0] - 16
    packed[first : first + TAPS, :count] = taps[...].astype(F32).T
    for i, row in enumerate((bias, rate_bias, gate_bias, decay, gain_one, gain_two)):
        packed[first + TAPS + i : first + TAPS + i + 1, : row.shape[1]] = row[...].astype(F32)


def lay_kernel(ranks, upper, me, *refs):
    pieces, whole = refs[:-1], refs[-1]
    for i, piece in enumerate(pieces):
        rank = jnp.bitwise_xor(me[0], i)
        size = piece.shape[1] // upper
        for u in range(upper):
            start = pl.multiple_of((u * ranks + rank) * size, 128)
            whole[:, pl.ds(start, size)] = piece[:, u * size : (u + 1) * size].astype(F32)


def feed_forward(tokens, cot, gate_w, up_w, down_w):
    count, width = tokens.shape
    units = gate_w.shape[0]
    tile = 256
    whole = pl.BlockSpec((count, width), lambda i: (0, 0))
    row_tile = pl.BlockSpec((tile, width), lambda i: (i, 0))
    column_tile = pl.BlockSpec((count, tile), lambda i: (0, i))
    return pl.pallas_call(
        forward_backward_kernel,
        grid=(units // tile,),
        out_shape=[jax.ShapeDtypeStruct((count, width), BF16)] * 2
        + [jax.ShapeDtypeStruct((count, units), BF16)] * 3,
        in_specs=[whole, whole, row_tile, row_tile, pl.BlockSpec((width, tile), lambda i: (0, i))],
        out_specs=[whole, whole] + [column_tile] * 3,
        scratch_shapes=[pltpu.VMEM((count, width), F32)] * 2,
        compiler_params=pltpu.CompilerParams(
            dimension_semantics=("arbitrary",), vmem_limit_bytes=VMEM_BYTES
        ),
        cost_estimate=pl.CostEstimate(
            flops=12 * count * width * units,
            bytes_accessed=2 * (4 * count * width + 3 * width * units + 3 * count * units),
            transcendentals=count * units,
        ),
    )(tokens, cot, gate_w, up_w, down_w)


def shards(
    block_input,
    seq_lengths,
    mixer_gain,
    branch_weight,
    recur_weight,
    conv_kernel,
    conv_bias,
    recur_gate_weight,
    recur_gate_bias,
    input_gate_weight,
    input_gate_bias,
    decay_param,
    mixer_weight,
    mlp_gain,
    gate_weight,
    up_weight,
    down_weight,
    cotangent,
):
    rows, span, width = block_input.shape
    tokens = rows * span
    seq_count, fsdp_count = lax.axis_size("seq"), lax.axis_size("fsdp")
    device_count = seq_count * fsdp_count
    channel_rows = branch_weight.shape[0]
    hidden_rows = gate_weight.shape[0]
    out_rows = mixer_weight.shape[0]
    block_size = recur_gate_weight.shape[1]
    low, every = device_bits(seq_count, fsdp_count, channel_rows, block_size)
    wide = 4 * low
    tp, tp_wide = (2 * low, low), (wide, 2 * low, low)
    dp = tuple(b for b in every if b not in tp)
    dp_wide = tuple(b for b in every if b not in tp_wide)
    above, below = tuple(b for b in dp if b > low), tuple(b for b in dp if b < low)
    above_wide = tuple(b for b in above if b != wide)
    step = low // fsdp_count
    me = linear_index().astype(jnp.int32)
    seq_index = lax.axis_index("seq")
    tp_index = number_of(me, tp)
    share, share_wide = 1 << len(dp), 1 << len(dp_wide)
    high, deep, high_wide = 1 << len(above), 1 << len(below), 1 << len(above_wide)
    channels = share * channel_rows
    hidden = share_wide * hidden_rows
    blocks = 4 * rows
    seq_dp = tuple(b for b in dp if b >= fsdp_count)
    streams = Streams()

    def across_blocks(own):
        units = sorted(gather_units([own], seq_dp, trade)[0], key=lambda unit: unit[0])
        every_slot = jnp.stack([unit for _, unit in units])
        every_slot = every_slot.reshape((-1, step) + own.shape)
        return jnp.moveaxis(every_slot, 2, 1).reshape((seq_count,) + own.shape[1:])

    def place_rows(units):
        def places(i, at):
            return [(None, 0, number_of(jnp.bitwise_xor(at, units[i][0]), dp))]

        one = units[0][1].shape
        pieces = [unit for _, unit in units]
        (whole,) = assemble(pieces, [(len(units),) + one], places, me, len(units))
        return whole.reshape(-1, one[1])

    def place_columns(units):
        def places(i, at):
            owner = jnp.bitwise_xor(at, units[i][0])
            return [(None, 0, (number_of(owner, above), slice(None), number_of(owner, below)))]

        ranks, one = units[0][1].shape[0], units[0][1].shape[1:]
        pieces = [unit for _, unit in units]
        (whole,) = assemble(pieces, [(high, ranks, deep) + one], places, me, len(units))
        return whole.reshape(-1, one[1])

    def by_rank(weight, upper, ranks):
        split = weight.reshape(weight.shape[0], upper, ranks, -1)
        return jnp.transpose(split, (2, 0, 1, 3)).reshape(ranks, weight.shape[0], -1)

    input_own = block_input.reshape(tokens, width)
    cot_own = cotangent.reshape(tokens, width)
    packed_width = -(-(2 * block_size + 8) // 128) * 128
    extra = -(-channel_rows // 16) * 16
    small = pl.pallas_call(
        pack_kernel,
        out_shape=jax.ShapeDtypeStruct((extra + 16, packed_width), F32),
        compiler_params=pltpu.CompilerParams(vmem_limit_bytes=VMEM_BYTES),
    )(
        conv_kernel,
        *(v[None] for v in (conv_bias, recur_gate_bias, input_gate_bias, decay_param)),
        mixer_gain[None],
        mlp_gain[None],
        recur_gate_weight,
        input_gate_weight,
    ).astype(BF16)
    one = small.shape
    for i, b in enumerate(dp):
        got = trade(small, b)
        if i == 0:
            first_got = got
        mine = bit_of(me, b) == 0
        small = jnp.stack([jnp.where(mine, small, got), jnp.where(mine, got, small)], axis=i)
    small = small.reshape((share,) + one)
    gains = small[:, extra + TAPS + 4 : extra + TAPS + 6, :out_rows].reshape(high, deep, 2, out_rows)
    for i, b in enumerate(tp):
        got = trade(gains, b)
        mine = bit_of(me, b) == 0
        gains = jnp.stack([jnp.where(mine, gains, got), jnp.where(mine, got, gains)], axis=i + 1)
    last_got = got
    gains = jnp.moveaxis(gains, 4, 0).reshape(2, width)
    gain_one, gain_two = gains[0].astype(F32), gains[1].astype(F32)
    numbers = jnp.moveaxis(small[:, extra : extra + TAPS + 4, :channel_rows], 1, 0)
    numbers = numbers.reshape(TAPS + 4, channels).astype(F32)
    gate_rows = small[:, :channel_rows, : 2 * block_size].reshape(channels, -1)

    input_list = share_list(input_own, low)
    recur_units, branch_units = gather_units(
        [fence(recur_weight, first_got), branch_weight], dp, streams.trade
    )
    input_all = place_tokens(input_list, low, me)
    piece = exchange(fence(by_rank(mixer_weight, high, 4), *input_list[1:]), step)
    (mixer_units,) = gather_units([piece], dp, streams.trade)
    recur_q, branch_q = place_rows(recur_units), place_rows(branch_units)
    mixer_q = place_columns(mixer_units)
    cot_near_list = share_direct(fence(cot_own, input_all), low)

    coef = numbers
    decay_vec = coef[7:]
    coef = jnp.concatenate(
        [
            coef[:7],
            DECAY_SCALE * jax.nn.softplus(-decay_vec),
            DECAY_SCALE * jax.nn.sigmoid(-decay_vec),
            jnp.zeros((7, channels), F32),
        ]
    )
    rate_rows, gate_rows = gate_rows[:, :block_size], gate_rows[:, block_size:]
    number = np.arange(channels)
    spread = jnp.asarray(number[None] % block_size == np.arange(block_size)[:, None], BF16)
    diagonal = jnp.asarray(number[None] // block_size == number[:, None] // block_size, BF16)
    eye = jnp.asarray(np.eye(channels), BF16)
    collect = np.zeros((channels, 3, packed_width))
    collect[number, 0, number % block_size] = 1
    collect[number, 1, block_size + number % block_size] = 1
    collect[np.arange(8), 2, 2 * block_size + np.arange(8)] = 1
    collect = jnp.asarray(collect.reshape(channels, -1), BF16)
    lengths = lax.dynamic_slice_in_dim(seq_lengths, lax.axis_index("fsdp") * rows, rows, 0)
    base = seq_index.astype(jnp.int32) - tp_index * step
    scalars = jnp.concatenate([base[None], lengths.reshape(-1)])

    def join_ranks(parts, upper):
        got = exchange(parts, step)
        got = got.reshape(got.shape[:2] + (upper, -1))
        return jnp.transpose(got, (1, 2, 0, 3)).reshape(got.shape[1], -1).astype(F32)

    scale_one = inverse_rms(input_all.astype(F32))
    normed = (input_all.astype(F32) * scale_one * gain_one).astype(BF16)
    recur_in = project(normed, recur_q).astype(BF16)
    edge = recur_in.reshape(blocks, span, channels)[:, span - 4 :].reshape(4, rows, 4, channels)
    halo = across_blocks(edge)
    cot_far = trade(fence(cot_own, halo), wide)
    halo = halo.astype(F32).reshape(seq_count * rows, 4, channels)
    recur_in = recur_in.reshape(blocks, span, channels)
    shape = (blocks, span, channels)
    one = (blocks, 1, channels)
    everything = (seq_count * rows, 1, channels)
    square = (channels, channels)
    padded = (span + 8, channels)
    conv, s_val, q_val, prod, part, ends, marks, rate_wide, gate_wide = call(
        functools.partial(forward_kernel, rows, step, seq_count * span),
        [(shape, BF16)] + [(shape, F32)] * 4
        + [((blocks, 2, channels), F32), ((blocks, span, 8), F32), (square, BF16), (square, BF16)],
        scalars,
        [recur_in, halo, coef, rate_rows, gate_rows, spread, diagonal],
        [pltpu.VMEM(padded, F32)],
        4,
    )
    ends_all = across_blocks(ends.reshape(4, rows, 2, channels)).reshape(-1, 2, channels)
    branch = project(normed, fence(branch_q, ends)).reshape(blocks, span, channels)
    ends = fence(ends_all, branch)
    state, mixed, came = call(
        functools.partial(state_kernel, rows, step),
        [(shape, F32), (shape, BF16), (one, F32)],
        scalars,
        [prod, part, ends, branch],
        [pltpu.VMEM(everything, F32)],
        2,
    )
    cot_far_list = share_direct(fence(cot_far, mixed), low)
    down_piece = exchange(fence(by_rank(down_weight, high_wide, 8), mixed), step)
    gate_pair, up_pair, down_pair = (
        pair_up(fence(weight, recur_q), above_wide, me)
        for weight in (gate_weight, up_weight, down_piece)
    )
    gate_q = gather_along(gate_pair, below, 1).reshape(hidden, width)
    up_q = gather_along(up_pair, below, 1).reshape(hidden, width)
    down_q = gather_along(down_pair, below, 2).reshape(width, hidden)
    mixed_flat = mixed.reshape(4 * tokens, channels)
    cot_near = place_tokens(fence_all(cot_near_list, mixed), low, me)
    mixer_part = project(mixed_flat, mixer_q).astype(BF16).reshape(4, tokens, width)
    residual = input_own.astype(F32) + sum_tokens(mixer_part, step)


    scale_two = inverse_rms(residual)
    unit_two = residual * scale_two
    normed_own = (unit_two * gain_two).astype(BF16)
    normed_far = trade(normed_own, wide)
    near_list = share_direct(normed_own, low)
    far_list = share_direct(fence(normed_far, *near_list[1:]), low)
    near = place_tokens(near_list, low, me)
    cot_far = place_tokens(fence_all(cot_far_list, normed_own), low, me)
    near_out = feed_forward(near, cot_near, gate_q, up_q, down_q)
    ranks_shape = (4, tokens, width)
    far = place_tokens(far_list, low, me)
    far_out = feed_forward(far, cot_far, gate_q, up_q, down_q)
    grad_far_parts = exchange(far_out[1].reshape(ranks_shape), step)

    def finish(partial, bits):
        partial = partial.reshape((2,) * len(bits) + partial.shape[1:])
        grad = Reduction(partial, range(len(bits)), bits, me)
        if bits:
            grad.send_to(0)
        return grad.total()

    def both(one, two, k):
        return outer(one[k], near) + outer(two[k], far)

    down_grad = outer(cot_near, near_out[2]) + outer(cot_far, far_out[2])
    down_grad = down_grad.astype(BF16).reshape(high_wide, 8, -1, hidden)
    grad_far_parts = fence(grad_far_parts, down_grad)
    down_grad = finish(scatter_along(down_grad, below, 2), above_wide).reshape(8, out_rows, hidden)
    grad_two_far = jnp.sum(grad_far_parts.astype(F32), axis=0).astype(BF16)
    grad_two_near = sum_tokens(fence(near_out[1], grad_two_far).reshape(ranks_shape), step)
    grad_two = grad_two_near + trade(grad_two_far, wide).astype(F32)
    scaled = grad_two * gain_two
    grad_residual = cot_own.astype(F32) + scale_two * (
        scaled - unit_two * jnp.mean(scaled * unit_two, axis=-1, keepdims=True)
    )
    gain_two_part = jnp.sum(grad_two * unit_two, axis=0)

    grad_mix_own = grad_residual.astype(BF16)
    grad_mix_list = share_list(grad_mix_own, low)
    late = [fence_all(out[3:], grad_mix_own) for out in (near_out, far_out)]
    gate_grad = both(*late, 0).astype(BF16).reshape(high_wide, -1, width)
    up_grad = both(*late, 1).astype(BF16).reshape(high_wide, -1, width)
    down_far = fence(far_out[0].reshape(ranks_shape), grad_mix_list[1], grad_mix_list[2])
    down_far = exchange(down_far, step)
    down_parts = fence(down_grad, grad_mix_own).reshape(2, 4, out_rows, hidden)
    down_sent, down_kept = halves(down_parts, 0, wide, me)
    down_got = trade(down_sent, wide)
    grad_mix = place_tokens(fence_all(grad_mix_list, gate_grad, up_grad, down_got), low, me)
    gate_grad = finish(scatter_along(gate_grad, below, 1), above_wide)
    up_grad = finish(scatter_along(up_grad, below, 1), above_wide)
    grad_mixed = back_project(grad_mix, mixer_q).reshape(shape)
    grad_branch, prod_back, part_back, own_ends = call(
        adjoint_kernel,
        [(shape, BF16), (shape, F32), (shape, F32), ((blocks, 2, channels), F32)],
        scalars,
        [grad_mixed, state, branch, s_val, marks, coef],
        [pltpu.VMEM(padded, F32)],
        3,
    )
    ends_back = across_blocks(own_ends.reshape(4, rows, 2, channels)).reshape(-1, 2, channels)
    grad_branch = grad_branch.reshape(4 * tokens, channels)
    branch_grad = reduce_rows(outer(grad_branch, normed), dp, me)
    mixer_grad = reduce_columns(outer(fence(grad_mix, own_ends), mixed_flat), dp, 4, low, me)
    ends_back = fence(ends_back, branch_grad.send(), mixer_grad.send())
    packed_shape = (channels, packed_width)
    grad_conv, edge_back, packed = call(
        functools.partial(gates_kernel, rows, step),
        [(shape, F32), ((blocks, 4, channels), BF16), (packed_shape, BF16)],
        scalars,
        [
            prod_back, part_back, ends_back, s_val, q_val, conv, state, came, recur_in, halo,
            marks, coef, rate_wide, gate_wide, collect, diagonal, eye,
        ],
        [
            pltpu.VMEM((4 * tokens, channels), BF16),
            pltpu.VMEM((4 * tokens, channels), BF16),
            pltpu.VMEM((8, channels), F32),
            pltpu.VMEM(everything, F32),
            pltpu.VMEM(padded, F32),
            pltpu.VMEM(padded, F32),
        ],
        4,
    )
    edge_back = edge_back.reshape(4, rows, 4, channels)
    down_far = jnp.sum(fence(down_far, edge_back).astype(F32), axis=0).astype(BF16)
    down_far_own = trade(down_far, wide)
    down_near = fence(near_out[0].reshape(ranks_shape), edge_back)
    down_near = [pick(down_near, jnp.bitwise_xor(tp_index, j), 0) for j in range(4)]
    down_near[1:] = [trade(down_near[j], j * low) for j in (1, 2, 3)]
    halo_back = across_blocks(edge_back)
    last = len(dp)
    aways = [grad.send_to(last - 2, edge_back) for grad in (mixer_grad, branch_grad)]
    halo_back = fence(halo_back, *aways, down_far)
    halo_back = halo_back.astype(F32).reshape(seq_count * rows, 4, channels)
    (grad_recur,) = call(
        functools.partial(unconvolve_kernel, rows, step, seq_count),
        [(shape, BF16)],
        scalars,
        [grad_conv, halo_back, marks, coef],
        [pltpu.VMEM(padded, F32)],
        4,
    )
    grad_recur = grad_recur.reshape(4 * tokens, channels)
    recur_grad = reduce_rows(outer(grad_recur, normed), dp, me)
    grad_recur = fence(grad_recur, recur_grad.send())
    grad_normed_part = back_project(grad_branch, branch_q) + back_project(grad_recur, recur_q)
    grad_normed_sent = grad_normed_part.astype(BF16)
    aways = [grad.send_to(0, grad_recur) for grad in (mixer_grad, branch_grad)]
    aways.append(recur_grad.send_to(last - 2, grad_normed_sent))
    grad_normed_sent = fence(grad_normed_sent, *aways, down_far_own)
    gain_one_part = jnp.sum(grad_normed_sent.astype(F32) * input_all.astype(F32) * scale_one, axis=0)
    grad_normed = sum_tokens(grad_normed_sent.reshape(ranks_shape), step)
    own_scale = inverse_rms(input_own.astype(F32))
    unit_one = input_own.astype(F32) * own_scale
    scaled_one = grad_normed * gain_one
    input_grad = (
        grad_residual
        + own_scale
        * (scaled_one - unit_one * jnp.mean(scaled_one * unit_one, axis=-1, keepdims=True))
    ).astype(BF16)
    packed = reduce_rows(fence(packed, grad_normed_sent), dp, me)
    packed_sent = packed.send_to(last - 2)
    sent = recur_grad.send_to(0, packed_sent)
    packed_sent = packed.send_to(0, sent)
    down_got, down_kept = fence_all([down_got, down_kept], packed_sent)
    down_pieces = []
    for j in range(4):
        peer = jnp.bitwise_xor(tp_index, j)
        pair = jnp.stack([pick(down_kept, peer, 0), pick(down_got, peer, 0)])
        down_pieces.append(trade(pair, j * low) if j else pair)
    down_sum = sum(fence(part, packed_sent).astype(F32) for part in down_near + [down_far_own])
    block_output = (residual + down_sum).astype(BF16)
    branch_weight_grad = branch_grad.total(block_output)
    own_half = number_of(me, (wide,))
    flat_pieces = [pair[h] for h in range(2) for pair in down_pieces]
    down_weight_grad = pl.pallas_call(
        functools.partial(lay_kernel, 8, high_wide),
        out_shape=jax.ShapeDtypeStruct((out_rows, 8 * hidden), F32),
        in_specs=[pl.BlockSpec(memory_space=pltpu.SMEM)]
        + [pl.BlockSpec(memory_space=pltpu.VMEM)] * len(flat_pieces),
        out_specs=pl.BlockSpec(memory_space=pltpu.VMEM),
        compiler_params=pltpu.CompilerParams(vmem_limit_bytes=VMEM_BYTES),
    )((own_half * 4 + tp_index).reshape(1), *flat_pieces)
    recur_weight_grad = recur_grad.total(branch_weight_grad)
    packed = packed.total(branch_weight_grad)
    mixer_grad = mixer_grad.total(branch_weight_grad).astype(BF16).reshape(4, out_rows, channels)
    mixer_weight_grad = join_ranks(fence(mixer_grad, grad_normed), high)

    gain_parts = jnp.stack([gain_one_part, gain_two_part]).astype(BF16)
    gain_parts = jnp.moveaxis(gain_parts.reshape(2, device_count, out_rows), 1, 0)
    gain_parts = lax.all_to_all(fence(gain_parts, grad_normed), AXES, 0, 0, tiled=True)
    gain_grads = jnp.sum(gain_parts.astype(F32), axis=0)
    numbers = packed[:, 2 * block_size : 2 * block_size + 8]
    return (
        block_output.reshape(rows, span, width),
        input_grad.reshape(rows, span, width),
        gain_grads[0],
        branch_weight_grad,
        recur_weight_grad,
        numbers[:, :TAPS],
        numbers[:, 4],
        packed[:, :block_size],
        numbers[:, 5],
        packed[:, block_size : 2 * block_size],
        numbers[:, 6],
        numbers[:, 7],
        mixer_weight_grad,
        gain_grads[1],
        gate_grad.reshape(hidden_rows, width).astype(F32),
        up_grad.reshape(hidden_rows, width).astype(F32),
        down_weight_grad,
    )


def solution(mesh):
    tokens, spread, table = P("fsdp", "seq", None), P(AXES), P(AXES, None)
    in_specs = (
        tokens, P(), spread, table, table, table, spread, table, spread, table, spread, spread,
        table, spread, table, table, table, tokens,
    )
    out_specs = (
        tokens, tokens, spread, table, table, table, spread, table, spread, table, spread, spread,
        table, spread, table, table, table,
    )
    return jax.shard_map(shards, mesh=mesh, in_specs=in_specs, out_specs=out_specs, check_vma=False)
```

```python
import functools
import math

import jax
import jax.numpy as jnp
import numpy as np
from jax import lax
from jax.experimental import pallas as pl
from jax.experimental.pallas import tpu as pltpu
from jax.sharding import PartitionSpec as P

AXES = ("seq", "fsdp")
TAPS = 4
EPSILON = 1e-06
DECAY_SCALE = 8.0
VMEM_BYTES = 56 * 1024 * 1024
BF16 = jnp.bfloat16
F32 = jnp.float32


def device_bits(seq_count, fsdp_count, rows, block):
    low = fsdp_count
    while low * rows < block:
        low *= 2
    total = seq_count * fsdp_count
    every = [1 << k for k in reversed(range(total.bit_length() - 1))]
    return low, tuple(every)


def linear_index():
    return lax.axis_index("seq") * lax.axis_size("fsdp") + lax.axis_index("fsdp")


def bit_of(index, bit):
    return lax.rem(lax.div(index, jnp.int32(bit)), jnp.int32(2))


def number_of(index, bits):
    value = jnp.int32(0)
    for b in bits:
        value = value * 2 + bit_of(index, b)
    return value


def fence(value, *others):
    return lax.optimization_barrier((value,) + others)[0]


def fence_all(values, *others):
    return list(lax.optimization_barrier(tuple(values) + others)[: len(values)])


def trade(value, mask):
    count = lax.axis_size("seq") * lax.axis_size("fsdp")
    return lax.ppermute(value, AXES, [(i, i ^ mask) for i in range(count)])


class Streams:
    def __init__(self):
        self.last = {}

    def trade(self, value, bit):
        if bit > 1:
            if bit in self.last:
                value = fence(value, self.last[bit])
            self.last[bit] = value = trade(value, bit)
            return value
        return trade(value, bit)


def pick(value, index, axis):
    return lax.dynamic_index_in_dim(value, index, axis, keepdims=False)


def put(buffer, part, index, axis):
    return lax.dynamic_update_index_in_dim(buffer, part, index, axis)


def gather_units(owns, bits, send):
    lists = [[(0, own)] for own in owns]
    for b in bits:
        fresh = [[] for _ in owns]
        for k in range(len(lists[0])):
            for units, new in zip(lists, fresh):
                mask, unit = units[k]
                new.append((mask | b, send(unit, b)))
        lists = [units + new for units, new in zip(lists, fresh)]
    return lists


def copy_kernel(count, shapes, places, scalars, *refs):
    pieces, wholes, sems = refs[:count], refs[count:-1], refs[-1]
    copies = []
    for i, piece in enumerate(pieces):
        for source, which, target in places(i, scalars[0]):
            here = piece if source is None else piece.at[source]
            copies.append(
                pltpu.make_async_copy(here, wholes[which].at[target], sems.at[len(copies)])
            )
    for c in copies:
        c.start()
    for c in copies:
        c.wait()


def assemble(pieces, shapes, places, me, copies):
    where = pl.BlockSpec(memory_space=pl.ANY)
    return pl.pallas_call(
        functools.partial(copy_kernel, len(pieces), shapes, places),
        out_shape=[jax.ShapeDtypeStruct(shape, pieces[0].dtype) for shape in shapes],
        in_specs=[pl.BlockSpec(memory_space=pltpu.SMEM)] + [where] * len(pieces),
        out_specs=[pl.BlockSpec(memory_space=pltpu.VMEM)] * len(shapes),
        scratch_shapes=[pltpu.SemaphoreType.DMA((copies,))],
        compiler_params=pltpu.CompilerParams(vmem_limit_bytes=VMEM_BYTES),
        cost_estimate=pl.CostEstimate(
            flops=0, bytes_accessed=4 * sum(piece.size for piece in pieces), transcendentals=0
        ),
    )(me.astype(jnp.int32).reshape(1), *pieces)


def halves(value, axis, bit, me):
    mine = bit_of(me, bit)
    return pick(value, 1 - mine, axis), pick(value, mine, axis)


class Reduction:
    def __init__(self, value, axes, bits, me):
        self.kept, self.got, self.me = value, None, me
        self.left = list(zip(axes, bits))

    def send(self, *after):
        value = self.total(*after).astype(BF16)
        axis, bit = self.left.pop()
        away, self.kept = halves(value, axis, bit, self.me)
        self.got = trade(away, bit)
        return away

    def send_to(self, count, *after):
        while len(self.left) > count:
            away = self.send(*after)
        return away

    def total(self, *after):
        if self.got is None:
            return self.kept
        return self.kept.astype(F32) + fence(self.got, *after).astype(F32)


def reduce_rows(whole, bits, me):
    whole = whole.astype(BF16).reshape((2,) * len(bits) + (whole.shape[0] >> len(bits), -1))
    return Reduction(whole, range(len(bits)), bits, me)


def reduce_columns(whole, bits, ranks, low, me):
    above = sum(b > low for b in bits)
    split = (2,) * above + (ranks,) + (2,) * (len(bits) - above)
    rows = whole.shape[0] // (ranks << len(bits))
    whole = whole.astype(BF16).reshape(split + (rows, whole.shape[1]))
    return Reduction(whole, [k if b > low else k + 1 for k, b in enumerate(bits)], bits, me)


def share_list(own, low):
    half = own.shape[-2] // 2
    one, two = trade(own, low), trade(own, 2 * low)
    three = (trade(two[..., :half, :], low), trade(one[..., half:, :], 2 * low))
    return [own, one, two, *three]


def share_direct(own, low):
    return [own] + [trade(own, j * low) for j in (1, 2, 3)]


def place_tokens(units, low, me):
    rows, width = units[0].shape
    pieces = list(units)

    def places(i, at):
        slot = jnp.bitwise_xor(number_of(at, (2 * low, low)), min(i, 3))
        start = pl.multiple_of(slot * rows + (rows // 2 if i == 4 else 0), rows // 2)
        return [(None, 0, pl.ds(start, pieces[i].shape[0]))]

    (whole,) = assemble(pieces, [(4 * rows, width)], places, me, len(pieces))
    return whole


def groups_of(bits, count):
    inside = [0]
    for b in bits:
        inside = [i | k for i in inside for k in (0, b)]
    return [[first | i for i in inside] for first in range(count) if not first & sum(bits)]


def line_of(bits):
    fsdp_count, count = lax.axis_size("fsdp"), lax.axis_size("seq") * lax.axis_size("fsdp")
    if sum(bits) == fsdp_count - 1:
        return {"axis_name": "fsdp"}
    if sum(bits) == count - 1:
        return {"axis_name": AXES}
    return {"axis_name": AXES, "axis_index_groups": groups_of(bits, count)}


def gather_along(own, bits, axis):
    return lax.all_gather(own, axis=axis, tiled=True, **line_of(bits))


def scatter_along(partial, bits, axis):
    return lax.psum_scatter(partial, scatter_dimension=axis, tiled=True, **line_of(bits))


def pair_up(own, bits, me, *pins):
    value = own
    for i, b in enumerate(bits):
        got = fence(trade(value, b), *pins)
        mine = bit_of(me, b) == 0
        value = jnp.stack([jnp.where(mine, value, got), jnp.where(mine, got, value)], axis=i)
    return value.reshape((1 << len(bits),) + own.shape)


def exchange(parts, step):
    ranks, count = parts.shape[0], lax.axis_size("seq")
    inside = [r * step for r in range(ranks)]
    groups = [[b + i for i in inside] for b in range(count) if not b & ((ranks - 1) * step)]
    return lax.all_to_all(parts, "seq", 0, 0, axis_index_groups=groups, tiled=True)


def sum_tokens(partial, step):
    return jnp.sum(exchange(partial, step).astype(F32), axis=0)


def project(left, weight):
    return lax.dot_general(left, weight, (((1,), (1,)), ((), ())), preferred_element_type=F32)


def back_project(left, weight):
    return lax.dot_general(left, weight, (((1,), (0,)), ((), ())), preferred_element_type=F32)


def outer(grads, values):
    return lax.dot_general(grads, values, (((0,), (0,)), ((), ())), preferred_element_type=F32)


def inverse_rms(values):
    return lax.rsqrt(jnp.mean(values * values, axis=-1, keepdims=True) + EPSILON)


def gelu_parts(v):
    c = 0.7978845608028654
    t = jnp.tanh(c * (v + 0.044715 * v * v * v))
    act = 0.5 * v * (1.0 + t)
    slope = 0.5 * (1.0 + t) + 0.5 * v * (1.0 - t * t) * c * (1.0 + 3 * 0.044715 * v * v)
    return act, slope


def call(body, outs, scalars, arrays, scratch=(), passes=1):
    sizes = [array.size * array.dtype.itemsize for array in arrays]
    sizes += [math.prod(shape) * jnp.dtype(kind).itemsize for shape, kind in outs]
    return pl.pallas_call(
        body,
        out_shape=[jax.ShapeDtypeStruct(shape, kind) for shape, kind in outs],
        in_specs=[pl.BlockSpec(memory_space=pltpu.SMEM)]
        + [pl.BlockSpec(memory_space=pltpu.VMEM)] * len(arrays),
        out_specs=[pl.BlockSpec(memory_space=pltpu.VMEM)] * len(outs),
        scratch_shapes=list(scratch),
        compiler_params=pltpu.CompilerParams(vmem_limit_bytes=VMEM_BYTES),
        cost_estimate=pl.CostEstimate(
            flops=0, bytes_accessed=passes * sum(sizes), transcendentals=0
        ),
    )(scalars, *arrays)


def block_number(scalars, n, rows, step):
    return jnp.bitwise_xor(scalars[0], (n // rows) * step)


def injection(s, speed):
    y = speed * s
    e = jnp.exp(-y)
    z = 2.0 * y
    series = 1.0 - z * (1 / 7)
    for k in (6, 5, 4, 3, 2):
        series = 1.0 - z * (1 / k) * series
    return e, jnp.sqrt(jnp.where(z < 0.35, z * series, 1.0 - e * e))


def span_scan(a, b, reverse):
    span, channels = a.shape
    within = lax.broadcasted_iota(jnp.int32, (span, channels), 0) % 8
    for k in (1, 2, 4):
        turn = span - k if reverse else k
        reached = within < 8 - k if reverse else within >= k
        a_far = jnp.where(reached, pltpu.roll(a, turn, 0), 1.0)
        b_far = jnp.where(reached, pltpu.roll(b, turn, 0), 0.0)
        b = b + a * b_far
        a = a * a_far
    count = span // 8
    order = range(count - 1, -1, -1) if reverse else range(count)
    edge = 0 if reverse else 7
    a_all, b_all = [None] * count, [None] * count
    p = jnp.ones((1, channels), F32)
    h = jnp.zeros((1, channels), F32)
    for i in order:
        a_i, b_i = a[8 * i : 8 * i + 8], b[8 * i : 8 * i + 8]
        b_all[i] = b_i + a_i * h
        a_all[i] = a_i * p
        p = a_all[i][edge : edge + 1]
        h = b_all[i][edge : edge + 1]
    return jnp.concatenate(a_all, axis=0), jnp.concatenate(b_all, axis=0), p, h


def sequence_marks(scalars, block, row, span, total_len):
    rows = row[1]
    slots = (scalars.shape[0] - 1) // rows
    place = block * span + lax.broadcasted_iota(jnp.int32, (span, 8), 0)
    column = lax.broadcasted_iota(jnp.int32, (span, 8), 1)
    other = place + jnp.where(column <= 3, -column, column - 3)
    here = jnp.full((span, 8), -1, jnp.int32)
    there = jnp.full((span, 8), -1, jnp.int32)
    first = jnp.zeros((span, 8), jnp.int32)
    offset = jnp.int32(0)
    for j in range(slots):
        length = scalars[1 + row[0] * slots + j]
        live = jnp.where(length > 0, 1, 0)
        here = here + jnp.where(place >= offset, live, 0)
        there = there + jnp.where(other >= offset, live, 0)
        first = first + jnp.where(place == offset, live, 0)
        offset = offset + length
    inside = (other >= 0) & (other < total_len)
    same = jnp.where(inside & (here == there), 1, 0)
    return jnp.where(column == 0, first, same).astype(F32)


def forward_kernel(
    rows, step, total_len, scalars, recur, halo, coef, rate_rows, gate_rows, spread, diagonal,
    conv, s_out, q_out, prod, part, ends, marks, rate_w, gate_w, pad,
):
    count, span, channels = recur.shape

    def mark(n, carry):
        block = block_number(scalars, n, rows, step)
        marks[n] = sequence_marks(scalars, block, (n % rows, rows), span, total_len)
        return carry

    lax.fori_loop(0, count, mark, 0)
    for narrow, wide in ((rate_rows, rate_w), (gate_rows, gate_w)):
        wide[...] = (back_project(narrow[...], spread[...]) * diagonal[...].astype(F32)).astype(BF16)

    def convolve(n, carry):
        block = block_number(scalars, n, rows, step)
        before = jnp.bitwise_xor(jnp.maximum(block - 1, 0), scalars[0])
        pad[4:8, :] = halo[before * rows + n % rows]
        pad[8:, :] = recur[n].astype(F32)
        total = coef[4:5, :] + coef[0:1, :] * pad[8:, :]
        for k in range(1, TAPS):
            total = total + coef[k : k + 1, :] * pad[8 - k : 8 - k + span, :] * marks[n][:, k : k + 1]
        conv[n] = total.astype(BF16)
        return carry

    lax.fori_loop(0, count, convolve, 0)
    flat = conv[...].reshape(count * span, channels)
    s_out[...] = project(flat, rate_w[...]).reshape(count, span, channels)
    q_out[...] = project(flat, gate_w[...]).reshape(count, span, channels)

    def scan(n, carry):
        s = jax.nn.sigmoid(s_out[n] + coef[5:6, :])
        q = jax.nn.sigmoid(q_out[n] + coef[6:7, :])
        s_out[n] = s
        q_out[n] = q
        e, m = injection(s, coef[7:8, :])
        decay = e * (1.0 - marks[n][:, 0:1])
        p_all, h_all, p, h = span_scan(decay, m * q * conv[n].astype(F32), False)
        prod[n] = p_all
        part[n] = h_all
        ends[n, 0:1, :] = p
        ends[n, 1:2, :] = h
        return carry

    lax.fori_loop(0, count, scan, 0)


def join(ends, into, scalars, rows, blocks, reverse):
    def lap(k, carry):
        block = blocks - 1 - k if reverse else k
        place = jnp.bitwise_xor(block, scalars[0]) * rows
        new = []
        for r in range(rows):
            into[block * rows + r] = carry[r]
            pair = ends[place + r]
            new.append(pair[0:1] * carry[r] + pair[1:2])
        return tuple(new)

    channels = into.shape[-1]
    lax.fori_loop(0, blocks, lap, (jnp.zeros((1, channels), F32),) * rows)


def state_kernel(rows, step, scalars, prod, part, ends, branch, state, mixed, came, into):
    count = prod.shape[0]
    join(ends, into, scalars, rows, into.shape[0] // rows, False)

    def finish(n, carry):
        incoming = into[block_number(scalars, n, rows, step) * rows + n % rows]
        h = part[n] + prod[n] * incoming
        came[n] = incoming
        state[n] = h
        mixed[n] = (h * gelu_parts(branch[n])[0]).astype(BF16)
        return carry

    lax.fori_loop(0, count, finish, 0)


def adjoint_kernel(
    scalars, grad_mixed, state, branch, s_in, marks, coef, grad_branch, prod, part, ends, pad
):
    count, span, channels = state.shape
    pad[span:, :] = jnp.ones((8, channels), F32)

    def scan(n, carry):
        act, slope = gelu_parts(branch[n])
        grad = grad_mixed[n]
        grad_branch[n] = (grad * state[n] * slope).astype(BF16)
        decay = jnp.exp(-coef[7:8, :] * s_in[n]) * (1.0 - marks[n][:, 0:1])
        pad[:span, :] = decay
        p_all, h_all, p, h = span_scan(pad[1 : span + 1, :], grad * act, True)
        prod[n] = p_all
        part[n] = h_all
        ends[n, 0:1, :] = decay[0:1] * p
        ends[n, 1:2, :] = decay[0:1] * h
        return carry

    lax.fori_loop(0, count, scan, 0)


def gates_kernel(
    rows, step, scalars, prod, part, ends, s_in, q_in, conv, state, came, recur, halo, marks, coef,
    rate_w, gate_w, collect, diagonal, eye, grad_conv, edges, packed, grad_rate, grad_gate, sums,
    into, pad, pad_two,
):
    count, span, channels = prod.shape
    join(ends, into, scalars, rows, into.shape[0] // rows, True)
    sums[...] = jnp.zeros((8, channels), F32)

    def terms(n, carry):
        block = block_number(scalars, n, rows, step)
        total = part[n] + prod[n] * into[block * rows + n % rows]
        pad[7:8, :] = came[n]
        pad[8:, :] = state[n]
        s, q = s_in[n], q_in[n]
        e, m = injection(s, coef[7:8, :])
        c = conv[n].astype(F32)
        first = marks[n][:, 0:1]
        grad_log = total * (pad[7 : 7 + span, :] * e * (1.0 - first) - e * e * q * c / m)
        rate = -coef[7:8, :] * s * (1.0 - s) * grad_log
        gate = total * m * c * q * (1.0 - q)
        grad_conv[n] = total * m * q
        grad_rate[pl.ds(pl.multiple_of(n * span, span), span), :] = rate.astype(BF16)
        grad_gate[pl.ds(pl.multiple_of(n * span, span), span), :] = gate.astype(BF16)
        sums[5:6, :] += jnp.sum(rate, axis=0, keepdims=True)
        sums[6:7, :] += jnp.sum(gate, axis=0, keepdims=True)
        sums[7:8, :] += jnp.sum(coef[8:9, :] * s * grad_log, axis=0, keepdims=True)
        return carry

    lax.fori_loop(0, count, terms, 0)
    through = back_project(grad_rate[...], rate_w[...]) + back_project(grad_gate[...], gate_w[...])
    grad_conv[...] += through.reshape(count, span, channels)
    flat = conv[...].reshape(count * span, channels)

    def kernel_terms(n, carry):
        block = block_number(scalars, n, rows, step)
        before = jnp.bitwise_xor(jnp.maximum(block - 1, 0), scalars[0])
        pad_two[4:8, :] = halo[before * rows + n % rows]
        pad_two[8:, :] = recur[n].astype(F32)
        grad = grad_conv[n]
        edges[n] = grad[:4].astype(BF16)
        sums[4:5, :] += jnp.sum(grad, axis=0, keepdims=True)
        sums[0:1, :] += jnp.sum(grad * pad_two[8:, :], axis=0, keepdims=True)
        for k in range(1, TAPS):
            term = grad * pad_two[8 - k : 8 - k + span, :] * marks[n][:, k : k + 1]
            sums[k : k + 1, :] += jnp.sum(term, axis=0, keepdims=True)
        return carry

    lax.fori_loop(0, count, kernel_terms, 0)
    on = diagonal[...].astype(F32)
    size = collect.shape[1] // 3
    total = back_project((outer(grad_rate[...], flat) * on).astype(BF16), collect[:, :size])
    total += back_project((outer(grad_gate[...], flat) * on).astype(BF16), collect[:, size : 2 * size])
    turned = project(eye[...], sums[...].astype(BF16))
    total += back_project(turned.astype(BF16), collect[:8, 2 * size :])
    packed[...] = total.astype(BF16)


def unconvolve_kernel(rows, step, blocks, scalars, grad_conv, halo, marks, coef, grad_recur, pad):
    count, span, channels = grad_conv.shape

    def body(n, carry):
        block = block_number(scalars, n, rows, step)
        behind = jnp.bitwise_xor(jnp.minimum(block + 1, blocks - 1), scalars[0])
        pad[:span, :] = grad_conv[n]
        pad[span : span + 4, :] = halo[behind * rows + n % rows]
        total = coef[0:1, :] * pad[:span, :]
        for k in range(1, TAPS):
            seen = marks[n][:, 3 + k : 4 + k]
            total = total + coef[k : k + 1, :] * pad[k : k + span, :] * seen
        grad_recur[n] = total.astype(BF16)
        return carry

    lax.fori_loop(0, count, body, 0)


def pack_kernel(taps, bias, rate_bias, gate_bias, decay, gains, rate_w, gate_w, packed):
    count, size = rate_w.shape
    packed[...] = jnp.zeros(packed.shape, F32)
    packed[:count, :size] = rate_w[...].astype(F32)
    packed[:count, size : 2 * size] = gate_w[...].astype(F32)
    first = packed.shape[0] - 16
    packed[first : first + TAPS, :count] = taps[...].astype(F32).T
    for i, row in enumerate((bias, rate_bias, gate_bias, decay)):
        packed[first + TAPS + i : first + TAPS + i + 1, :count] = row[...].astype(F32)
    packed[first + 8 :, : gains.shape[1]] = gains[...].astype(F32)


def lay_kernel(ranks, upper, half, *refs):
    pieces, whole = refs[:-1], refs[-1]
    for i, piece in enumerate(pieces):
        rank = jnp.bitwise_xor(half[0], i // ranks) * ranks + i % ranks
        size = piece.shape[1] // upper
        for u in range(upper):
            start = pl.multiple_of((u * 2 * ranks + rank) * size, 128)
            whole[:, pl.ds(start, size)] = piece[:, u * size : (u + 1) * size].astype(F32)


def feed_forward(tokens, cot, gate_w, up_w, down_w):
    act, slope = gelu_parts(project(tokens, gate_w))
    up_val = project(tokens, up_w)
    hidden = (act * up_val).astype(BF16)
    grad_hidden = back_project(cot, down_w)
    grad_gate = (grad_hidden * up_val * slope).astype(BF16)
    grad_up = (grad_hidden * act).astype(BF16)
    grad = (back_project(grad_gate, gate_w) + back_project(grad_up, up_w)).astype(BF16)
    return grad, hidden, grad_gate, grad_up


def shards(
    block_input,
    seq_lengths,
    mixer_gain,
    branch_weight,
    recur_weight,
    conv_kernel,
    conv_bias,
    recur_gate_weight,
    recur_gate_bias,
    input_gate_weight,
    input_gate_bias,
    decay_param,
    mixer_weight,
    mlp_gain,
    gate_weight,
    up_weight,
    down_weight,
    cotangent,
):
    rows, span, width = block_input.shape
    tokens = rows * span
    seq_count, fsdp_count = lax.axis_size("seq"), lax.axis_size("fsdp")
    device_count = seq_count * fsdp_count
    channel_rows = branch_weight.shape[0]
    hidden_rows = gate_weight.shape[0]
    out_rows = mixer_weight.shape[0]
    block_size = recur_gate_weight.shape[1]
    low, every = device_bits(seq_count, fsdp_count, channel_rows, block_size)
    wide = 4 * low
    tp, tp_wide = (2 * low, low), (wide, 2 * low, low)
    dp = tuple(b for b in every if b not in tp)
    dp_wide = tuple(b for b in every if b not in tp_wide)
    above, below = tuple(b for b in dp if b > low), tuple(b for b in dp if b < low)
    above_wide = tuple(b for b in above if b != wide)
    step = low // fsdp_count
    me = linear_index().astype(jnp.int32)
    seq_index = lax.axis_index("seq")
    tp_index = number_of(me, tp)
    share, share_wide = 1 << len(dp), 1 << len(dp_wide)
    high, deep, high_wide = 1 << len(above), 1 << len(below), 1 << len(above_wide)
    channels = share * channel_rows
    hidden = share_wide * hidden_rows
    blocks = 4 * rows
    seq_dp = tuple(b for b in dp if b >= fsdp_count)
    streams = Streams()

    def across_blocks(own):
        units = sorted(gather_units([own], seq_dp, trade)[0], key=lambda unit: unit[0])
        every_slot = jnp.stack([unit for _, unit in units])
        every_slot = every_slot.reshape((-1, step) + own.shape)
        return jnp.moveaxis(every_slot, 2, 1).reshape((seq_count,) + own.shape[1:])

    def place_rows(units):
        def places(i, at):
            return [(None, 0, number_of(jnp.bitwise_xor(at, units[i][0]), dp))]

        one = units[0][1].shape
        pieces = [unit for _, unit in units]
        (whole,) = assemble(pieces, [(len(units),) + one], places, me, len(units))
        return whole.reshape(-1, one[1])

    def place_columns(units):
        def places(i, at):
            owner = jnp.bitwise_xor(at, units[i][0])
            return [(None, 0, (number_of(owner, above), slice(None), number_of(owner, below)))]

        ranks, one = units[0][1].shape[0], units[0][1].shape[1:]
        pieces = [unit for _, unit in units]
        (whole,) = assemble(pieces, [(high, ranks, deep) + one], places, me, len(units))
        return whole.reshape(-1, one[1])

    def by_rank(weight, upper, ranks):
        split = weight.reshape(weight.shape[0], upper, ranks, -1)
        return jnp.transpose(split, (2, 0, 1, 3)).reshape(ranks, weight.shape[0], -1)

    input_own = block_input.reshape(tokens, width)
    cot_own = cotangent.reshape(tokens, width)
    half = tokens // 2

    def stacked(value, bit, axis, *pins):
        got = fence(trade(value, bit), *pins)
        mine = bit_of(me, bit) == 0
        return jnp.stack([jnp.where(mine, value, got), jnp.where(mine, got, value)], axis=axis), got

    gains = jnp.stack([mixer_gain, mlp_gain])
    for i, b in enumerate(tp):
        gains, gains_got = stacked(gains, b, i)
    packed_width = -(-(2 * block_size + 8) // 128) * 128
    extra = -(-channel_rows // 16) * 16
    small = pl.pallas_call(
        pack_kernel,
        out_shape=jax.ShapeDtypeStruct((extra + 16, packed_width), F32),
        compiler_params=pltpu.CompilerParams(vmem_limit_bytes=VMEM_BYTES),
    )(
        conv_kernel,
        *(v[None] for v in (conv_bias, recur_gate_bias, input_gate_bias, decay_param)),
        gains.reshape(8, out_rows),
        recur_gate_weight,
        input_gate_weight,
    ).astype(BF16)
    small_shape = small.shape
    recur_pair = pair_up(recur_weight, above, me, small)
    recur_q = gather_along(recur_pair, below, 1).reshape(channels, width)
    one, two = (trade(fence(input_own, recur_pair), mask) for mask in (low, 2 * low))
    small = fence(small, recur_pair)
    for i, b in enumerate(dp):
        small, small_got = stacked(small, b, i)
        if i == 0:
            first_got = small_got
    three = [trade(two[:half], low), trade(one[half:], 2 * low)]
    piece = exchange(fence(by_rank(mixer_weight, high, 4), recur_pair), step)
    branch_pair = pair_up(fence(branch_weight, first_got), above, me, piece, small_got, *three)
    branch_q = gather_along(branch_pair, below, 1).reshape(channels, width)
    down_piece = exchange(fence(by_rank(down_weight, high_wide, 8), piece), step)
    mixer_pair = pair_up(fence(piece, branch_pair), above, me, down_piece)
    mixer_q = gather_along(mixer_pair, below, 2).reshape(width, channels)
    small = small.reshape((share,) + small_shape)
    gains = small[:, extra + 8 :, :out_rows].reshape(high, deep, 4, 2, out_rows)
    gains = gains.transpose(3, 0, 2, 1, 4).reshape(2, width)
    gain_one, gain_two = gains[0].astype(F32), gains[1].astype(F32)
    numbers = jnp.moveaxis(small[:, extra : extra + 8, :channel_rows], 1, 0)
    numbers = numbers.reshape(TAPS + 4, channels).astype(F32)
    gate_rows = small[:, :channel_rows, : 2 * block_size].reshape(channels, -1)
    input_all = place_tokens([input_own, one, two, *three], low, me)
    cot_near_list = share_direct(fence(cot_own, three[0]), low)

    coef = numbers
    decay_vec = coef[7:]
    coef = jnp.concatenate(
        [
            coef[:7],
            DECAY_SCALE * jax.nn.softplus(-decay_vec),
            DECAY_SCALE * jax.nn.sigmoid(-decay_vec),
            jnp.zeros((7, channels), F32),
        ]
    )
    rate_rows, gate_rows = gate_rows[:, :block_size], gate_rows[:, block_size:]
    number = np.arange(channels)
    spread = jnp.asarray(number[None] % block_size == np.arange(block_size)[:, None], BF16)
    diagonal = jnp.asarray(number[None] // block_size == number[:, None] // block_size, BF16)
    eye = jnp.asarray(np.eye(channels), BF16)
    collect = np.zeros((channels, 3, packed_width))
    collect[number, 0, number % block_size] = 1
    collect[number, 1, block_size + number % block_size] = 1
    collect[np.arange(8), 2, 2 * block_size + np.arange(8)] = 1
    collect = jnp.asarray(collect.reshape(channels, -1), BF16)
    lengths = lax.dynamic_slice_in_dim(seq_lengths, lax.axis_index("fsdp") * rows, rows, 0)
    base = seq_index.astype(jnp.int32) - tp_index * step
    scalars = jnp.concatenate([base[None], lengths.reshape(-1)])

    def join_ranks(parts, upper):
        got = exchange(parts, step)
        got = got.reshape(got.shape[:2] + (upper, -1))
        return jnp.transpose(got, (1, 2, 0, 3)).reshape(got.shape[1], -1).astype(F32)

    scale_one = inverse_rms(input_all.astype(F32))
    normed = (input_all.astype(F32) * scale_one * gain_one).astype(BF16)
    recur_in = project(normed, recur_q).astype(BF16)
    edge = recur_in.reshape(blocks, span, channels)[:, span - 4 :].reshape(4, rows, 4, channels)
    halo = across_blocks(edge)
    cot_far = trade(fence(cot_own, halo), wide)
    halo = halo.astype(F32).reshape(seq_count * rows, 4, channels)
    recur_in = recur_in.reshape(blocks, span, channels)
    shape = (blocks, span, channels)
    one = (blocks, 1, channels)
    everything = (seq_count * rows, 1, channels)
    square = (channels, channels)
    padded = (span + 8, channels)
    conv, s_val, q_val, prod, part, ends, marks, rate_wide, gate_wide = call(
        functools.partial(forward_kernel, rows, step, seq_count * span),
        [(shape, BF16)] + [(shape, F32)] * 4
        + [((blocks, 2, channels), F32), ((blocks, span, 8), F32), (square, BF16), (square, BF16)],
        scalars,
        [recur_in, halo, coef, rate_rows, gate_rows, spread, diagonal],
        [pltpu.VMEM(padded, F32)],
        4,
    )
    ends_all = across_blocks(ends.reshape(4, rows, 2, channels)).reshape(-1, 2, channels)
    branch = project(normed, fence(branch_q, ends, *cot_near_list[1:], cot_far))
    branch = branch.reshape(blocks, span, channels)
    ends = fence(ends_all, branch)
    state, mixed, came = call(
        functools.partial(state_kernel, rows, step),
        [(shape, F32), (shape, BF16), (one, F32)],
        scalars,
        [prod, part, ends, branch],
        [pltpu.VMEM(everything, F32)],
        2,
    )
    gate_pair, up_pair, down_pair = (
        pair_up(fence(weight, mixer_pair), above_wide, me)
        for weight in (gate_weight, up_weight, down_piece)
    )
    gate_q = gather_along(gate_pair, below, 1).reshape(hidden, width)
    up_q = gather_along(up_pair, below, 1).reshape(hidden, width)
    down_q = gather_along(down_pair, below, 2).reshape(width, hidden)
    mixed_flat = mixed.reshape(4 * tokens, channels)
    cot_near = place_tokens(fence_all(cot_near_list, mixed), low, me)
    mixer_part = project(mixed_flat, mixer_q).astype(BF16).reshape(4, tokens, width)
    cot_far_list = share_direct(fence(cot_far, mixer_part), low)
    mixer_parts = fence(exchange(mixer_part, step), *cot_far_list[1:])
    residual = input_own.astype(F32) + jnp.sum(mixer_parts.astype(F32), axis=0)


    scale_two = inverse_rms(residual)
    unit_two = residual * scale_two
    normed_own = (unit_two * gain_two).astype(BF16)
    normed_far = trade(normed_own, wide)
    near_list = share_direct(normed_own, low)
    far_list = share_direct(normed_far, low)
    near = place_tokens(near_list, low, me)
    cot_far = place_tokens(fence_all(cot_far_list, normed_own), low, me)
    near_out = feed_forward(near, cot_near, gate_q, up_q, down_q)
    ranks_shape = (4, tokens, width)
    far = place_tokens(fence_all(far_list, near_out[0]), low, me)
    far_out = feed_forward(far, cot_far, gate_q, up_q, down_q)
    grad_far_parts = exchange(far_out[0].reshape(ranks_shape), step)

    def finish(partial, bits):
        partial = partial.reshape((2,) * len(bits) + partial.shape[1:])
        grad = Reduction(partial, range(len(bits)), bits, me)
        if bits:
            grad.send_to(0)
        return grad.total()

    def both(one, two, k):
        return outer(one[k], near) + outer(two[k], far)

    down_grad = outer(cot_near, near_out[1]) + outer(cot_far, far_out[1])
    down_grad = down_grad.astype(BF16).reshape(high_wide, 8, -1, hidden)
    grad_far_parts = fence(grad_far_parts, down_grad)
    down_grad = finish(scatter_along(down_grad, below, 2), above_wide).reshape(8, out_rows, hidden)
    grad_two_far = jnp.sum(grad_far_parts.astype(F32), axis=0).astype(BF16)
    grad_near_parts = exchange(fence(near_out[0], grad_two_far).reshape(ranks_shape), step)
    grad_two_near = jnp.sum(grad_near_parts.astype(F32), axis=0)
    grad_two = grad_two_near + trade(grad_two_far, wide).astype(F32)
    scaled = grad_two * gain_two
    grad_residual = cot_own.astype(F32) + scale_two * (
        scaled - unit_two * jnp.mean(scaled * unit_two, axis=-1, keepdims=True)
    )
    gain_two_part = jnp.sum(grad_two * unit_two, axis=0)

    grad_mix_own = grad_residual.astype(BF16)
    grad_mix_list = share_list(grad_mix_own, low)
    down_far = project(fence(far_out[1], grad_mix_own), down_q).astype(BF16)
    late = [fence_all(out[2:], grad_mix_own) for out in (near_out, far_out)]
    gate_grad = both(*late, 0).astype(BF16).reshape(high_wide, -1, width)
    up_grad = both(*late, 1).astype(BF16).reshape(high_wide, -1, width)
    down_far_parts = exchange(fence(down_far, *grad_mix_list[1:3]).reshape(ranks_shape), step)
    down_parts = fence(down_grad, grad_mix_own).reshape(2, 4, out_rows, hidden)
    down_sent, down_kept = halves(down_parts, 0, wide, me)
    down_got = trade(down_sent, wide)
    grad_mix = place_tokens(fence_all(grad_mix_list, down_got, gate_grad, up_grad, down_far), low, me)
    gate_grad = finish(scatter_along(gate_grad, below, 1), above_wide)
    up_grad = finish(scatter_along(up_grad, below, 1), above_wide)
    grad_mixed = back_project(grad_mix, mixer_q).reshape(shape)
    grad_branch, prod_back, part_back, own_ends = call(
        adjoint_kernel,
        [(shape, BF16), (shape, F32), (shape, F32), ((blocks, 2, channels), F32)],
        scalars,
        [grad_mixed, state, branch, s_val, marks, coef],
        [pltpu.VMEM(padded, F32)],
        3,
    )
    ends_back = across_blocks(own_ends.reshape(4, rows, 2, channels)).reshape(-1, 2, channels)
    grad_branch = grad_branch.reshape(4 * tokens, channels)
    mixer_grad = outer(fence(grad_mix, own_ends), mixed_flat).astype(BF16)
    mixer_grad = mixer_grad.reshape(high, 4, -1, channels)
    down_far = jnp.sum(fence(down_far_parts, own_ends).astype(F32), axis=0).astype(BF16)
    ends_back = fence(ends_back, mixer_grad, down_far)
    mixer_grad = scatter_along(mixer_grad, below, 2)
    down_far_own = trade(down_far, wide)
    packed_shape = (channels, packed_width)
    grad_conv, edge_back, packed = call(
        functools.partial(gates_kernel, rows, step),
        [(shape, F32), ((blocks, 4, channels), BF16), (packed_shape, BF16)],
        scalars,
        [
            prod_back, part_back, ends_back, s_val, q_val, conv, state, came, recur_in, halo,
            marks, coef, rate_wide, gate_wide, collect, diagonal, eye,
        ],
        [
            pltpu.VMEM((4 * tokens, channels), BF16),
            pltpu.VMEM((4 * tokens, channels), BF16),
            pltpu.VMEM((8, channels), F32),
            pltpu.VMEM(everything, F32),
            pltpu.VMEM(padded, F32),
            pltpu.VMEM(padded, F32),
        ],
        4,
    )
    edge_back = edge_back.reshape(4, rows, 4, channels)
    down_near = project(fence(near_out[1], own_ends), down_q).astype(BF16).reshape(ranks_shape)
    down_near = fence(down_near, edge_back)
    down_near = [pick(down_near, jnp.bitwise_xor(tp_index, j), 0) for j in range(4)]
    down_near[1:] = [trade(down_near[j], j * low) for j in (1, 2, 3)]
    halo_back = across_blocks(edge_back)
    last = len(dp)
    branch_grad = outer(fence(grad_branch, edge_back), normed).astype(BF16).reshape(high, -1, width)
    halo_back = fence(halo_back, down_far_own, branch_grad)
    branch_grad = scatter_along(branch_grad, below, 1)
    halo_back = halo_back.astype(F32).reshape(seq_count * rows, 4, channels)
    (grad_recur,) = call(
        functools.partial(unconvolve_kernel, rows, step, seq_count),
        [(shape, BF16)],
        scalars,
        [grad_conv, halo_back, marks, coef],
        [pltpu.VMEM(padded, F32)],
        4,
    )
    grad_recur = grad_recur.reshape(4 * tokens, channels)
    recur_grad = reduce_rows(outer(grad_recur, normed), dp, me)
    grad_recur = fence(grad_recur, recur_grad.send())
    grad_normed_part = back_project(grad_branch, branch_q) + back_project(grad_recur, recur_q)
    grad_normed_sent = grad_normed_part.astype(BF16)
    recur_sent = recur_grad.send_to(last - 2, grad_normed_sent)
    packed = reduce_rows(fence(packed, grad_recur), dp, me)
    grad_normed_sent = fence(grad_normed_sent, recur_sent, packed.send())
    gain_one_part = jnp.sum(grad_normed_sent.astype(F32) * input_all.astype(F32) * scale_one, axis=0)
    grad_normed = sum_tokens(grad_normed_sent.reshape(ranks_shape), step)
    own_scale = inverse_rms(input_own.astype(F32))
    unit_one = input_own.astype(F32) * own_scale
    scaled_one = grad_normed * gain_one
    input_grad = (
        grad_residual
        + own_scale
        * (scaled_one - unit_one * jnp.mean(scaled_one * unit_one, axis=-1, keepdims=True))
    ).astype(BF16)
    def halve(partial):
        partial = fence(partial, grad_normed).reshape((2,) * len(above) + partial.shape[1:])
        return Reduction(partial, range(len(above)), above, me)

    mixer_grad, branch_grad = halve(mixer_grad), halve(branch_grad)
    mixer_sent = mixer_grad.send_to(0)
    recur_sent = recur_grad.send_to(0, grad_normed, mixer_sent)
    sent = branch_grad.send_to(0, recur_sent)
    packed_sent = packed.send_to(0, sent)
    pair = jnp.stack([fence(part, packed_sent) for part in (down_kept, down_got)], axis=1)
    pair = exchange(pair, step)
    own_half = number_of(me, (wide,))
    flat_pieces = [pair[j, h] for h in range(2) for j in range(4)]
    down_weight_grad = pl.pallas_call(
        functools.partial(lay_kernel, 4, high_wide),
        out_shape=jax.ShapeDtypeStruct((out_rows, 8 * hidden), F32),
        in_specs=[pl.BlockSpec(memory_space=pltpu.SMEM)]
        + [pl.BlockSpec(memory_space=pltpu.VMEM)] * len(flat_pieces),
        out_specs=pl.BlockSpec(memory_space=pltpu.VMEM),
        compiler_params=pltpu.CompilerParams(vmem_limit_bytes=VMEM_BYTES),
    )(own_half.reshape(1), *flat_pieces)
    mixer_rows = mixer_grad.total(sent).astype(BF16).reshape(4, out_rows, channels)
    mixer_weight_grad = join_ranks(mixer_rows, high)
    down_sum = sum(fence(part, mixer_rows).astype(F32) for part in down_near + [down_far_own])
    block_output = (residual + down_sum).astype(BF16)
    recur_weight_grad = recur_grad.total(mixer_rows)
    branch_weight_grad = branch_grad.total(recur_weight_grad)
    packed = packed.total(recur_weight_grad)

    gain_parts = jnp.stack([gain_one_part, gain_two_part]).astype(BF16)
    gain_parts = jnp.moveaxis(gain_parts.reshape(2, device_count, out_rows), 1, 0)
    gain_parts = lax.all_to_all(fence(gain_parts, sent), AXES, 0, 0, tiled=True)
    gain_grads = jnp.sum(gain_parts.astype(F32), axis=0)
    numbers = packed[:, 2 * block_size : 2 * block_size + 8]
    return (
        block_output.reshape(rows, span, width),
        input_grad.reshape(rows, span, width),
        gain_grads[0],
        branch_weight_grad,
        recur_weight_grad,
        numbers[:, :TAPS],
        numbers[:, 4],
        packed[:, :block_size],
        numbers[:, 5],
        packed[:, block_size : 2 * block_size],
        numbers[:, 6],
        numbers[:, 7],
        mixer_weight_grad,
        gain_grads[1],
        gate_grad.reshape(hidden_rows, width).astype(F32),
        up_grad.reshape(hidden_rows, width).astype(F32),
        down_weight_grad,
    )


def solution(mesh):
    tokens, spread, table = P("fsdp", "seq", None), P(AXES), P(AXES, None)
    in_specs = (
        tokens, P(), spread, table, table, table, spread, table, spread, table, spread, spread,
        table, spread, table, table, table, tokens,
    )
    out_specs = (
        tokens, tokens, spread, table, table, table, spread, table, spread, table, spread, spread,
        table, spread, table, table, table,
    )
    return jax.shard_map(shards, mesh=mesh, in_specs=in_specs, out_specs=out_specs, check_vma=False)
```

```python
import functools
import math

import jax
import jax.numpy as jnp
import numpy as np
from jax import lax
from jax.experimental import pallas as pl
from jax.experimental.pallas import tpu as pltpu
from jax.sharding import PartitionSpec as P

AXES = ("seq", "fsdp")
TAPS = 4
EPSILON = 1e-06
DECAY_SCALE = 8.0
VMEM_BYTES = 56 * 1024 * 1024
BF16 = jnp.bfloat16
F32 = jnp.float32


def device_bits(seq_count, fsdp_count, rows, block):
    low = fsdp_count
    while low * rows < block:
        low *= 2
    total = seq_count * fsdp_count
    every = [1 << k for k in reversed(range(total.bit_length() - 1))]
    return low, tuple(every)


def linear_index():
    return lax.axis_index("seq") * lax.axis_size("fsdp") + lax.axis_index("fsdp")


def bit_of(index, bit):
    return lax.rem(lax.div(index, jnp.int32(bit)), jnp.int32(2))


def number_of(index, bits):
    value = jnp.int32(0)
    for b in bits:
        value = value * 2 + bit_of(index, b)
    return value


def fence(value, *others):
    return lax.optimization_barrier((value,) + others)[0]


def fence_all(values, *others):
    return list(lax.optimization_barrier(tuple(values) + others)[: len(values)])


def trade(value, mask):
    count = lax.axis_size("seq") * lax.axis_size("fsdp")
    return lax.ppermute(value, AXES, [(i, i ^ mask) for i in range(count)])


class Streams:
    def __init__(self):
        self.last = {}

    def trade(self, value, bit):
        if bit > 1:
            if bit in self.last:
                value = fence(value, self.last[bit])
            self.last[bit] = value = trade(value, bit)
            return value
        return trade(value, bit)


def pick(value, index, axis):
    return lax.dynamic_index_in_dim(value, index, axis, keepdims=False)


def put(buffer, part, index, axis):
    return lax.dynamic_update_index_in_dim(buffer, part, index, axis)


def gather_units(owns, bits, send):
    lists = [[(0, own)] for own in owns]
    for b in bits:
        fresh = [[] for _ in owns]
        for k in range(len(lists[0])):
            for units, new in zip(lists, fresh):
                mask, unit = units[k]
                new.append((mask | b, send(unit, b)))
        lists = [units + new for units, new in zip(lists, fresh)]
    return lists


def expand(units, bits):
    for b in bits:
        units = units + [(mask | b, trade(unit, b)) for mask, unit in units]
    return units


def pin_units(units, *others):
    return list(zip([mask for mask, _ in units], fence_all([unit for _, unit in units], *others)))


def copy_kernel(count, shapes, places, scalars, *refs):
    pieces, wholes, sems = refs[:count], refs[count:-1], refs[-1]
    copies = []
    for i, piece in enumerate(pieces):
        for source, which, target in places(i, scalars[0]):
            here = piece if source is None else piece.at[source]
            copies.append(
                pltpu.make_async_copy(here, wholes[which].at[target], sems.at[len(copies)])
            )
    for c in copies:
        c.start()
    for c in copies:
        c.wait()


def assemble(pieces, shapes, places, me, copies):
    where = pl.BlockSpec(memory_space=pl.ANY)
    return pl.pallas_call(
        functools.partial(copy_kernel, len(pieces), shapes, places),
        out_shape=[jax.ShapeDtypeStruct(shape, pieces[0].dtype) for shape in shapes],
        in_specs=[pl.BlockSpec(memory_space=pltpu.SMEM)] + [where] * len(pieces),
        out_specs=[pl.BlockSpec(memory_space=pltpu.VMEM)] * len(shapes),
        scratch_shapes=[pltpu.SemaphoreType.DMA((copies,))],
        compiler_params=pltpu.CompilerParams(vmem_limit_bytes=VMEM_BYTES),
        cost_estimate=pl.CostEstimate(
            flops=0, bytes_accessed=4 * sum(piece.size for piece in pieces), transcendentals=0
        ),
    )(me.astype(jnp.int32).reshape(1), *pieces)


def halves(value, axis, bit, me):
    mine = bit_of(me, bit)
    return pick(value, 1 - mine, axis), pick(value, mine, axis)


class Reduction:
    def __init__(self, value, axes, bits, me):
        self.kept, self.got, self.me = value, None, me
        self.left = list(zip(axes, bits))

    def send(self, *after):
        value = self.total(*after).astype(BF16)
        axis, bit = self.left.pop()
        away, self.kept = halves(value, axis, bit, self.me)
        self.got = trade(away, bit)
        return away

    def send_to(self, count, *after):
        while len(self.left) > count:
            away = self.send(*after)
        return away

    def total(self, *after):
        if self.got is None:
            return self.kept
        return self.kept.astype(F32) + fence(self.got, *after).astype(F32)


def reduce_rows(whole, bits, me):
    whole = whole.astype(BF16).reshape((2,) * len(bits) + (whole.shape[0] >> len(bits), -1))
    return Reduction(whole, range(len(bits)), bits, me)


def reduce_columns(whole, bits, ranks, low, me):
    above = sum(b > low for b in bits)
    split = (2,) * above + (ranks,) + (2,) * (len(bits) - above)
    rows = whole.shape[0] // (ranks << len(bits))
    whole = whole.astype(BF16).reshape(split + (rows, whole.shape[1]))
    return Reduction(whole, [k if b > low else k + 1 for k, b in enumerate(bits)], bits, me)


def share_list(own, low):
    half = own.shape[-2] // 2
    one, two = trade(own, low), trade(own, 2 * low)
    three = (trade(two[..., :half, :], low), trade(one[..., half:, :], 2 * low))
    return [own, one, two, *three]


def share_direct(own, low):
    return [own] + [trade(own, j * low) for j in (1, 2, 3)]


def place_tokens(units, low, me):
    rows, width = units[0].shape
    pieces = list(units)

    def places(i, at):
        slot = jnp.bitwise_xor(number_of(at, (2 * low, low)), min(i, 3))
        start = pl.multiple_of(slot * rows + (rows // 2 if i == 4 else 0), rows // 2)
        return [(None, 0, pl.ds(start, pieces[i].shape[0]))]

    (whole,) = assemble(pieces, [(4 * rows, width)], places, me, len(pieces))
    return whole


def groups_of(bits, count):
    inside = [0]
    for b in bits:
        inside = [i | k for i in inside for k in (0, b)]
    return [[first | i for i in inside] for first in range(count) if not first & sum(bits)]


def line_of(bits):
    fsdp_count, count = lax.axis_size("fsdp"), lax.axis_size("seq") * lax.axis_size("fsdp")
    if sum(bits) == fsdp_count - 1:
        return {"axis_name": "fsdp"}
    if sum(bits) == count - fsdp_count:
        return {"axis_name": "seq"}
    if sum(bits) == count - 1:
        return {"axis_name": AXES}
    return {"axis_name": AXES, "axis_index_groups": groups_of(bits, count)}


def gather_along(own, bits, axis):
    return lax.all_gather(own, axis=axis, tiled=True, **line_of(bits))


def scatter_along(partial, bits, axis):
    return lax.psum_scatter(partial, scatter_dimension=axis, tiled=True, **line_of(bits))


def pair_up(own, bits, me, *pins):
    value = own
    for i, b in enumerate(bits):
        got = fence(trade(value, b), *pins)
        mine = bit_of(me, b) == 0
        value = jnp.stack([jnp.where(mine, value, got), jnp.where(mine, got, value)], axis=i)
    return value.reshape((1 << len(bits),) + own.shape)


def exchange(parts, step):
    ranks, count = parts.shape[0], lax.axis_size("seq")
    inside = [r * step for r in range(ranks)]
    groups = [[b + i for i in inside] for b in range(count) if not b & ((ranks - 1) * step)]
    return lax.all_to_all(parts, "seq", 0, 0, axis_index_groups=groups, tiled=True)


def sum_tokens(partial, step):
    return jnp.sum(exchange(partial, step).astype(F32), axis=0)


def project(left, weight):
    return lax.dot_general(left, weight, (((1,), (1,)), ((), ())), preferred_element_type=F32)


def back_project(left, weight):
    return lax.dot_general(left, weight, (((1,), (0,)), ((), ())), preferred_element_type=F32)


def outer(grads, values):
    return lax.dot_general(grads, values, (((0,), (0,)), ((), ())), preferred_element_type=F32)


def inverse_rms(values):
    return lax.rsqrt(jnp.mean(values * values, axis=-1, keepdims=True) + EPSILON)


def gelu_parts(v):
    c = 0.7978845608028654
    t = jnp.tanh(c * (v + 0.044715 * v * v * v))
    act = 0.5 * v * (1.0 + t)
    slope = 0.5 * (1.0 + t) + 0.5 * v * (1.0 - t * t) * c * (1.0 + 3 * 0.044715 * v * v)
    return act, slope


def call(body, outs, scalars, arrays, scratch=(), passes=1):
    sizes = [array.size * array.dtype.itemsize for array in arrays]
    sizes += [math.prod(shape) * jnp.dtype(kind).itemsize for shape, kind in outs]
    return pl.pallas_call(
        body,
        out_shape=[jax.ShapeDtypeStruct(shape, kind) for shape, kind in outs],
        in_specs=[pl.BlockSpec(memory_space=pltpu.SMEM)]
        + [pl.BlockSpec(memory_space=pltpu.VMEM)] * len(arrays),
        out_specs=[pl.BlockSpec(memory_space=pltpu.VMEM)] * len(outs),
        scratch_shapes=list(scratch),
        compiler_params=pltpu.CompilerParams(vmem_limit_bytes=VMEM_BYTES),
        cost_estimate=pl.CostEstimate(
            flops=0, bytes_accessed=passes * sum(sizes), transcendentals=0
        ),
    )(scalars, *arrays)


def block_number(scalars, n, rows, step):
    return jnp.bitwise_xor(scalars[0], (n // rows) * step)


def injection(s, speed):
    y = speed * s
    e = jnp.exp(-y)
    z = 2.0 * y
    series = 1.0 - z * (1 / 7)
    for k in (6, 5, 4, 3, 2):
        series = 1.0 - z * (1 / k) * series
    return e, jnp.sqrt(jnp.where(z < 0.35, z * series, 1.0 - e * e))


def span_scan(a, b, reverse):
    span, channels = a.shape
    within = lax.broadcasted_iota(jnp.int32, (span, channels), 0) % 8
    for k in (1, 2, 4):
        turn = span - k if reverse else k
        reached = within < 8 - k if reverse else within >= k
        a_far = jnp.where(reached, pltpu.roll(a, turn, 0), 1.0)
        b_far = jnp.where(reached, pltpu.roll(b, turn, 0), 0.0)
        b = b + a * b_far
        a = a * a_far
    count = span // 8
    order = range(count - 1, -1, -1) if reverse else range(count)
    edge = 0 if reverse else 7
    a_all, b_all = [None] * count, [None] * count
    p = jnp.ones((1, channels), F32)
    h = jnp.zeros((1, channels), F32)
    for i in order:
        a_i, b_i = a[8 * i : 8 * i + 8], b[8 * i : 8 * i + 8]
        b_all[i] = b_i + a_i * h
        a_all[i] = a_i * p
        p = a_all[i][edge : edge + 1]
        h = b_all[i][edge : edge + 1]
    return jnp.concatenate(a_all, axis=0), jnp.concatenate(b_all, axis=0), p, h


def sequence_marks(scalars, block, row, span, total_len):
    rows = row[1]
    slots = (scalars.shape[0] - 1) // rows
    place = block * span + lax.broadcasted_iota(jnp.int32, (span, 8), 0)
    column = lax.broadcasted_iota(jnp.int32, (span, 8), 1)
    other = place + jnp.where(column <= 3, -column, column - 3)
    here = jnp.full((span, 8), -1, jnp.int32)
    there = jnp.full((span, 8), -1, jnp.int32)
    first = jnp.zeros((span, 8), jnp.int32)
    offset = jnp.int32(0)
    for j in range(slots):
        length = scalars[1 + row[0] * slots + j]
        live = jnp.where(length > 0, 1, 0)
        here = here + jnp.where(place >= offset, live, 0)
        there = there + jnp.where(other >= offset, live, 0)
        first = first + jnp.where(place == offset, live, 0)
        offset = offset + length
    inside = (other >= 0) & (other < total_len)
    same = jnp.where(inside & (here == there), 1, 0)
    return jnp.where(column == 0, first, same).astype(F32)


def forward_kernel(
    rows, step, total_len, scalars, recur, halo, coef, rate_rows, gate_rows, spread, diagonal,
    conv, s_out, q_out, prod, part, ends, marks, rate_w, gate_w, pad,
):
    count, span, channels = recur.shape

    def mark(n, carry):
        block = block_number(scalars, n, rows, step)
        marks[n] = sequence_marks(scalars, block, (n % rows, rows), span, total_len)
        return carry

    lax.fori_loop(0, count, mark, 0)
    for narrow, wide in ((rate_rows, rate_w), (gate_rows, gate_w)):
        wide[...] = (back_project(narrow[...], spread[...]) * diagonal[...].astype(F32)).astype(BF16)

    def convolve(n, carry):
        block = block_number(scalars, n, rows, step)
        before = jnp.bitwise_xor(jnp.maximum(block - 1, 0), scalars[0])
        pad[4:8, :] = halo[before * rows + n % rows]
        pad[8:, :] = recur[n].astype(F32)
        total = coef[4:5, :] + coef[0:1, :] * pad[8:, :]
        for k in range(1, TAPS):
            total = total + coef[k : k + 1, :] * pad[8 - k : 8 - k + span, :] * marks[n][:, k : k + 1]
        conv[n] = total.astype(BF16)
        return carry

    lax.fori_loop(0, count, convolve, 0)
    flat = conv[...].reshape(count * span, channels)
    s_out[...] = project(flat, rate_w[...]).reshape(count, span, channels)
    q_out[...] = project(flat, gate_w[...]).reshape(count, span, channels)

    def scan(n, carry):
        s = jax.nn.sigmoid(s_out[n] + coef[5:6, :])
        q = jax.nn.sigmoid(q_out[n] + coef[6:7, :])
        s_out[n] = s
        q_out[n] = q
        e, m = injection(s, coef[7:8, :])
        decay = e * (1.0 - marks[n][:, 0:1])
        p_all, h_all, p, h = span_scan(decay, m * q * conv[n].astype(F32), False)
        prod[n] = p_all
        part[n] = h_all
        ends[n, 0:1, :] = p
        ends[n, 1:2, :] = h
        return carry

    lax.fori_loop(0, count, scan, 0)


def join(ends, into, scalars, rows, blocks, reverse):
    def lap(k, carry):
        block = blocks - 1 - k if reverse else k
        place = jnp.bitwise_xor(block, scalars[0]) * rows
        new = []
        for r in range(rows):
            into[block * rows + r] = carry[r]
            pair = ends[place + r]
            new.append(pair[0:1] * carry[r] + pair[1:2])
        return tuple(new)

    channels = into.shape[-1]
    lax.fori_loop(0, blocks, lap, (jnp.zeros((1, channels), F32),) * rows)


def state_kernel(rows, step, scalars, prod, part, ends, branch, state, mixed, came, into):
    count = prod.shape[0]
    join(ends, into, scalars, rows, into.shape[0] // rows, False)

    def finish(n, carry):
        incoming = into[block_number(scalars, n, rows, step) * rows + n % rows]
        h = part[n] + prod[n] * incoming
        came[n] = incoming
        state[n] = h
        mixed[n] = (h * gelu_parts(branch[n])[0]).astype(BF16)
        return carry

    lax.fori_loop(0, count, finish, 0)


def adjoint_kernel(
    scalars, grad_mixed, state, branch, s_in, marks, coef, grad_branch, prod, part, ends, pad
):
    count, span, channels = state.shape
    pad[span:, :] = jnp.ones((8, channels), F32)

    def scan(n, carry):
        act, slope = gelu_parts(branch[n])
        grad = grad_mixed[n]
        grad_branch[n] = (grad * state[n] * slope).astype(BF16)
        decay = jnp.exp(-coef[7:8, :] * s_in[n]) * (1.0 - marks[n][:, 0:1])
        pad[:span, :] = decay
        p_all, h_all, p, h = span_scan(pad[1 : span + 1, :], grad * act, True)
        prod[n] = p_all
        part[n] = h_all
        ends[n, 0:1, :] = decay[0:1] * p
        ends[n, 1:2, :] = decay[0:1] * h
        return carry

    lax.fori_loop(0, count, scan, 0)


def gates_kernel(
    rows, step, scalars, prod, part, ends, s_in, q_in, conv, state, came, recur, halo, marks, coef,
    rate_w, gate_w, collect, diagonal, eye, grad_conv, edges, packed, grad_rate, grad_gate, sums,
    into, pad, pad_two,
):
    count, span, channels = prod.shape
    join(ends, into, scalars, rows, into.shape[0] // rows, True)
    sums[...] = jnp.zeros((8, channels), F32)

    def terms(n, carry):
        block = block_number(scalars, n, rows, step)
        total = part[n] + prod[n] * into[block * rows + n % rows]
        pad[7:8, :] = came[n]
        pad[8:, :] = state[n]
        s, q = s_in[n], q_in[n]
        e, m = injection(s, coef[7:8, :])
        c = conv[n].astype(F32)
        first = marks[n][:, 0:1]
        grad_log = total * (pad[7 : 7 + span, :] * e * (1.0 - first) - e * e * q * c / m)
        rate = -coef[7:8, :] * s * (1.0 - s) * grad_log
        gate = total * m * c * q * (1.0 - q)
        grad_conv[n] = total * m * q
        grad_rate[pl.ds(pl.multiple_of(n * span, span), span), :] = rate.astype(BF16)
        grad_gate[pl.ds(pl.multiple_of(n * span, span), span), :] = gate.astype(BF16)
        sums[5:6, :] += jnp.sum(rate, axis=0, keepdims=True)
        sums[6:7, :] += jnp.sum(gate, axis=0, keepdims=True)
        sums[7:8, :] += jnp.sum(coef[8:9, :] * s * grad_log, axis=0, keepdims=True)
        return carry

    lax.fori_loop(0, count, terms, 0)
    through = back_project(grad_rate[...], rate_w[...]) + back_project(grad_gate[...], gate_w[...])
    grad_conv[...] += through.reshape(count, span, channels)
    flat = conv[...].reshape(count * span, channels)

    def kernel_terms(n, carry):
        block = block_number(scalars, n, rows, step)
        before = jnp.bitwise_xor(jnp.maximum(block - 1, 0), scalars[0])
        pad_two[4:8, :] = halo[before * rows + n % rows]
        pad_two[8:, :] = recur[n].astype(F32)
        grad = grad_conv[n]
        edges[n] = grad[:4].astype(BF16)
        sums[4:5, :] += jnp.sum(grad, axis=0, keepdims=True)
        sums[0:1, :] += jnp.sum(grad * pad_two[8:, :], axis=0, keepdims=True)
        for k in range(1, TAPS):
            term = grad * pad_two[8 - k : 8 - k + span, :] * marks[n][:, k : k + 1]
            sums[k : k + 1, :] += jnp.sum(term, axis=0, keepdims=True)
        return carry

    lax.fori_loop(0, count, kernel_terms, 0)
    on = diagonal[...].astype(F32)
    size = collect.shape[1] // 3
    total = back_project((outer(grad_rate[...], flat) * on).astype(BF16), collect[:, :size])
    total += back_project((outer(grad_gate[...], flat) * on).astype(BF16), collect[:, size : 2 * size])
    turned = project(eye[...], sums[...].astype(BF16))
    total += back_project(turned.astype(BF16), collect[:8, 2 * size :])
    packed[...] = total.astype(BF16)


def unconvolve_kernel(rows, step, blocks, scalars, grad_conv, halo, marks, coef, grad_recur, pad):
    count, span, channels = grad_conv.shape

    def body(n, carry):
        block = block_number(scalars, n, rows, step)
        behind = jnp.bitwise_xor(jnp.minimum(block + 1, blocks - 1), scalars[0])
        pad[:span, :] = grad_conv[n]
        pad[span : span + 4, :] = halo[behind * rows + n % rows]
        total = coef[0:1, :] * pad[:span, :]
        for k in range(1, TAPS):
            seen = marks[n][:, 3 + k : 4 + k]
            total = total + coef[k : k + 1, :] * pad[k : k + span, :] * seen
        grad_recur[n] = total.astype(BF16)
        return carry

    lax.fori_loop(0, count, body, 0)


def pack_kernel(taps, bias, rate_bias, gate_bias, decay, gains, rate_w, gate_w, packed):
    count, size = rate_w.shape
    packed[...] = jnp.zeros(packed.shape, F32)
    packed[:count, :size] = rate_w[...].astype(F32)
    packed[:count, size : 2 * size] = gate_w[...].astype(F32)
    first = packed.shape[0] - 16
    packed[first : first + TAPS, :count] = taps[...].astype(F32).T
    for i, row in enumerate((bias, rate_bias, gate_bias, decay)):
        packed[first + TAPS + i : first + TAPS + i + 1, :count] = row[...].astype(F32)
    packed[first + 8 :, : gains.shape[1]] = gains[...].astype(F32)


def lay_kernel(ranks, upper, half, *refs):
    pieces, whole = refs[:-1], refs[-1]
    for i, piece in enumerate(pieces):
        rank = jnp.bitwise_xor(half[0], i // ranks) * ranks + i % ranks
        size = piece.shape[1] // upper
        for u in range(upper):
            start = pl.multiple_of((u * 2 * ranks + rank) * size, 128)
            whole[:, pl.ds(start, size)] = piece[:, u * size : (u + 1) * size].astype(F32)


def feed_forward(tokens, cot, gate_w, up_w, down_w):
    act, slope = gelu_parts(project(tokens, gate_w))
    up_val = project(tokens, up_w)
    hidden = (act * up_val).astype(BF16)
    grad_hidden = back_project(cot, down_w)
    grad_gate = (grad_hidden * up_val * slope).astype(BF16)
    grad_up = (grad_hidden * act).astype(BF16)
    grad = (back_project(grad_gate, gate_w) + back_project(grad_up, up_w)).astype(BF16)
    return grad, hidden, grad_gate, grad_up


def shards(
    block_input,
    seq_lengths,
    mixer_gain,
    branch_weight,
    recur_weight,
    conv_kernel,
    conv_bias,
    recur_gate_weight,
    recur_gate_bias,
    input_gate_weight,
    input_gate_bias,
    decay_param,
    mixer_weight,
    mlp_gain,
    gate_weight,
    up_weight,
    down_weight,
    cotangent,
):
    rows, span, width = block_input.shape
    tokens = rows * span
    seq_count, fsdp_count = lax.axis_size("seq"), lax.axis_size("fsdp")
    device_count = seq_count * fsdp_count
    channel_rows = branch_weight.shape[0]
    hidden_rows = gate_weight.shape[0]
    out_rows = mixer_weight.shape[0]
    block_size = recur_gate_weight.shape[1]
    low, every = device_bits(seq_count, fsdp_count, channel_rows, block_size)
    wide = 4 * low
    tp, tp_wide = (2 * low, low), (wide, 2 * low, low)
    dp = tuple(b for b in every if b not in tp)
    dp_wide = tuple(b for b in every if b not in tp_wide)
    above, below = tuple(b for b in dp if b > low), tuple(b for b in dp if b < low)
    above_wide = tuple(b for b in above if b != wide)
    step = low // fsdp_count
    me = linear_index().astype(jnp.int32)
    seq_index = lax.axis_index("seq")
    tp_index = number_of(me, tp)
    share, share_wide = 1 << len(dp), 1 << len(dp_wide)
    high, deep, high_wide = 1 << len(above), 1 << len(below), 1 << len(above_wide)
    channels = share * channel_rows
    hidden = share_wide * hidden_rows
    blocks = 4 * rows
    seq_dp = tuple(b for b in dp if b >= fsdp_count)
    streams = Streams()

    def across_blocks(own):
        units = sorted(gather_units([own], seq_dp, trade)[0], key=lambda unit: unit[0])
        every_slot = jnp.stack([unit for _, unit in units])
        every_slot = every_slot.reshape((-1, step) + own.shape)
        return jnp.moveaxis(every_slot, 2, 1).reshape((seq_count,) + own.shape[1:])

    def place_rows(units, bits):
        def places(i, at):
            return [(None, 0, number_of(jnp.bitwise_xor(at, units[i][0]), bits))]

        one = units[0][1].shape
        pieces = [unit for _, unit in units]
        (whole,) = assemble(pieces, [(len(units),) + one], places, me, len(units))
        return whole.reshape(-1, one[1])

    def place_columns(units):
        def places(i, at):
            owner = jnp.bitwise_xor(at, units[i][0])
            return [(None, 0, (number_of(owner, above), slice(None), number_of(owner, below)))]

        ranks, one = units[0][1].shape[0], units[0][1].shape[1:]
        pieces = [unit for _, unit in units]
        (whole,) = assemble(pieces, [(high, ranks, deep) + one], places, me, len(units))
        return whole.reshape(-1, one[1])

    def by_rank(weight, upper, ranks):
        split = weight.reshape(weight.shape[0], upper, ranks, -1)
        return jnp.transpose(split, (2, 0, 1, 3)).reshape(ranks, weight.shape[0], -1)

    input_own = block_input.reshape(tokens, width)
    cot_own = cotangent.reshape(tokens, width)
    half = tokens // 2

    def stacked(value, bit, axis, *pins):
        got = fence(trade(value, bit), *pins)
        mine = bit_of(me, bit) == 0
        return jnp.stack([jnp.where(mine, value, got), jnp.where(mine, got, value)], axis=axis), got

    gains = jnp.stack([mixer_gain, mlp_gain])
    for i, b in enumerate(tp):
        gains, gains_got = stacked(gains, b, i)
    packed_width = -(-(2 * block_size + 8) // 128) * 128
    extra = -(-channel_rows // 16) * 16
    small = pl.pallas_call(
        pack_kernel,
        out_shape=jax.ShapeDtypeStruct((extra + 16, packed_width), F32),
        compiler_params=pltpu.CompilerParams(vmem_limit_bytes=VMEM_BYTES),
    )(
        conv_kernel,
        *(v[None] for v in (conv_bias, recur_gate_bias, input_gate_bias, decay_param)),
        gains.reshape(8, out_rows),
        recur_gate_weight,
        input_gate_weight,
    ).astype(BF16)
    small_shape = small.shape
    one, two = (trade(fence(input_own, gains_got), mask) for mask in (low, 2 * low))
    recur_pair = pair_up(recur_weight, above, me, small, one, two)
    recur_q = gather_along(recur_pair, below, 1).reshape(channels, width)
    small = fence(small, recur_pair)
    for i, b in enumerate(dp):
        small, small_got = stacked(small, b, i)
        if i == 0:
            first_got = small_got
    three = [trade(two[:half], low), trade(one[half:], 2 * low)]
    piece = exchange(fence(by_rank(mixer_weight, high, 4), recur_pair), step)
    branch_pair = pair_up(fence(branch_weight, first_got), above, me, piece, small_got, *three)
    branch_q = gather_along(branch_pair, below, 1).reshape(channels, width)
    mixer_pair = pair_up(fence(piece, branch_pair), above, me)
    cot_all = gather_along(fence(cot_own, mixer_pair)[None], tp_wide, 0)
    own_half = number_of(me, (wide,))
    cot_all = cot_all.reshape(2, 4 * tokens, width)
    mixer_q = gather_along(mixer_pair, below, 2).reshape(width, channels)
    small = small.reshape((share,) + small_shape)
    gains = small[:, extra + 8 :, :out_rows].reshape(high, deep, 4, 2, out_rows)
    gains = gains.transpose(3, 0, 2, 1, 4).reshape(2, width)
    gain_one, gain_two = gains[0].astype(F32), gains[1].astype(F32)
    numbers = jnp.moveaxis(small[:, extra : extra + 8, :channel_rows], 1, 0)
    numbers = numbers.reshape(TAPS + 4, channels).astype(F32)
    gate_rows = small[:, :channel_rows, : 2 * block_size].reshape(channels, -1)
    input_all = place_tokens([input_own, one, two, *three], low, me)

    coef = numbers
    decay_vec = coef[7:]
    coef = jnp.concatenate(
        [
            coef[:7],
            DECAY_SCALE * jax.nn.softplus(-decay_vec),
            DECAY_SCALE * jax.nn.sigmoid(-decay_vec),
            jnp.zeros((7, channels), F32),
        ]
    )
    rate_rows, gate_rows = gate_rows[:, :block_size], gate_rows[:, block_size:]
    number = np.arange(channels)
    spread = jnp.asarray(number[None] % block_size == np.arange(block_size)[:, None], BF16)
    diagonal = jnp.asarray(number[None] // block_size == number[:, None] // block_size, BF16)
    eye = jnp.asarray(np.eye(channels), BF16)
    collect = np.zeros((channels, 3, packed_width))
    collect[number, 0, number % block_size] = 1
    collect[number, 1, block_size + number % block_size] = 1
    collect[np.arange(8), 2, 2 * block_size + np.arange(8)] = 1
    collect = jnp.asarray(collect.reshape(channels, -1), BF16)
    lengths = lax.dynamic_slice_in_dim(seq_lengths, lax.axis_index("fsdp") * rows, rows, 0)
    base = seq_index.astype(jnp.int32) - tp_index * step
    scalars = jnp.concatenate([base[None], lengths.reshape(-1)])

    def join_ranks(parts, upper):
        got = exchange(parts, step)
        got = got.reshape(got.shape[:2] + (upper, -1))
        return jnp.transpose(got, (1, 2, 0, 3)).reshape(got.shape[1], -1).astype(F32)

    scale_one = inverse_rms(input_all.astype(F32))
    normed = (input_all.astype(F32) * scale_one * gain_one).astype(BF16)
    recur_in = project(normed, recur_q).astype(BF16)
    edge = recur_in.reshape(blocks, span, channels)[:, span - 4 :].reshape(4, rows, 4, channels)
    halo = across_blocks(edge)
    halo = halo.astype(F32).reshape(seq_count * rows, 4, channels)
    down_piece = exchange(fence(by_rank(down_weight, high_wide, 8), halo), step)
    recur_in = recur_in.reshape(blocks, span, channels)
    shape = (blocks, span, channels)
    one = (blocks, 1, channels)
    everything = (seq_count * rows, 1, channels)
    square = (channels, channels)
    padded = (span + 8, channels)
    conv, s_val, q_val, prod, part, ends, marks, rate_wide, gate_wide = call(
        functools.partial(forward_kernel, rows, step, seq_count * span),
        [(shape, BF16)] + [(shape, F32)] * 4
        + [((blocks, 2, channels), F32), ((blocks, span, 8), F32), (square, BF16), (square, BF16)],
        scalars,
        [recur_in, halo, coef, rate_rows, gate_rows, spread, diagonal],
        [pltpu.VMEM(padded, F32)],
        4,
    )
    ends_all = across_blocks(ends.reshape(4, rows, 2, channels)).reshape(-1, 2, channels)
    branch = project(normed, fence(branch_q, ends))
    branch = branch.reshape(blocks, span, channels)
    down_piece = fence(down_piece, ends_all)
    ends = fence(ends_all, branch)
    state, mixed, came = call(
        functools.partial(state_kernel, rows, step),
        [(shape, F32), (shape, BF16), (one, F32)],
        scalars,
        [prod, part, ends, branch],
        [pltpu.VMEM(everything, F32)],
        2,
    )
    down_pair = pair_up(fence(down_piece, cot_own), above_wide, me)
    down_q = gather_along(down_pair, below, 2).reshape(width, hidden)
    mixed_flat = mixed.reshape(4 * tokens, channels)
    mixer_part = project(fence(mixed_flat, down_piece), mixer_q).astype(BF16).reshape(4, tokens, width)
    gate_units = expand([(0, fence(gate_weight, mixed))], dp_wide)
    up_units = expand([(0, fence(up_weight, mixed))], dp_wide)
    gate_q, up_q = place_rows(gate_units, dp_wide), place_rows(up_units, dp_wide)
    mixer_parts = fence(exchange(mixer_part, step), gate_q, up_q)
    residual = input_own.astype(F32) + jnp.sum(mixer_parts.astype(F32), axis=0)


    scale_two = inverse_rms(residual)
    unit_two = residual * scale_two
    normed_own = (unit_two * gain_two).astype(BF16)
    normed_far = trade(normed_own, wide)
    near_list = share_direct(normed_own, low)
    far_list = share_direct(normed_far, low)
    near = place_tokens(near_list, low, me)
    cot_all = fence(cot_all, normed_own)
    cot_near, cot_far = pick(cot_all, own_half, 0), pick(cot_all, 1 - own_half, 0)
    near_out = feed_forward(near, cot_near, gate_q, up_q, down_q)
    ranks_shape = (4, tokens, width)
    far = place_tokens(fence_all(far_list, near_out[0]), low, me)
    far_out = feed_forward(far, cot_far, gate_q, up_q, down_q)
    grad_two_near = sum_tokens(near_out[0].reshape(ranks_shape), step)
    grad_far_parts = exchange(fence(far_out[0], grad_two_near).reshape(ranks_shape), step)

    def finish(partial, bits):
        partial = partial.reshape((2,) * len(bits) + partial.shape[1:])
        grad = Reduction(partial, range(len(bits)), bits, me)
        if bits:
            grad.send_to(0)
        return grad.total()

    def both(one, two, k):
        return outer(one[k], near) + outer(two[k], far)

    down_grad = outer(cot_near, near_out[1]) + outer(cot_far, far_out[1])
    down_grad = down_grad.astype(BF16).reshape(high_wide, 8, -1, hidden)
    grad_far_parts = fence(grad_far_parts, down_grad)
    down_grad = finish(scatter_along(down_grad, below, 2), above_wide).reshape(8, out_rows, hidden)
    grad_two_far = jnp.sum(grad_far_parts.astype(F32), axis=0).astype(BF16)
    grad_two = grad_two_near + trade(grad_two_far, wide).astype(F32)
    scaled = grad_two * gain_two
    grad_residual = cot_own.astype(F32) + scale_two * (
        scaled - unit_two * jnp.mean(scaled * unit_two, axis=-1, keepdims=True)
    )
    gain_two_part = jnp.sum(grad_two * unit_two, axis=0)

    grad_mix_own = grad_residual.astype(BF16)
    grad_mix_list = share_list(grad_mix_own, low)
    down_far = project(fence(far_out[1], grad_mix_own), down_q).astype(BF16)
    late = [fence_all(out[2:], grad_mix_own) for out in (near_out, far_out)]
    gate_grad = both(*late, 0).astype(BF16).reshape(high_wide, -1, width)
    up_grad = both(*late, 1).astype(BF16).reshape(high_wide, -1, width)
    down_far_parts = exchange(fence(down_far, *grad_mix_list[1:3]).reshape(ranks_shape), step)
    down_parts = fence(down_grad, grad_mix_own).reshape(2, 4, out_rows, hidden)
    down_sent, down_kept = halves(down_parts, 0, wide, me)
    down_got = trade(down_sent, wide)
    grad_mix = place_tokens(fence_all(grad_mix_list, down_got, gate_grad, up_grad, down_far), low, me)
    gate_grad = finish(scatter_along(gate_grad, below, 1), above_wide)
    up_grad = finish(scatter_along(up_grad, below, 1), above_wide)
    grad_mixed = back_project(grad_mix, mixer_q).reshape(shape)
    grad_branch, prod_back, part_back, own_ends = call(
        adjoint_kernel,
        [(shape, BF16), (shape, F32), (shape, F32), ((blocks, 2, channels), F32)],
        scalars,
        [grad_mixed, state, branch, s_val, marks, coef],
        [pltpu.VMEM(padded, F32)],
        3,
    )
    ends_back = across_blocks(own_ends.reshape(4, rows, 2, channels)).reshape(-1, 2, channels)
    grad_branch = grad_branch.reshape(4 * tokens, channels)
    mixer_grad = outer(fence(grad_mix, own_ends), mixed_flat).astype(BF16)
    mixer_grad = mixer_grad.reshape(high, 4, -1, channels)
    down_far = jnp.sum(fence(down_far_parts, own_ends).astype(F32), axis=0).astype(BF16)
    ends_back = fence(ends_back, mixer_grad, down_far)
    mixer_grad = scatter_along(mixer_grad, below, 2)
    down_far_own = trade(down_far, wide)
    packed_shape = (channels, packed_width)
    grad_conv, edge_back, packed = call(
        functools.partial(gates_kernel, rows, step),
        [(shape, F32), ((blocks, 4, channels), BF16), (packed_shape, BF16)],
        scalars,
        [
            prod_back, part_back, ends_back, s_val, q_val, conv, state, came, recur_in, halo,
            marks, coef, rate_wide, gate_wide, collect, diagonal, eye,
        ],
        [
            pltpu.VMEM((4 * tokens, channels), BF16),
            pltpu.VMEM((4 * tokens, channels), BF16),
            pltpu.VMEM((8, channels), F32),
            pltpu.VMEM(everything, F32),
            pltpu.VMEM(padded, F32),
            pltpu.VMEM(padded, F32),
        ],
        4,
    )
    edge_back = edge_back.reshape(4, rows, 4, channels)
    down_near = project(fence(near_out[1], own_ends), down_q).astype(BF16).reshape(ranks_shape)
    down_near = fence(down_near, edge_back)
    down_near = [pick(down_near, jnp.bitwise_xor(tp_index, j), 0) for j in range(4)]
    down_near[1:] = [trade(down_near[j], j * low) for j in (1, 2, 3)]
    halo_back = across_blocks(edge_back)
    last = len(dp)
    branch_grad = outer(fence(grad_branch, edge_back), normed).astype(BF16).reshape(high, -1, width)
    first_part = back_project(grad_branch, branch_q)
    halo_back = fence(halo_back, down_far_own, branch_grad, first_part)
    branch_grad = scatter_along(branch_grad, below, 1)
    halo_back = halo_back.astype(F32).reshape(seq_count * rows, 4, channels)
    (grad_recur,) = call(
        functools.partial(unconvolve_kernel, rows, step, seq_count),
        [(shape, BF16)],
        scalars,
        [grad_conv, halo_back, marks, coef],
        [pltpu.VMEM(padded, F32)],
        4,
    )
    grad_recur = grad_recur.reshape(4 * tokens, channels)
    recur_grad = reduce_rows(outer(grad_recur, normed), dp, me)
    grad_recur = fence(grad_recur, recur_grad.send())
    grad_normed_part = first_part + back_project(grad_recur, recur_q)
    grad_normed_sent = grad_normed_part.astype(BF16)
    recur_sent = recur_grad.send_to(last - 2, grad_normed_sent)
    packed = reduce_rows(fence(packed, grad_recur), dp, me)
    grad_normed_sent = fence(grad_normed_sent, recur_sent, packed.send())
    gain_one_part = jnp.sum(grad_normed_sent.astype(F32) * input_all.astype(F32) * scale_one, axis=0)
    grad_normed = sum_tokens(grad_normed_sent.reshape(ranks_shape), step)
    own_scale = inverse_rms(input_own.astype(F32))
    unit_one = input_own.astype(F32) * own_scale
    scaled_one = grad_normed * gain_one
    input_grad = (
        grad_residual
        + own_scale
        * (scaled_one - unit_one * jnp.mean(scaled_one * unit_one, axis=-1, keepdims=True))
    ).astype(BF16)
    def halve(partial):
        partial = fence(partial, grad_normed).reshape((2,) * len(above) + partial.shape[1:])
        return Reduction(partial, range(len(above)), above, me)

    mixer_grad, branch_grad = halve(mixer_grad), halve(branch_grad)
    mixer_sent = mixer_grad.send_to(0)
    recur_sent = recur_grad.send_to(0, grad_normed, mixer_sent)
    sent = branch_grad.send_to(0, recur_sent)
    packed_sent = packed.send_to(0, sent)
    pair = jnp.stack([fence(part, packed_sent) for part in (down_kept, down_got)], axis=1)
    pair = exchange(pair, step)
    flat_pieces = [pair[j, h] for h in range(2) for j in range(4)]
    down_weight_grad = pl.pallas_call(
        functools.partial(lay_kernel, 4, high_wide),
        out_shape=jax.ShapeDtypeStruct((out_rows, 8 * hidden), F32),
        in_specs=[pl.BlockSpec(memory_space=pltpu.SMEM)]
        + [pl.BlockSpec(memory_space=pltpu.VMEM)] * len(flat_pieces),
        out_specs=pl.BlockSpec(memory_space=pltpu.VMEM),
        compiler_params=pltpu.CompilerParams(vmem_limit_bytes=VMEM_BYTES),
    )(own_half.reshape(1), *flat_pieces)
    mixer_rows = mixer_grad.total(sent).astype(BF16).reshape(4, out_rows, channels)
    mixer_weight_grad = join_ranks(mixer_rows, high)
    down_sum = sum(fence(part, mixer_rows).astype(F32) for part in down_near + [down_far_own])
    block_output = (residual + down_sum).astype(BF16)
    recur_weight_grad = recur_grad.total(mixer_rows)
    branch_weight_grad = branch_grad.total(recur_weight_grad)
    packed = packed.total(recur_weight_grad)

    gain_parts = jnp.stack([gain_one_part, gain_two_part]).astype(BF16)
    gain_parts = jnp.moveaxis(gain_parts.reshape(2, device_count, out_rows), 1, 0)
    gain_parts = lax.all_to_all(fence(gain_parts, sent), AXES, 0, 0, tiled=True)
    gain_grads = jnp.sum(gain_parts.astype(F32), axis=0)
    numbers = packed[:, 2 * block_size : 2 * block_size + 8]
    return (
        block_output.reshape(rows, span, width),
        input_grad.reshape(rows, span, width),
        gain_grads[0],
        branch_weight_grad,
        recur_weight_grad,
        numbers[:, :TAPS],
        numbers[:, 4],
        packed[:, :block_size],
        numbers[:, 5],
        packed[:, block_size : 2 * block_size],
        numbers[:, 6],
        numbers[:, 7],
        mixer_weight_grad,
        gain_grads[1],
        gate_grad.reshape(hidden_rows, width).astype(F32),
        up_grad.reshape(hidden_rows, width).astype(F32),
        down_weight_grad,
    )


def solution(mesh):
    tokens, spread, table = P("fsdp", "seq", None), P(AXES), P(AXES, None)
    in_specs = (
        tokens, P(), spread, table, table, table, spread, table, spread, table, spread, spread,
        table, spread, table, table, table, tokens,
    )
    out_specs = (
        tokens, tokens, spread, table, table, table, spread, table, spread, table, spread, spread,
        table, spread, table, table, table,
    )
    return jax.shard_map(shards, mesh=mesh, in_specs=in_specs, out_specs=out_specs, check_vma=False)
```

```python
import functools
import math

import jax
import jax.numpy as jnp
import numpy as np
from jax import lax
from jax.experimental import pallas as pl
from jax.experimental.pallas import tpu as pltpu
from jax.sharding import PartitionSpec as P

AXES = ("seq", "fsdp")
TAPS = 4
EPSILON = 1e-06
DECAY_SCALE = 8.0
VMEM_BYTES = 56 * 1024 * 1024
BF16 = jnp.bfloat16
F32 = jnp.float32


def device_bits(seq_count, fsdp_count, rows, block):
    low = fsdp_count
    while low * rows < block:
        low *= 2
    total = seq_count * fsdp_count
    every = [1 << k for k in reversed(range(total.bit_length() - 1))]
    return low, tuple(every)


def linear_index():
    return lax.axis_index("seq") * lax.axis_size("fsdp") + lax.axis_index("fsdp")


def bit_of(index, bit):
    return lax.rem(lax.div(index, jnp.int32(bit)), jnp.int32(2))


def number_of(index, bits):
    value = jnp.int32(0)
    for b in bits:
        value = value * 2 + bit_of(index, b)
    return value


def fence(value, *others):
    return lax.optimization_barrier((value,) + others)[0]


def fence_all(values, *others):
    return list(lax.optimization_barrier(tuple(values) + others)[: len(values)])


def trade(value, mask):
    count = lax.axis_size("seq") * lax.axis_size("fsdp")
    return lax.ppermute(value, AXES, [(i, i ^ mask) for i in range(count)])


class Streams:
    def __init__(self):
        self.last = {}

    def trade(self, value, bit):
        if bit > 1:
            if bit in self.last:
                value = fence(value, self.last[bit])
            self.last[bit] = value = trade(value, bit)
            return value
        return trade(value, bit)


def pick(value, index, axis):
    return lax.dynamic_index_in_dim(value, index, axis, keepdims=False)


def put(buffer, part, index, axis):
    return lax.dynamic_update_index_in_dim(buffer, part, index, axis)


def gather_units(owns, bits, send):
    lists = [[(0, own)] for own in owns]
    for b in bits:
        fresh = [[] for _ in owns]
        for k in range(len(lists[0])):
            for units, new in zip(lists, fresh):
                mask, unit = units[k]
                new.append((mask | b, send(unit, b)))
        lists = [units + new for units, new in zip(lists, fresh)]
    return lists


def expand(units, bits):
    for b in bits:
        units = units + [(mask | b, trade(unit, b)) for mask, unit in units]
    return units


def pin_units(units, *others):
    return list(zip([mask for mask, _ in units], fence_all([unit for _, unit in units], *others)))


def copy_kernel(count, shapes, places, scalars, *refs):
    pieces, wholes, sems = refs[:count], refs[count:-1], refs[-1]
    copies = []
    for i, piece in enumerate(pieces):
        for source, which, target in places(i, scalars[0]):
            here = piece if source is None else piece.at[source]
            copies.append(
                pltpu.make_async_copy(here, wholes[which].at[target], sems.at[len(copies)])
            )
    for c in copies:
        c.start()
    for c in copies:
        c.wait()


def assemble(pieces, shapes, places, me, copies):
    where = pl.BlockSpec(memory_space=pl.ANY)
    return pl.pallas_call(
        functools.partial(copy_kernel, len(pieces), shapes, places),
        out_shape=[jax.ShapeDtypeStruct(shape, pieces[0].dtype) for shape in shapes],
        in_specs=[pl.BlockSpec(memory_space=pltpu.SMEM)] + [where] * len(pieces),
        out_specs=[pl.BlockSpec(memory_space=pltpu.VMEM)] * len(shapes),
        scratch_shapes=[pltpu.SemaphoreType.DMA((copies,))],
        compiler_params=pltpu.CompilerParams(vmem_limit_bytes=VMEM_BYTES),
        cost_estimate=pl.CostEstimate(
            flops=0, bytes_accessed=4 * sum(piece.size for piece in pieces), transcendentals=0
        ),
    )(me.astype(jnp.int32).reshape(1), *pieces)


def halves(value, axis, bit, me):
    mine = bit_of(me, bit)
    return pick(value, 1 - mine, axis), pick(value, mine, axis)


class Reduction:
    def __init__(self, value, axes, bits, me):
        self.kept, self.got, self.me = value, None, me
        self.left = list(zip(axes, bits))

    def send(self, *after):
        value = self.total(*after).astype(BF16)
        axis, bit = self.left.pop()
        away, self.kept = halves(value, axis, bit, self.me)
        self.got = trade(away, bit)
        return away

    def send_to(self, count, *after):
        while len(self.left) > count:
            away = self.send(*after)
        return away

    def total(self, *after):
        if self.got is None:
            return self.kept
        return self.kept.astype(F32) + fence(self.got, *after).astype(F32)


def reduce_rows(whole, bits, me):
    whole = whole.astype(BF16).reshape((2,) * len(bits) + (whole.shape[0] >> len(bits), -1))
    return Reduction(whole, range(len(bits)), bits, me)


def reduce_columns(whole, bits, ranks, low, me):
    above = sum(b > low for b in bits)
    split = (2,) * above + (ranks,) + (2,) * (len(bits) - above)
    rows = whole.shape[0] // (ranks << len(bits))
    whole = whole.astype(BF16).reshape(split + (rows, whole.shape[1]))
    return Reduction(whole, [k if b > low else k + 1 for k, b in enumerate(bits)], bits, me)


def share_list(own, low):
    half = own.shape[-2] // 2
    one, two = trade(own, low), trade(own, 2 * low)
    three = (trade(two[..., :half, :], low), trade(one[..., half:, :], 2 * low))
    return [own, one, two, *three]


def share_direct(own, low):
    return [own] + [trade(own, j * low) for j in (1, 2, 3)]


def place_tokens(units, low, me):
    rows, width = units[0].shape
    pieces = list(units)

    def places(i, at):
        slot = jnp.bitwise_xor(number_of(at, (2 * low, low)), min(i, 3))
        start = pl.multiple_of(slot * rows + (rows // 2 if i == 4 else 0), rows // 2)
        return [(None, 0, pl.ds(start, pieces[i].shape[0]))]

    (whole,) = assemble(pieces, [(4 * rows, width)], places, me, len(pieces))
    return whole


def groups_of(bits, count):
    inside = [0]
    for b in bits:
        inside = [i | k for i in inside for k in (0, b)]
    return [[first | i for i in inside] for first in range(count) if not first & sum(bits)]


def line_of(bits):
    fsdp_count, count = lax.axis_size("fsdp"), lax.axis_size("seq") * lax.axis_size("fsdp")
    if sum(bits) == fsdp_count - 1:
        return {"axis_name": "fsdp"}
    if sum(bits) == count - fsdp_count:
        return {"axis_name": "seq"}
    if sum(bits) == count - 1:
        return {"axis_name": AXES}
    return {"axis_name": AXES, "axis_index_groups": groups_of(bits, count)}


def gather_along(own, bits, axis):
    return lax.all_gather(own, axis=axis, tiled=True, **line_of(bits))


def scatter_along(partial, bits, axis):
    return lax.psum_scatter(partial, scatter_dimension=axis, tiled=True, **line_of(bits))


def pair_up(own, bits, me, *pins):
    value = own
    for i, b in enumerate(bits):
        got = fence(trade(value, b), *pins)
        mine = bit_of(me, b) == 0
        value = jnp.stack([jnp.where(mine, value, got), jnp.where(mine, got, value)], axis=i)
    return value.reshape((1 << len(bits),) + own.shape)


def exchange(parts, step):
    ranks, count = parts.shape[0], lax.axis_size("seq")
    inside = [r * step for r in range(ranks)]
    groups = [[b + i for i in inside] for b in range(count) if not b & ((ranks - 1) * step)]
    return lax.all_to_all(parts, "seq", 0, 0, axis_index_groups=groups, tiled=True)


def sum_tokens(partial, step):
    return jnp.sum(exchange(partial, step).astype(F32), axis=0)


def project(left, weight):
    return lax.dot_general(left, weight, (((1,), (1,)), ((), ())), preferred_element_type=F32)


def back_project(left, weight):
    return lax.dot_general(left, weight, (((1,), (0,)), ((), ())), preferred_element_type=F32)


def outer(grads, values):
    return lax.dot_general(grads, values, (((0,), (0,)), ((), ())), preferred_element_type=F32)


def inverse_rms(values):
    return lax.rsqrt(jnp.mean(values * values, axis=-1, keepdims=True) + EPSILON)


def gelu_parts(v):
    c = 0.7978845608028654
    t = jnp.tanh(c * (v + 0.044715 * v * v * v))
    act = 0.5 * v * (1.0 + t)
    slope = 0.5 * (1.0 + t) + 0.5 * v * (1.0 - t * t) * c * (1.0 + 3 * 0.044715 * v * v)
    return act, slope


def call(body, outs, scalars, arrays, scratch=(), passes=1):
    sizes = [array.size * array.dtype.itemsize for array in arrays]
    sizes += [math.prod(shape) * jnp.dtype(kind).itemsize for shape, kind in outs]
    return pl.pallas_call(
        body,
        out_shape=[jax.ShapeDtypeStruct(shape, kind) for shape, kind in outs],
        in_specs=[pl.BlockSpec(memory_space=pltpu.SMEM)]
        + [pl.BlockSpec(memory_space=pltpu.VMEM)] * len(arrays),
        out_specs=[pl.BlockSpec(memory_space=pltpu.VMEM)] * len(outs),
        scratch_shapes=list(scratch),
        compiler_params=pltpu.CompilerParams(vmem_limit_bytes=VMEM_BYTES),
        cost_estimate=pl.CostEstimate(
            flops=0, bytes_accessed=passes * sum(sizes), transcendentals=0
        ),
    )(scalars, *arrays)


LANES = 128


def lane_groups(channels):
    return [slice(c, c + LANES) for c in range(0, channels, LANES)]


def column(marks, n, k):
    return jnp.broadcast_to(marks[n][:, k : k + 1], (marks.shape[1], LANES))


def block_number(scalars, n, rows, step):
    return jnp.bitwise_xor(scalars[0], (n // rows) * step)


def injection(s, speed):
    y = speed * s
    e = jnp.exp(-y)
    z = 2.0 * y
    series = 1.0 - z * (1 / 7)
    for k in (6, 5, 4, 3, 2):
        series = 1.0 - z * (1 / k) * series
    return e, jnp.sqrt(jnp.where(z < 0.35, z * series, 1.0 - e * e))


def span_scan(a, b, reverse):
    span, channels = a.shape
    within = lax.broadcasted_iota(jnp.int32, (span, channels), 0) % 8
    for k in (1, 2, 4):
        turn = span - k if reverse else k
        reached = within < 8 - k if reverse else within >= k
        a_far = jnp.where(reached, pltpu.roll(a, turn, 0), 1.0)
        b_far = jnp.where(reached, pltpu.roll(b, turn, 0), 0.0)
        b = b + a * b_far
        a = a * a_far
    count = span // 8
    order = range(count - 1, -1, -1) if reverse else range(count)
    edge = 0 if reverse else 7
    a_all, b_all = [None] * count, [None] * count
    p = jnp.ones((1, channels), F32)
    h = jnp.zeros((1, channels), F32)
    for i in order:
        a_i, b_i = a[8 * i : 8 * i + 8], b[8 * i : 8 * i + 8]
        b_all[i] = b_i + a_i * h
        a_all[i] = a_i * p
        p = a_all[i][edge : edge + 1]
        h = b_all[i][edge : edge + 1]
    return jnp.concatenate(a_all, axis=0), jnp.concatenate(b_all, axis=0), p, h


def sequence_marks(scalars, block, row, span, total_len):
    rows = row[1]
    slots = (scalars.shape[0] - 1) // rows
    place = block * span + lax.broadcasted_iota(jnp.int32, (span, 8), 0)
    column = lax.broadcasted_iota(jnp.int32, (span, 8), 1)
    other = place + jnp.where(column <= 3, -column, column - 3)
    here = jnp.full((span, 8), -1, jnp.int32)
    there = jnp.full((span, 8), -1, jnp.int32)
    first = jnp.zeros((span, 8), jnp.int32)
    offset = jnp.int32(0)
    for j in range(slots):
        length = scalars[1 + row[0] * slots + j]
        live = jnp.where(length > 0, 1, 0)
        here = here + jnp.where(place >= offset, live, 0)
        there = there + jnp.where(other >= offset, live, 0)
        first = first + jnp.where(place == offset, live, 0)
        offset = offset + length
    inside = (other >= 0) & (other < total_len)
    same = jnp.where(inside & (here == there), 1, 0)
    return jnp.where(column == 0, first, same).astype(F32)


def forward_kernel(
    rows, step, total_len, scalars, recur, halo, coef, rate_rows, gate_rows, spread, diagonal,
    conv, s_out, q_out, prod, part, ends, marks, rate_w, gate_w, pad,
):
    count, span, channels = recur.shape

    def mark(n, carry):
        block = block_number(scalars, n, rows, step)
        marks[n] = sequence_marks(scalars, block, (n % rows, rows), span, total_len)
        return carry

    lax.fori_loop(0, count, mark, 0)
    for narrow, wide in ((rate_rows, rate_w), (gate_rows, gate_w)):
        wide[...] = (back_project(narrow[...], spread[...]) * diagonal[...].astype(F32)).astype(BF16)

    def convolve(n, carry):
        block = block_number(scalars, n, rows, step)
        before = jnp.bitwise_xor(jnp.maximum(block - 1, 0), scalars[0])
        same = [column(marks, n, k) for k in range(1, TAPS)]
        for at in lane_groups(channels):
            pad[4:8, at] = halo[before * rows + n % rows, :, at]
            pad[8:, at] = recur[n, :, at].astype(F32)
            total = coef[4:5, at] + coef[0:1, at] * pad[8:, at]
            for k in range(1, TAPS):
                total = total + coef[k : k + 1, at] * pad[8 - k : 8 - k + span, at] * same[k - 1]
            conv[n, :, at] = total.astype(BF16)
        return carry

    lax.fori_loop(0, count, convolve, 0)
    flat = conv[...].reshape(count * span, channels)
    s_out[...] = project(flat, rate_w[...]).reshape(count, span, channels)
    q_out[...] = project(flat, gate_w[...]).reshape(count, span, channels)

    def scan(n, carry):
        going = 1.0 - column(marks, n, 0)
        for at in lane_groups(channels):
            s = jax.nn.sigmoid(s_out[n, :, at] + coef[5:6, at])
            q = jax.nn.sigmoid(q_out[n, :, at] + coef[6:7, at])
            s_out[n, :, at] = s
            q_out[n, :, at] = q
            e, m = injection(s, coef[7:8, at])
            inject = m * q * conv[n, :, at].astype(F32)
            p_all, h_all, p, h = span_scan(e * going, inject, False)
            prod[n, :, at] = p_all
            part[n, :, at] = h_all
            ends[n, 0:1, at] = p
            ends[n, 1:2, at] = h
        return carry

    lax.fori_loop(0, count, scan, 0)


def join(ends, into, scalars, rows, blocks, reverse):
    def lap(k, carry):
        block = blocks - 1 - k if reverse else k
        place = jnp.bitwise_xor(block, scalars[0]) * rows
        new = []
        for r in range(rows):
            into[block * rows + r] = carry[r]
            pair = ends[place + r]
            new.append(pair[0:1] * carry[r] + pair[1:2])
        return tuple(new)

    channels = into.shape[-1]
    lax.fori_loop(0, blocks, lap, (jnp.zeros((1, channels), F32),) * rows)


def state_kernel(rows, step, scalars, prod, part, ends, branch, state, mixed, came, into):
    count = prod.shape[0]
    join(ends, into, scalars, rows, into.shape[0] // rows, False)

    def finish(n, carry):
        place = block_number(scalars, n, rows, step) * rows + n % rows
        for at in lane_groups(prod.shape[2]):
            incoming = into[place, :, at]
            h = part[n, :, at] + prod[n, :, at] * incoming
            came[n, :, at] = incoming
            state[n, :, at] = h
            mixed[n, :, at] = (h * gelu_parts(branch[n, :, at])[0]).astype(BF16)
        return carry

    lax.fori_loop(0, count, finish, 0)


def adjoint_kernel(
    scalars, grad_mixed, state, branch, s_in, marks, coef, grad_branch, prod, part, ends, pad
):
    count, span, channels = state.shape
    pad[span:, :] = jnp.ones((8, channels), F32)

    def scan(n, carry):
        going = 1.0 - column(marks, n, 0)
        for at in lane_groups(channels):
            act, slope = gelu_parts(branch[n, :, at])
            grad = grad_mixed[n, :, at]
            grad_branch[n, :, at] = (grad * state[n, :, at] * slope).astype(BF16)
            decay = jnp.exp(-coef[7:8, at] * s_in[n, :, at]) * going
            pad[:span, at] = decay
            p_all, h_all, p, h = span_scan(pad[1 : span + 1, at], grad * act, True)
            prod[n, :, at] = p_all
            part[n, :, at] = h_all
            ends[n, 0:1, at] = decay[0:1] * p
            ends[n, 1:2, at] = decay[0:1] * h
        return carry

    lax.fori_loop(0, count, scan, 0)


def gates_kernel(
    rows, step, scalars, prod, part, ends, s_in, q_in, conv, state, came, recur, halo, marks, coef,
    rate_w, gate_w, collect, diagonal, eye, grad_conv, edges, packed, grad_rate, grad_gate, sums,
    into, pad, pad_two,
):
    count, span, channels = prod.shape
    join(ends, into, scalars, rows, into.shape[0] // rows, True)
    sums[...] = jnp.zeros((8, channels), F32)

    def terms(n, carry):
        place = block_number(scalars, n, rows, step) * rows + n % rows
        going = 1.0 - column(marks, n, 0)
        here = pl.ds(pl.multiple_of(n * span, span), span)
        for at in lane_groups(channels):
            total = part[n, :, at] + prod[n, :, at] * into[place, :, at]
            pad[7:8, at] = came[n, :, at]
            pad[8:, at] = state[n, :, at]
            s, q = s_in[n, :, at], q_in[n, :, at]
            speed = coef[7:8, at]
            e, m = injection(s, speed)
            c = conv[n, :, at].astype(F32)
            qc = q * c
            grad_log = total * e * (pad[7 : 7 + span, at] * going - e * qc / m)
            rate = -speed * (s * (1.0 - s)) * grad_log
            gate = total * m * qc * (1.0 - q)
            grad_conv[n, :, at] = total * m * q
            grad_rate[here, at] = rate.astype(BF16)
            grad_gate[here, at] = gate.astype(BF16)
            sums[5:6, at] += jnp.sum(rate, axis=0, keepdims=True)
            sums[6:7, at] += jnp.sum(gate, axis=0, keepdims=True)
            sums[7:8, at] += jnp.sum(coef[8:9, at] * s * grad_log, axis=0, keepdims=True)
        return carry

    lax.fori_loop(0, count, terms, 0)
    through = back_project(grad_rate[...], rate_w[...]) + back_project(grad_gate[...], gate_w[...])
    grad_conv[...] += through.reshape(count, span, channels)
    flat = conv[...].reshape(count * span, channels)

    def kernel_terms(n, carry):
        block = block_number(scalars, n, rows, step)
        before = jnp.bitwise_xor(jnp.maximum(block - 1, 0), scalars[0])
        same = [column(marks, n, k) for k in range(1, TAPS)]
        for at in lane_groups(channels):
            pad_two[4:8, at] = halo[before * rows + n % rows, :, at]
            pad_two[8:, at] = recur[n, :, at].astype(F32)
            grad = grad_conv[n, :, at]
            edges[n, :, at] = grad[:4].astype(BF16)
            sums[4:5, at] += jnp.sum(grad, axis=0, keepdims=True)
            sums[0:1, at] += jnp.sum(grad * pad_two[8:, at], axis=0, keepdims=True)
            for k in range(1, TAPS):
                term = grad * pad_two[8 - k : 8 - k + span, at] * same[k - 1]
                sums[k : k + 1, at] += jnp.sum(term, axis=0, keepdims=True)
        return carry

    lax.fori_loop(0, count, kernel_terms, 0)
    on = diagonal[...].astype(F32)
    size = collect.shape[1] // 3
    total = back_project((outer(grad_rate[...], flat) * on).astype(BF16), collect[:, :size])
    total += back_project((outer(grad_gate[...], flat) * on).astype(BF16), collect[:, size : 2 * size])
    turned = project(eye[...], sums[...].astype(BF16))
    total += back_project(turned.astype(BF16), collect[:8, 2 * size :])
    packed[...] = total.astype(BF16)


def unconvolve_kernel(rows, step, blocks, scalars, grad_conv, halo, marks, coef, grad_recur, pad):
    count, span, channels = grad_conv.shape

    def body(n, carry):
        block = block_number(scalars, n, rows, step)
        behind = jnp.bitwise_xor(jnp.minimum(block + 1, blocks - 1), scalars[0])
        seen = [column(marks, n, 3 + k) for k in range(1, TAPS)]
        for at in lane_groups(channels):
            pad[:span, at] = grad_conv[n, :, at]
            pad[span : span + 4, at] = halo[behind * rows + n % rows, :, at]
            total = coef[0:1, at] * pad[:span, at]
            for k in range(1, TAPS):
                total = total + coef[k : k + 1, at] * pad[k : k + span, at] * seen[k - 1]
            grad_recur[n, :, at] = total.astype(BF16)
        return carry

    lax.fori_loop(0, count, body, 0)


def pack_kernel(taps, bias, rate_bias, gate_bias, decay, gains, rate_w, gate_w, packed):
    count, size = rate_w.shape
    packed[...] = jnp.zeros(packed.shape, F32)
    packed[:count, :size] = rate_w[...].astype(F32)
    packed[:count, size : 2 * size] = gate_w[...].astype(F32)
    first = packed.shape[0] - 16
    packed[first : first + TAPS, :count] = taps[...].astype(F32).T
    for i, row in enumerate((bias, rate_bias, gate_bias, decay)):
        packed[first + TAPS + i : first + TAPS + i + 1, :count] = row[...].astype(F32)
    packed[first + 8 :, : gains.shape[1]] = gains[...].astype(F32)


def lay_kernel(ranks, upper, half, *refs):
    pieces, whole = refs[:-1], refs[-1]
    for i, piece in enumerate(pieces):
        rank = jnp.bitwise_xor(half[0], i // ranks) * ranks + i % ranks
        size = piece.shape[1] // upper
        for u in range(upper):
            start = pl.multiple_of((u * 2 * ranks + rank) * size, 128)
            whole[:, pl.ds(start, size)] = piece[:, u * size : (u + 1) * size].astype(F32)


def feed_forward(tokens, cot, gate_w, up_w, down_w):
    act, slope = gelu_parts(project(tokens, gate_w))
    up_val = project(tokens, up_w)
    hidden = (act * up_val).astype(BF16)
    grad_hidden = back_project(cot, down_w)
    grad_gate = (grad_hidden * up_val * slope).astype(BF16)
    grad_up = (grad_hidden * act).astype(BF16)
    grad = (back_project(grad_gate, gate_w) + back_project(grad_up, up_w)).astype(BF16)
    return grad, hidden, grad_gate, grad_up


def shards(
    block_input,
    seq_lengths,
    mixer_gain,
    branch_weight,
    recur_weight,
    conv_kernel,
    conv_bias,
    recur_gate_weight,
    recur_gate_bias,
    input_gate_weight,
    input_gate_bias,
    decay_param,
    mixer_weight,
    mlp_gain,
    gate_weight,
    up_weight,
    down_weight,
    cotangent,
):
    rows, span, width = block_input.shape
    tokens = rows * span
    seq_count, fsdp_count = lax.axis_size("seq"), lax.axis_size("fsdp")
    device_count = seq_count * fsdp_count
    channel_rows = branch_weight.shape[0]
    hidden_rows = gate_weight.shape[0]
    out_rows = mixer_weight.shape[0]
    block_size = recur_gate_weight.shape[1]
    low, every = device_bits(seq_count, fsdp_count, channel_rows, block_size)
    wide = 4 * low
    tp, tp_wide = (2 * low, low), (wide, 2 * low, low)
    dp = tuple(b for b in every if b not in tp)
    dp_wide = tuple(b for b in every if b not in tp_wide)
    above, below = tuple(b for b in dp if b > low), tuple(b for b in dp if b < low)
    above_wide = tuple(b for b in above if b != wide)
    step = low // fsdp_count
    me = linear_index().astype(jnp.int32)
    seq_index = lax.axis_index("seq")
    tp_index = number_of(me, tp)
    share, share_wide = 1 << len(dp), 1 << len(dp_wide)
    high, deep, high_wide = 1 << len(above), 1 << len(below), 1 << len(above_wide)
    channels = share * channel_rows
    hidden = share_wide * hidden_rows
    blocks = 4 * rows
    seq_dp = tuple(b for b in dp if b >= fsdp_count)
    streams = Streams()

    def across_blocks(own):
        units = sorted(gather_units([own], seq_dp, trade)[0], key=lambda unit: unit[0])
        every_slot = jnp.stack([unit for _, unit in units])
        every_slot = every_slot.reshape((-1, step) + own.shape)
        return jnp.moveaxis(every_slot, 2, 1).reshape((seq_count,) + own.shape[1:])

    def place_rows(units, bits):
        def places(i, at):
            return [(None, 0, number_of(jnp.bitwise_xor(at, units[i][0]), bits))]

        one = units[0][1].shape
        pieces = [unit for _, unit in units]
        (whole,) = assemble(pieces, [(len(units),) + one], places, me, len(units))
        return whole.reshape(-1, one[1])

    def place_columns(units):
        def places(i, at):
            owner = jnp.bitwise_xor(at, units[i][0])
            return [(None, 0, (number_of(owner, above), slice(None), number_of(owner, below)))]

        ranks, one = units[0][1].shape[0], units[0][1].shape[1:]
        pieces = [unit for _, unit in units]
        (whole,) = assemble(pieces, [(high, ranks, deep) + one], places, me, len(units))
        return whole.reshape(-1, one[1])

    def by_rank(weight, upper, ranks):
        split = weight.reshape(weight.shape[0], upper, ranks, -1)
        return jnp.transpose(split, (2, 0, 1, 3)).reshape(ranks, weight.shape[0], -1)

    input_own = block_input.reshape(tokens, width)
    cot_own = cotangent.reshape(tokens, width)
    half = tokens // 2

    def stacked(value, bit, axis, *pins):
        got = fence(trade(value, bit), *pins)
        mine = bit_of(me, bit) == 0
        return jnp.stack([jnp.where(mine, value, got), jnp.where(mine, got, value)], axis=axis), got

    gains = jnp.stack([mixer_gain, mlp_gain])
    for i, b in enumerate(tp):
        gains, gains_got = stacked(gains, b, i)
    packed_width = -(-(2 * block_size + 8) // 128) * 128
    extra = -(-channel_rows // 16) * 16
    small = pl.pallas_call(
        pack_kernel,
        out_shape=jax.ShapeDtypeStruct((extra + 16, packed_width), F32),
        compiler_params=pltpu.CompilerParams(vmem_limit_bytes=VMEM_BYTES),
    )(
        conv_kernel,
        *(v[None] for v in (conv_bias, recur_gate_bias, input_gate_bias, decay_param)),
        gains.reshape(8, out_rows),
        recur_gate_weight,
        input_gate_weight,
    ).astype(BF16)
    small_shape = small.shape
    one, two = (trade(input_own, mask) for mask in (low, 2 * low))
    recur_pair = pair_up(recur_weight, above, me, gains_got)
    recur_q = gather_along(recur_pair, below, 1).reshape(channels, width)
    small = fence(small, recur_pair)
    for i, b in enumerate(dp):
        small, small_got = stacked(small, b, i)
        if i == 0:
            first_got = small_got
    three = [trade(two[:half], low), trade(one[half:], 2 * low)]
    piece = exchange(fence(by_rank(mixer_weight, high, 4), recur_pair), step)
    branch_pair = pair_up(fence(branch_weight, first_got), above, me, piece, small_got, *three)
    branch_q = gather_along(branch_pair, below, 1).reshape(channels, width)
    mixer_pair = pair_up(fence(piece, branch_pair), above, me)
    cot_all = gather_along(fence(cot_own, mixer_pair)[None], tp_wide, 0)
    own_half = number_of(me, (wide,))
    cot_all = cot_all.reshape(2, 4 * tokens, width)
    mixer_q = gather_along(mixer_pair, below, 2).reshape(width, channels)
    small = small.reshape((share,) + small_shape)
    gains = small[:, extra + 8 :, :out_rows].reshape(high, deep, 4, 2, out_rows)
    gains = gains.transpose(3, 0, 2, 1, 4).reshape(2, width)
    gain_one, gain_two = gains[0].astype(F32), gains[1].astype(F32)
    numbers = jnp.moveaxis(small[:, extra : extra + 8, :channel_rows], 1, 0)
    numbers = numbers.reshape(TAPS + 4, channels).astype(F32)
    gate_rows = small[:, :channel_rows, : 2 * block_size].reshape(channels, -1)
    input_all = place_tokens([input_own, one, two, *three], low, me)

    coef = numbers
    decay_vec = coef[7:]
    coef = jnp.concatenate(
        [
            coef[:7],
            DECAY_SCALE * jax.nn.softplus(-decay_vec),
            DECAY_SCALE * jax.nn.sigmoid(-decay_vec),
            jnp.zeros((7, channels), F32),
        ]
    )
    rate_rows, gate_rows = gate_rows[:, :block_size], gate_rows[:, block_size:]
    number = np.arange(channels)
    spread = jnp.asarray(number[None] % block_size == np.arange(block_size)[:, None], BF16)
    diagonal = jnp.asarray(number[None] // block_size == number[:, None] // block_size, BF16)
    eye = jnp.asarray(np.eye(channels), BF16)
    collect = np.zeros((channels, 3, packed_width))
    collect[number, 0, number % block_size] = 1
    collect[number, 1, block_size + number % block_size] = 1
    collect[np.arange(8), 2, 2 * block_size + np.arange(8)] = 1
    collect = jnp.asarray(collect.reshape(channels, -1), BF16)
    lengths = lax.dynamic_slice_in_dim(seq_lengths, lax.axis_index("fsdp") * rows, rows, 0)
    base = seq_index.astype(jnp.int32) - tp_index * step
    scalars = jnp.concatenate([base[None], lengths.reshape(-1)])

    def join_ranks(parts, upper):
        got = exchange(parts, step)
        got = got.reshape(got.shape[:2] + (upper, -1))
        return jnp.transpose(got, (1, 2, 0, 3)).reshape(got.shape[1], -1).astype(F32)

    scale_one = inverse_rms(input_all.astype(F32))
    normed = (input_all.astype(F32) * scale_one * gain_one).astype(BF16)
    recur_in = project(normed, recur_q).astype(BF16)
    edge = recur_in.reshape(blocks, span, channels)[:, span - 4 :].reshape(4, rows, 4, channels)
    halo = across_blocks(edge)
    halo = halo.astype(F32).reshape(seq_count * rows, 4, channels)
    down_piece = exchange(fence(by_rank(down_weight, high_wide, 8), halo), step)
    recur_in = recur_in.reshape(blocks, span, channels)
    shape = (blocks, span, channels)
    one = (blocks, 1, channels)
    everything = (seq_count * rows, 1, channels)
    square = (channels, channels)
    padded = (span + 8, channels)
    conv, s_val, q_val, prod, part, ends, marks, rate_wide, gate_wide = call(
        functools.partial(forward_kernel, rows, step, seq_count * span),
        [(shape, BF16)] + [(shape, F32)] * 4
        + [((blocks, 2, channels), F32), ((blocks, span, 8), F32), (square, BF16), (square, BF16)],
        scalars,
        [recur_in, halo, coef, rate_rows, gate_rows, spread, diagonal],
        [pltpu.VMEM(padded, F32)],
        4,
    )
    ends_all = across_blocks(ends.reshape(4, rows, 2, channels)).reshape(-1, 2, channels)
    branch = project(normed, fence(branch_q, ends))
    branch = branch.reshape(blocks, span, channels)
    down_piece = fence(down_piece, ends_all)
    ends = fence(ends_all, branch)
    state, mixed, came = call(
        functools.partial(state_kernel, rows, step),
        [(shape, F32), (shape, BF16), (one, F32)],
        scalars,
        [prod, part, ends, branch],
        [pltpu.VMEM(everything, F32)],
        2,
    )
    down_pair = pair_up(fence(down_piece, cot_own), above_wide, me)
    down_q = gather_along(down_pair, below, 2).reshape(width, hidden)
    mixed_flat = mixed.reshape(4 * tokens, channels)
    mixer_part = project(fence(mixed_flat, down_piece), mixer_q).astype(BF16).reshape(4, tokens, width)
    gate_units = expand([(0, fence(gate_weight, mixed))], dp_wide)
    up_units = expand([(0, fence(up_weight, mixed))], dp_wide)
    gate_q, up_q = place_rows(gate_units, dp_wide), place_rows(up_units, dp_wide)
    mixer_parts = fence(exchange(mixer_part, step), gate_q, up_q)
    residual = input_own.astype(F32) + jnp.sum(mixer_parts.astype(F32), axis=0)


    scale_two = inverse_rms(residual)
    unit_two = residual * scale_two
    normed_own = (unit_two * gain_two).astype(BF16)
    normed_far = trade(normed_own, wide)
    near_list = share_list(normed_own, low)
    far_list = share_direct(normed_far, low)
    near = place_tokens(near_list, low, me)
    cot_all = fence(cot_all, normed_own)
    cot_near, cot_far = pick(cot_all, own_half, 0), pick(cot_all, 1 - own_half, 0)
    near_out = feed_forward(near, cot_near, gate_q, up_q, down_q)
    ranks_shape = (4, tokens, width)
    far = place_tokens(fence_all(far_list, near_out[0]), low, me)
    far_out = feed_forward(far, cot_far, gate_q, up_q, down_q)
    grad_far_parts = exchange(far_out[0].reshape(ranks_shape), step)

    def finish(partial, bits):
        partial = partial.reshape((2,) * len(bits) + partial.shape[1:])
        grad = Reduction(partial, range(len(bits)), bits, me)
        if bits:
            grad.send_to(0)
        return grad.total()

    def both(one, two, k):
        return outer(one[k], near) + outer(two[k], far)

    down_grad = outer(cot_near, near_out[1]) + outer(cot_far, far_out[1])
    down_grad = down_grad.astype(BF16).reshape(high_wide, 8, -1, hidden)
    grad_far_parts = fence(grad_far_parts, down_grad)
    down_grad = finish(scatter_along(down_grad, below, 2), above_wide).reshape(8, out_rows, hidden)
    grad_two_far = jnp.sum(grad_far_parts.astype(F32), axis=0).astype(BF16)
    grad_near_parts = exchange(fence(near_out[0], grad_two_far).reshape(ranks_shape), step)
    gate_grad = both(near_out, far_out, 2).astype(BF16).reshape(high_wide, -1, width)
    up_grad = both(near_out, far_out, 3).astype(BF16).reshape(high_wide, -1, width)
    grad_near_parts = fence(grad_near_parts, gate_grad, up_grad)
    gate_grad = finish(scatter_along(gate_grad, below, 1), above_wide)
    up_grad = finish(scatter_along(up_grad, below, 1), above_wide)
    grad_two_near = jnp.sum(grad_near_parts.astype(F32), axis=0)
    grad_two = grad_two_near + trade(grad_two_far, wide).astype(F32)
    scaled = grad_two * gain_two
    grad_residual = cot_own.astype(F32) + scale_two * (
        scaled - unit_two * jnp.mean(scaled * unit_two, axis=-1, keepdims=True)
    )
    gain_two_part = jnp.sum(grad_two * unit_two, axis=0)

    grad_mix_own = grad_residual.astype(BF16)
    grad_mix_list = share_list(grad_mix_own, low)
    down_far = project(fence(far_out[1], grad_mix_own), down_q).astype(BF16)
    down_far_parts = exchange(fence(down_far, *grad_mix_list[1:3]).reshape(ranks_shape), step)
    down_parts = fence(down_grad, grad_mix_own).reshape(2, 4, out_rows, hidden)
    down_sent, down_kept = halves(down_parts, 0, wide, me)
    down_got = trade(down_sent, wide)
    grad_mix = place_tokens(fence_all(grad_mix_list, down_got, down_far), low, me)
    grad_mixed = back_project(grad_mix, mixer_q).reshape(shape)
    grad_branch, prod_back, part_back, own_ends = call(
        adjoint_kernel,
        [(shape, BF16), (shape, F32), (shape, F32), ((blocks, 2, channels), F32)],
        scalars,
        [grad_mixed, state, branch, s_val, marks, coef],
        [pltpu.VMEM(padded, F32)],
        3,
    )
    ends_back = across_blocks(own_ends.reshape(4, rows, 2, channels)).reshape(-1, 2, channels)
    grad_branch = grad_branch.reshape(4 * tokens, channels)
    mixer_grad = outer(fence(grad_mix, own_ends), mixed_flat).astype(BF16)
    mixer_grad = mixer_grad.reshape(high, 4, -1, channels)
    down_far = jnp.sum(fence(down_far_parts, own_ends).astype(F32), axis=0).astype(BF16)
    ends_back = fence(ends_back, mixer_grad, down_far)
    mixer_grad = scatter_along(mixer_grad, below, 2)
    down_far_own = trade(down_far, wide)
    packed_shape = (channels, packed_width)
    grad_conv, edge_back, packed = call(
        functools.partial(gates_kernel, rows, step),
        [(shape, F32), ((blocks, 4, channels), BF16), (packed_shape, BF16)],
        scalars,
        [
            prod_back, part_back, ends_back, s_val, q_val, conv, state, came, recur_in, halo,
            marks, coef, rate_wide, gate_wide, collect, diagonal, eye,
        ],
        [
            pltpu.VMEM((4 * tokens, channels), BF16),
            pltpu.VMEM((4 * tokens, channels), BF16),
            pltpu.VMEM((8, channels), F32),
            pltpu.VMEM(everything, F32),
            pltpu.VMEM(padded, F32),
            pltpu.VMEM(padded, F32),
        ],
        4,
    )
    edge_back = edge_back.reshape(4, rows, 4, channels)
    down_near = project(fence(near_out[1], own_ends), down_q).astype(BF16).reshape(ranks_shape)
    down_near = fence(down_near, edge_back)
    down_near = [pick(down_near, jnp.bitwise_xor(tp_index, j), 0) for j in range(4)]
    down_near[1:] = [trade(down_near[j], j * low) for j in (1, 2, 3)]
    halo_back = across_blocks(edge_back)
    last = len(dp)
    branch_grad = outer(fence(grad_branch, edge_back), normed).astype(BF16).reshape(high, -1, width)
    first_part = back_project(grad_branch, branch_q)
    halo_back = fence(halo_back, down_far_own, branch_grad, first_part)
    branch_grad = scatter_along(branch_grad, below, 1)
    halo_back = halo_back.astype(F32).reshape(seq_count * rows, 4, channels)
    (grad_recur,) = call(
        functools.partial(unconvolve_kernel, rows, step, seq_count),
        [(shape, BF16)],
        scalars,
        [grad_conv, halo_back, marks, coef],
        [pltpu.VMEM(padded, F32)],
        4,
    )
    grad_recur = grad_recur.reshape(4 * tokens, channels)
    recur_grad = reduce_rows(outer(grad_recur, normed), dp, me)
    grad_recur = fence(grad_recur, recur_grad.send())
    grad_normed_part = first_part + back_project(grad_recur, recur_q)
    grad_normed_sent = grad_normed_part.astype(BF16)
    recur_sent = recur_grad.send_to(last - 2, grad_normed_sent)
    packed = reduce_rows(fence(packed, grad_recur), dp, me)
    grad_normed_sent = fence(grad_normed_sent, recur_sent, packed.send())
    gain_one_part = jnp.sum(grad_normed_sent.astype(F32) * input_all.astype(F32) * scale_one, axis=0)
    grad_normed = sum_tokens(grad_normed_sent.reshape(ranks_shape), step)
    own_scale = inverse_rms(input_own.astype(F32))
    unit_one = input_own.astype(F32) * own_scale
    scaled_one = grad_normed * gain_one
    input_grad = (
        grad_residual
        + own_scale
        * (scaled_one - unit_one * jnp.mean(scaled_one * unit_one, axis=-1, keepdims=True))
    ).astype(BF16)
    def halve(partial):
        partial = fence(partial, grad_normed).reshape((2,) * len(above) + partial.shape[1:])
        return Reduction(partial, range(len(above)), above, me)

    mixer_grad, branch_grad = halve(mixer_grad), halve(branch_grad)
    recur_sent = recur_grad.send_to(0, grad_normed)
    mixer_sent = mixer_grad.send_to(0, recur_sent)
    sent = branch_grad.send_to(0, mixer_sent)
    packed_sent = packed.send_to(0, sent)
    pair = jnp.stack([fence(part, packed_sent) for part in (down_kept, down_got)], axis=1)
    pair = exchange(pair, step)
    flat_pieces = [pair[j, h] for h in range(2) for j in range(4)]
    down_weight_grad = pl.pallas_call(
        functools.partial(lay_kernel, 4, high_wide),
        out_shape=jax.ShapeDtypeStruct((out_rows, 8 * hidden), F32),
        in_specs=[pl.BlockSpec(memory_space=pltpu.SMEM)]
        + [pl.BlockSpec(memory_space=pltpu.VMEM)] * len(flat_pieces),
        out_specs=pl.BlockSpec(memory_space=pltpu.VMEM),
        compiler_params=pltpu.CompilerParams(vmem_limit_bytes=VMEM_BYTES),
    )(own_half.reshape(1), *flat_pieces)
    mixer_rows = mixer_grad.total(sent).astype(BF16).reshape(4, out_rows, channels)
    mixer_weight_grad = join_ranks(mixer_rows, high)
    down_sum = sum(fence(part, mixer_rows).astype(F32) for part in down_near + [down_far_own])
    block_output = (residual + down_sum).astype(BF16)
    recur_weight_grad = recur_grad.total(mixer_rows)
    branch_weight_grad = branch_grad.total(recur_weight_grad)
    packed = packed.total(recur_weight_grad)

    gain_parts = jnp.stack([gain_one_part, gain_two_part]).astype(BF16)
    gain_parts = jnp.moveaxis(gain_parts.reshape(2, device_count, out_rows), 1, 0)
    gain_parts = lax.all_to_all(fence(gain_parts, sent), AXES, 0, 0, tiled=True)
    gain_grads = jnp.sum(gain_parts.astype(F32), axis=0)
    numbers = packed[:, 2 * block_size : 2 * block_size + 8]
    return (
        block_output.reshape(rows, span, width),
        input_grad.reshape(rows, span, width),
        gain_grads[0],
        branch_weight_grad,
        recur_weight_grad,
        numbers[:, :TAPS],
        numbers[:, 4],
        packed[:, :block_size],
        numbers[:, 5],
        packed[:, block_size : 2 * block_size],
        numbers[:, 6],
        numbers[:, 7],
        mixer_weight_grad,
        gain_grads[1],
        gate_grad.reshape(hidden_rows, width).astype(F32),
        up_grad.reshape(hidden_rows, width).astype(F32),
        down_weight_grad,
    )


def solution(mesh):
    tokens, spread, table = P("fsdp", "seq", None), P(AXES), P(AXES, None)
    in_specs = (
        tokens, P(), spread, table, table, table, spread, table, spread, table, spread, spread,
        table, spread, table, table, table, tokens,
    )
    out_specs = (
        tokens, tokens, spread, table, table, table, spread, table, spread, table, spread, spread,
        table, spread, table, table, table,
    )
    return jax.shard_map(shards, mesh=mesh, in_specs=in_specs, out_specs=out_specs, check_vma=False)
```
